32 devices in a mesh: group: 4 (over y, x), sub: 8 (over z, core).
Axes of the slice: x: 2, y: 2, z: 4, core: 2. Of those that a mesh axis runs over, the one named last changes fastest.
Arguments:
- points: float32 [3, 262144], P(None, ('group', 'sub')), as said below
- probes: float32 [32, 262144], P(None, ('group', 'sub')), may hold values from -6 to 6
- morton: int32 [262144], P(('group', 'sub')), may hold values from 0 to 8191, as said below
- near_list: int32 [2048, 27], P(('group', 'sub')), may hold values from -1 to 2047, as said below
- leaf_far: int32 [2048, 24], P(('group', 'sub')), may hold values from -1 to 2047, as said below
- box_far: int32 [256, 4], P(('group', 'sub')), may hold values from -1 to 255, as said below
- subtree_far: int32 [32, 4], P(('group', 'sub')), may hold values from -1 to 31, as said below
- leaf_skeleton: float32 [2048, 3, 64], P(('group', 'sub')), as said below
- box_skeleton: float32 [256, 3, 128], P(('group', 'sub')), as said below
- subtree_skeleton: float32 [32, 3, 256], P(('group', 'sub')), as said below
- group_skeleton: float32 [4, 3, 256], replicated, as said below
- leaf_basis: float32 [2048, 64, 128], P(('group', 'sub')), may hold values from -0.5 to 0.5
- leaf_transfer: float32 [2048, 64, 128], P(('group', 'sub')), may hold values from -0.25 to 0.25
- box_transfer: float32 [256, 128, 256], P(('group', 'sub')), may hold values from -0.1875 to 0.1875
- subtree_transfer: float32 [32, 256, 256], P(('group', 'sub')), may hold values from -0.375 to 0.375
Outputs:
- kernel_product: float32 [32, 262144], P(None, ('group', 'sub'))
The draws below stay inside these ranges and needn't reach their ends.
Inputs may be any that keep to these rules, and one draw needn't show every extreme that they name: `morton`: each block of 8192 entries is a permutation of 0 to 8191. `near_list`: row l starts with l, then distinct leaves within 32 of l; -1 marks an empty slot. `leaf_far`: row l holds distinct leaves within 32 of l, none in its near list; -1 marks an empty slot. `box_far`: row b holds distinct other boxes of the same subtree; -1 marks an empty slot. `subtree_far`: row c holds distinct other subtrees of the same group; -1 marks an empty slot. `points`: coordinates in leaf-cell units. `leaf_skeleton`: coordinates in leaf-cell units. `box_skeleton`: coordinates in leaf-cell units. `subtree_skeleton`: coordinates in leaf-cell units. `group_skeleton`: coordinates in leaf-cell units.
All inputs are finite; a program needn't handle non-finite values.
Results may differ from the reference program's by a relative error of at most 0.0003.
Values sent between devices are 32-bit elements; how exact they have to be, the bound alone decides.
A program may use at most 128 MiB of HBM per device.

```python
import math
import jax
import jax.numpy as jnp
from jax import lax

P_SIZE = 128
NV = 32
R0 = 64
R1 = 128
R2 = 256
R3 = 256
CH = 8
NEAR = 27
M0 = 24
M1 = 4
HALO = 32
LEAF_DEV = 64
PTS_DEV = 8192
LEAVES = 2048
NPTS = 262144
BOX1 = 256
BOX2 = 32
GROUP_BOXES = 8
M2 = 4
N_GROUP = 4


leaf_spread = 8.0


def decode_cells(codes):
    coords = []
    for axis_id in range(3):
        cell_bits = jnp.zeros_like(codes)
        for level_id in range(7):
            bit_pos = 3 * level_id + axis_id
            cell_bits = cell_bits | (codes >> bit_pos & 1) << level_id
        coords.append(cell_bits)
    return jnp.stack(coords).astype(jnp.float32)


def shared_points(key):
    first_key, second_key = jax.random.split(jax.random.fold_in(key, 11))
    device_total = NPTS // PTS_DEV
    orders = jax.vmap(lambda subkey: jax.random.permutation(subkey, PTS_DEV))(jax.random.split(first_key, device_total)).astype(jnp.int32)
    columns = (orders + (jnp.arange(device_total, dtype=jnp.int32) * PTS_DEV)[:, None]).reshape(NPTS)
    leaves_of = jnp.arange(NPTS, dtype=jnp.int32) // P_SIZE
    placed = decode_cells(leaves_of) + leaf_spread * jax.random.uniform(second_key, (3, NPTS), jnp.float32)
    points = jnp.zeros((3, NPTS), jnp.float32).at[:, columns].set(placed)
    return (points, orders.reshape(NPTS))


def draw_points(key, part):
    return shared_points(key)[0]


def draw_morton(key, part):
    return shared_points(key)[1]


def shared_lists(key):
    key_pick, key_near, key_far = jax.random.split(jax.random.fold_in(key, 23), 3)
    leaf_ids = jnp.arange(LEAVES, dtype=jnp.int32)
    offset_pool = jnp.concatenate([jnp.arange(-HALO, 0, dtype=jnp.int32), jnp.arange(1, HALO + 1, dtype=jnp.int32)])
    picks = jax.vmap(lambda subkey: jax.random.permutation(subkey, 2 * HALO))(jax.random.split(key_pick, LEAVES)).astype(jnp.int32)
    targets = leaf_ids[:, None] + offset_pool[picks]
    inside = (targets >= 0) & (targets < LEAVES)
    full_row = leaf_ids % LEAF_DEV == LEAF_DEV // 2
    near_counts = jax.random.randint(key_near, (LEAVES,), NEAR // 3, NEAR + 1)
    near_counts = jnp.where(full_row, NEAR, near_counts)
    near_slots = jnp.arange(NEAR - 1, dtype=jnp.int32)
    near_keep = (near_slots[None, :] < near_counts[:, None] - 1) & inside[:, :NEAR - 1]
    near_rest = jnp.where(near_keep, targets[:, :NEAR - 1], -1)
    near_table = jnp.concatenate([leaf_ids[:, None], near_rest], axis=1).astype(jnp.int32)
    far_counts = jax.random.randint(key_far, (LEAVES,), M0 // 3, M0 + 1)
    far_counts = jnp.where(full_row, M0, far_counts)
    far_slots = jnp.arange(M0, dtype=jnp.int32)
    far_keep = (far_slots[None, :] < far_counts[:, None]) & inside[:, NEAR - 1:NEAR - 1 + M0]
    far_table = jnp.where(far_keep, targets[:, NEAR - 1:NEAR - 1 + M0], -1).astype(jnp.int32)
    return (near_table, far_table)


def draw_near_list(key, part):
    return shared_lists(key)[0]


def draw_leaf_far(key, part):
    return shared_lists(key)[1]


def sibling_lists(key, node_count, family, most, fewest):
    key_pick, key_count = jax.random.split(key)
    node_ids = jnp.arange(node_count, dtype=jnp.int32)
    position = node_ids % family
    picks = jax.vmap(lambda subkey: jax.random.permutation(subkey, family - 1))(jax.random.split(key_pick, node_count)).astype(jnp.int32)[:, :most]
    others = picks + (picks >= position[:, None]).astype(jnp.int32)
    targets = (node_ids // family * family)[:, None] + others
    counts = jax.random.randint(key_count, (node_count,), fewest, most + 1)
    counts = jnp.where(position == 0, most, counts)
    slots = jnp.arange(most, dtype=jnp.int32)
    return jnp.where(slots[None, :] < counts[:, None], targets, -1).astype(jnp.int32)


def draw_box_far(key, part):
    return sibling_lists(jax.random.fold_in(key, 37), BOX1, CH, M1, 1)


def draw_subtree_far(key, part):
    return sibling_lists(jax.random.fold_in(key, 41), BOX2, GROUP_BOXES, M2, max(M2 // 2, 1))


def skeleton_points(key, node_count, leaf_span, rank_count, spread):
    key_leaf, key_place = jax.random.split(key)
    leaf_ids = jnp.arange(node_count, dtype=jnp.int32)[:, None] * leaf_span + jax.random.randint(key_leaf, (node_count, rank_count), 0, leaf_span)
    cells = decode_cells(leaf_ids).transpose(1, 0, 2)
    return cells + spread * jax.random.uniform(key_place, (node_count, 3, rank_count), jnp.float32)


def draw_leaf_skeleton(key, part):
    return skeleton_points(jax.random.fold_in(key, 51), LEAVES, 1, R0, leaf_spread)


def draw_box_skeleton(key, part):
    return skeleton_points(jax.random.fold_in(key, 53), BOX1, CH, R1, 1.0)


def draw_subtree_skeleton(key, part):
    return skeleton_points(jax.random.fold_in(key, 57), BOX2, CH * CH, R2, 1.0)


def draw_group_skeleton(key, part):
    return skeleton_points(jax.random.fold_in(key, 59), N_GROUP, LEAVES // N_GROUP, R3, 1.0)


def block_levels(key, dims, cuts, low, high):
    loudness = 1.0
    for dim, blocks in cuts:
        draws = jax.random.uniform(jax.random.fold_in(jax.random.fold_in(key, 6), dim), (blocks,), jnp.float32, low / len(cuts), high / len(cuts))
        loudness = loudness * jnp.repeat(jnp.exp(draws), dims[dim] // blocks).reshape((-1,) + (1,) * (len(dims) - 1 - dim))
    return loudness


def normal_values(rng, extent, width, bound, cuts=(), kind=jnp.bfloat16):
    factor_of = block_levels(rng, extent, cuts, -0.22, 0.18) if cuts else 1.0
    values = jax.random.normal(rng, extent, jnp.float32) * width * factor_of
    return jnp.minimum(jnp.maximum(values, -bound), bound).astype(kind)


def setup_inputs(seed: int = 0) -> dict:
    key_of = jax.random.split(jax.random.key(seed), 16)
    points = draw_points(jax.random.fold_in(key_of[15], 71), 0)
    probes = normal_values(key_of[1], (NV, NPTS), 1.0, 6.0, ((1, 32),), jnp.float32)
    morton = draw_morton(jax.random.fold_in(key_of[15], 71), 0)
    near_list = draw_near_list(jax.random.fold_in(key_of[15], 71), 0)
    leaf_far = draw_leaf_far(jax.random.fold_in(key_of[15], 71), 0)
    box_far = draw_box_far(jax.random.fold_in(key_of[15], 71), 0)
    subtree_far = draw_subtree_far(jax.random.fold_in(key_of[15], 71), 0)
    leaf_skeleton = draw_leaf_skeleton(jax.random.fold_in(key_of[15], 71), 0)
    box_skeleton = draw_box_skeleton(jax.random.fold_in(key_of[15], 71), 0)
    subtree_skeleton = draw_subtree_skeleton(jax.random.fold_in(key_of[15], 71), 0)
    group_skeleton = draw_group_skeleton(jax.random.fold_in(key_of[15], 71), 0)
    leaf_basis = normal_values(key_of[11], (LEAVES, R0, P_SIZE), P_SIZE ** -0.5, 0.5, ((0, 32),), jnp.float32)
    leaf_transfer = normal_values(key_of[12], (LEAVES, R0, R1), (CH * R0) ** -0.5, 0.25, ((0, 32),), jnp.float32)
    box_transfer = normal_values(key_of[13], (BOX1, R1, R2), (CH * R1) ** -0.5, 0.1875, ((0, 32),), jnp.float32)
    subtree_transfer = normal_values(key_of[14], (BOX2, R2, R3), R2 ** -0.5, 0.375, ((0, 32),), jnp.float32)
    return {"points": points, "probes": probes, "morton": morton, "near_list": near_list, "leaf_far": leaf_far, "box_far": box_far, "subtree_far": subtree_far, "leaf_skeleton": leaf_skeleton, "box_skeleton": box_skeleton, "subtree_skeleton": subtree_skeleton, "group_skeleton": group_skeleton, "leaf_basis": leaf_basis, "leaf_transfer": leaf_transfer, "box_transfer": box_transfer, "subtree_transfer": subtree_transfer}


highest = lax.Precision.HIGHEST
matern_rate = math.sqrt(3.0) / 12.0

def matern(source, target):
    squared = None
    for coord_id in range(3):
        offset = source[..., coord_id, :, None] - target[..., coord_id, None, :]
        squared = offset * offset if coord_id == 0 else squared + offset * offset
    radius = jnp.sqrt(squared + 0.0001) * matern_rate
    return (1.0 + radius) * jnp.exp(-radius)

def couple(skeleton, coefficients, partner_ids, factor):
    length = partner_ids.shape[0]

    def block_terms(first_row):
        anchor = lax.dynamic_slice_in_dim(skeleton, first_row, 8, 0)
        entries = lax.dynamic_slice_in_dim(partner_ids, first_row, 8, 0)
        usable = (entries >= 0).astype(skeleton.dtype)
        safe_ids = jnp.maximum(entries, 0)
        kernel_tiles = matern(anchor[:, None], skeleton[safe_ids]) * usable[:, :, None, None]
        return jnp.einsum('bjrs,bjvs->bvr', kernel_tiles, coefficients[safe_ids], precision=highest)
    starts = jnp.arange(length // 8, dtype=jnp.int32) * 8
    blocks = lax.map(block_terms, starts)
    return blocks.reshape((length,) + blocks.shape[2:]) * factor

def reference(points, probes, morton, near_list, leaf_far, box_far, subtree_far, leaf_skeleton, box_skeleton, subtree_skeleton, group_skeleton, leaf_basis, leaf_transfer, box_transfer, subtree_transfer):
    offsets = jnp.arange(NPTS, dtype=jnp.int32) // PTS_DEV * PTS_DEV
    columns = morton.astype(jnp.int32) + offsets
    leaf_points = points[:, columns].reshape(3, LEAVES, P_SIZE).transpose(1, 0, 2)
    leaf_probes = probes[:, columns].reshape(NV, LEAVES, P_SIZE).transpose(1, 0, 2)
    near_field = couple(leaf_points, leaf_probes, near_list, (P_SIZE * NEAR) ** (-0.5))
    coef_leaf = jnp.einsum('lvp,lrp->lvr', leaf_probes, leaf_basis, precision=highest)
    coef_box = jnp.einsum('lvr,lrs->lvs', coef_leaf, leaf_transfer, precision=highest).reshape(BOX1, CH, NV, R1).sum(axis=1)
    coef_subtree = jnp.einsum('bvr,brs->bvs', coef_box, box_transfer, precision=highest).reshape(BOX2, CH, NV, R2).sum(axis=1)
    coef_group = jnp.einsum('cvr,crs->cvs', coef_subtree, subtree_transfer, precision=highest).reshape(N_GROUP, GROUP_BOXES, NV, R3).sum(axis=1)
    local_leaf = couple(leaf_skeleton, coef_leaf, leaf_far, (R0 * M0) ** (-0.5))
    local_box = couple(box_skeleton, coef_box, box_far, (R1 * M1) ** (-0.5))
    local_subtree = couple(subtree_skeleton, coef_subtree, subtree_far, (R2 * M2) ** (-0.5))
    other_mask = 1.0 - jnp.eye(N_GROUP, dtype=group_skeleton.dtype)
    group_tiles = matern(group_skeleton[:, None], group_skeleton[None, :]) * other_mask[:, :, None, None]
    local_group = jnp.einsum('ghrs,hvs->gvr', group_tiles, coef_group, precision=highest) * R3 ** (-0.5)
    down_subtree = local_subtree + jnp.einsum('cvs,crs->cvr', jnp.repeat(local_group, GROUP_BOXES, axis=0), subtree_transfer, precision=highest)
    down_box = local_box + jnp.einsum('bvs,brs->bvr', jnp.repeat(down_subtree, CH, axis=0), box_transfer, precision=highest)
    down_leaf = local_leaf + jnp.einsum('lvs,lrs->lvr', jnp.repeat(down_box, CH, axis=0), leaf_transfer, precision=highest)
    result = near_field + jnp.einsum('lvr,lrp->lvp', down_leaf, leaf_basis, precision=highest)
    ordered = result.transpose(1, 0, 2).reshape(NV, NPTS)
    return jnp.zeros_like(ordered).at[:, columns].set(ordered)
```

```python
import functools
import math

import jax
import jax.numpy as jnp
from jax import lax
from jax.experimental import pallas as pl
from jax.experimental.pallas import tpu as pltpu
from jax.sharding import PartitionSpec as P

P_SIZE = 128
CH = 8
HALO = 32
SPLIT = 64
COUNT = 63
GROUPS = 62
NEAR_GROUP = 2
NEAR_BATCH = 8
FAR_GROUP = 2
FAR_BATCH = 12

highest = lax.Precision.HIGHEST
scale = math.sqrt(3.0) / 12.0
soft = 0.0001 * scale * scale
log2e = math.log2(math.e)
f32 = jnp.float32
bf16 = jnp.bfloat16
NT = (((1,), (1,)), ((), ()))


def hdot(a, b):
    return jnp.dot(a, b, precision=highest, preferred_element_type=f32)


def hdot_nt(a, b):
    return lax.dot_general(a, b, NT, precision=highest, preferred_element_type=f32)


def profile(squared):
    squared = jnp.maximum(squared, soft)
    u = squared * lax.rsqrt(squared)
    return (1.0 + u) * jnp.exp2(u * -log2e)


def split3(v):
    high = v.astype(bf16).astype(f32)
    rest = v - high
    mid = rest.astype(bf16).astype(f32)
    return high, mid, rest - mid


def augmented(x):
    row = lax.broadcasted_iota(jnp.int32, x.shape, 0)
    norm = jnp.sum(x * x, axis=0, keepdims=True)
    source = jnp.where(row < 3, -2.0 * x, jnp.where(row == 3, 1.0, jnp.where(row == 4, norm + soft, 0.0)))
    target = jnp.where(row < 3, x, jnp.where(row == 3, norm, jnp.where(row == 4, 1.0, 0.0)))
    return source, target


def source_rows(v):
    h, m, lo = split3(v)
    return jnp.concatenate([h, m, h, m, lo, h, lo, m], axis=0)


def target_rows(v):
    h, m, lo = split3(v)
    return jnp.concatenate([h, h, m, m, h, lo, m, lo], axis=0)


def coords(block, centre):
    row = lax.broadcasted_iota(jnp.int32, block.shape, 0)
    return jnp.where(row < 3, (block - centre) * scale, 0.0)


def sort_list(ids_ref, out, base, group):
    leaves, width = ids_ref.shape
    ids = ids_ref[...]
    place = ids - base
    valid = ids >= 0
    own = valid & (place >= 0) & (place < leaves)
    other = valid & jnp.logical_not(own)
    slot = jnp.where(own, place, jnp.where(place < 0, place + HALO, place - leaves + HALO))
    ones = jnp.concatenate([own.astype(f32), other.astype(f32)], axis=0)
    before = lax.broadcasted_iota(jnp.int32, (width, width), 0) < lax.broadcasted_iota(
        jnp.int32, (width, width), 1
    )
    rank = jnp.dot(ones.astype(bf16), before.astype(bf16), preferred_element_type=f32)
    rank = rank.astype(jnp.int32)
    key = jnp.where(own, rank[0:leaves], jnp.where(other, SPLIT + rank[leaves:], -1))
    lane = lax.broadcasted_iota(jnp.int32, (leaves, P_SIZE), 1)
    table = jnp.full((leaves, P_SIZE), 2 * HALO, jnp.int32)
    for j in range(width):
        table = jnp.where(lane == key[:, j : j + 1], slot[:, j : j + 1], table)
    row = lax.broadcasted_iota(jnp.int32, (8, P_SIZE), 1)
    last = jnp.full((8, P_SIZE), 2 * HALO, jnp.int32)
    for part, lane0 in ((ones[0:leaves], 0), (ones[leaves:], SPLIT)):
        many = jnp.sum(part, axis=1, keepdims=True).astype(jnp.int32)
        table = jnp.where(lane == lane0 + COUNT, many, table)
        groups = jnp.maximum((many + group - 1) // group, 1)
        groups = jnp.sum(groups.astype(f32), axis=0, keepdims=True).astype(jnp.int32)
        last = jnp.where(row == lane0 + GROUPS, groups, jnp.where(row == lane0 + COUNT, 0, last))
    out[0:leaves, :] = table
    out[leaves : leaves + 8, :] = last


def arrange_kernel(
    morton, near_list, leaf_far, points, probes, skel, basis, leaf_tr, box_tr, sub_tr,
    geo, near_ids, far_ids, q1_out, q2_out, q3_out, rows, pad, got,
):
    leaves = geo.shape[0]
    boxes = q1_out.shape[0]
    device = lax.axis_index("group") * lax.axis_size("sub") + lax.axis_index("sub")
    sort_list(near_list, near_ids, device * leaves, NEAR_GROUP)
    sort_list(leaf_far, far_ids, device * leaves, FAR_GROUP)
    pad[...] = jnp.zeros_like(pad)

    def flip(g, c):
        for j in range(4):
            at = pl.ds(pl.multiple_of((4 * g + j) * P_SIZE, P_SIZE), P_SIZE)
            pad[j, 0:32, :] = probes[:, at]
            pad[j, 32:35, :] = points[:, at]
        for j in range(4):
            at = pl.ds(pl.multiple_of((4 * g + j) * P_SIZE, P_SIZE), P_SIZE)
            rows[at, :] = pad[j].T
        return c

    lax.fori_loop(0, leaves // 4, flip, 0)

    def one_box(b, q2):
        for j in range(CH):
            base = (b * CH + j) * P_SIZE
            for k in range(P_SIZE):
                got[j, k : k + 1, :] = rows[pl.ds(morton[base + k], 1), :]
        turned = [got[j].T for j in range(CH)]
        parts = []
        for j in range(CH):
            i = b * CH + j
            geo[i, 0:40, :] = turned[j][0:40]
            geo[i, 35:38, 0:64] = skel[i]
            q0 = hdot_nt(turned[j][0:32], basis[i])
            geo[i, 40:56, 0:64] = q0[0:16]
            geo[i, 40:56, 64:128] = q0[16:32]
            parts.append(q0)
        q1 = jnp.zeros(q1_out.shape[1:], f32)
        for j in range(0, CH, 2):
            two = jnp.concatenate([leaf_tr[b * CH + j], leaf_tr[b * CH + j + 1]], axis=0)
            q1 = q1 + hdot(jnp.concatenate(parts[j : j + 2], axis=1), two)
        q1_out[b] = q1
        return q2 + hdot(q1, box_tr[b])

    q2 = lax.fori_loop(0, boxes, one_box, jnp.zeros(q2_out.shape, f32))
    q2_out[...] = q2
    q3_out[...] = hdot(q2, sub_tr[0])


def prepare_source(block, at, centre_pt, centre_sk, src, xw, src_lo, src_hi, qw):
    geo8 = block[32:40]
    s8, t8 = augmented(coords(geo8, centre_pt))
    src[at] = source_rows(s8).T.astype(bf16)
    turned = jnp.concatenate([geo8[3:8], geo8[0:3]], axis=0)
    ks8, kt8 = augmented(coords(turned, centre_sk))
    low = lax.broadcasted_iota(jnp.int32, (8, P_SIZE), 1) < 64
    ks8 = jnp.where(low, ks8, 0.0)
    src_lo[at] = source_rows(ks8).astype(bf16)
    src_hi[at] = source_rows(pltpu.roll(ks8, 64, 1)).astype(bf16)
    x = block[0:32]
    hi = x.astype(bf16)
    lo = (x - hi.astype(f32)).astype(bf16)
    xw[at] = jnp.concatenate([hi, lo], axis=0)
    q = block[40:56]
    q = jnp.concatenate([q, pltpu.roll(q, 64, 1)], axis=0)
    qhi = q.astype(bf16).astype(f32)
    four = jnp.concatenate([qhi, q - qhi, jnp.zeros((64, P_SIZE), f32)], axis=0)
    qw[at] = four.T[0:64].astype(bf16)
    return t8, kt8


def prepare_target(t8, kt8, at, tgt, tgt_far):
    tgt[at] = target_rows(t8).astype(bf16)
    far = target_rows(kt8)
    tgt_far[at] = jnp.concatenate([far, far], axis=0).T[0:64].astype(bf16)


def clear(refs, at):
    for ref in refs:
        ref[at] = jnp.zeros(ref.shape[1:], ref.dtype)


def batches(ids, lane0, leaves, group, batch, first, step):
    def follow(at):
        leaf, off = at
        more = off + group < ids[leaf, lane0 + COUNT]
        return (
            jnp.where(more, leaf, jnp.minimum(leaf + 1, leaves)),
            jnp.where(more, off + group, 0),
        )

    def take(at):
        got = []
        for _ in range(batch):
            got.append(at)
            at = follow(at)
        return got, at

    now, at = take((jnp.int32(0), jnp.int32(0)))
    first(now)
    later, at = take(at)

    def one(i, c):
        now, later, at = c
        step(now, later)
        after, at = take(at)
        return later, after, at

    total = ids[leaves, lane0 + GROUPS]
    lax.fori_loop(0, (total + batch - 1) // batch, one, (now, later, at))


def halves(k):
    hi = k.astype(bf16)
    return hi, (k - hi.astype(f32)).astype(bf16)


def near_pass(ids, lane0, src, tgt, xw, out, dist):
    leaves = tgt.shape[0] - 1

    def squared(at, u):
        leaf, off = at
        return jnp.dot(
            src[ids[leaf, lane0 + off + u]], tgt[leaf], preferred_element_type=f32
        )

    def first(now):
        for j in range(NEAR_BATCH):
            for u in range(NEAR_GROUP):
                dist[j * NEAR_GROUP + u] = squared(now[j], u)

    def step(now, later):
        for j in range(NEAR_BATCH):
            leaf, off = now[j]
            tiles, values = [], []
            for u in range(NEAR_GROUP):
                n = j * NEAR_GROUP + u
                tiles.append(jnp.concatenate(halves(profile(dist[n])), axis=1))
                values.append(xw[ids[leaf, lane0 + off + u]])
                dist[n] = squared(later[j], u)
            acc = jnp.dot(
                jnp.concatenate(values, axis=1),
                jnp.concatenate(tiles, axis=0),
                preferred_element_type=f32,
            )
            out[leaf] = out[leaf] + (acc[0:32, 0:128] + acc[0:32, 128:256] + acc[32:64, 0:128])

    batches(ids, lane0, leaves, NEAR_GROUP, NEAR_BATCH, first, step)


def far_pass(ids, lane0, src_lo, src_hi, tgt, qw, out, dist):
    leaves = tgt.shape[0] - 1

    def squared(at):
        leaf, off = at
        source = jnp.concatenate(
            [src_lo[ids[leaf, lane0 + off]], src_hi[ids[leaf, lane0 + off + 1]]], axis=0
        )
        return jnp.dot(tgt[leaf], source, preferred_element_type=f32)

    def first(now):
        for j in range(FAR_BATCH):
            dist[j] = squared(now[j])

    def step(now, later):
        for j in range(FAR_BATCH):
            leaf, off = now[j]
            tile = jnp.concatenate(halves(profile(dist[j])), axis=1)
            a, b = qw[ids[leaf, lane0 + off]], qw[ids[leaf, lane0 + off + 1]]
            dist[j] = squared(later[j])
            acc = jnp.dot(
                tile, jnp.concatenate([a, b, a, b], axis=0), preferred_element_type=f32
            )
            out[leaf] = out[leaf] + acc

    batches(ids, lane0, leaves, FAR_GROUP, FAR_BATCH, first, step)


def inner_kernel(
    near_ids, far_ids, geo,
    near_out, far_out, tgt, tgt_far,
    src, xw, src_lo, src_hi, qw, near_dist, far_dist,
):
    leaves = geo.shape[0]
    first = geo[0, 32:40, 0:1]
    centre_sk = jnp.concatenate([first[3:8], first[0:3]], axis=0)
    sources = (src, xw, src_lo, src_hi, qw)

    def load(g, c):
        for j in range(8):
            i = g * 8 + j
            t8, kt8 = prepare_source(geo[i], i, first, centre_sk, *sources)
            prepare_target(t8, kt8, i, tgt, tgt_far)
        for j in range(8):
            clear((near_out, far_out), g * 8 + j)
        return c

    lax.fori_loop(0, leaves // 8, load, 0)
    clear(sources, 2 * HALO)
    clear((near_out, far_out, tgt, tgt_far), leaves)
    near_pass(near_ids, 0, src, tgt, xw, near_out, near_dist)
    far_pass(far_ids, 0, src_lo, src_hi, tgt_far, qw, far_out, far_dist)


def outer_kernel(
    near_ids, far_ids, origin, left, right, tgt, tgt_far, near_in, far_in,
    near_out, far_out,
    src, xw, src_lo, src_hi, qw, near_dist, far_dist,
):
    leaves = near_in.shape[0] - 1
    first = origin[0, 32:40, 0:1]
    centre_sk = jnp.concatenate([first[3:8], first[0:3]], axis=0)
    sources = (src, xw, src_lo, src_hi, qw)

    def load(g, c):
        for j in range(4):
            i = g * 4 + j
            prepare_source(left[i], i, first, centre_sk, *sources)
            prepare_source(right[i], i + HALO, first, centre_sk, *sources)
            for k in (i, i + HALO):
                near_out[k] = near_in[k]
                far_out[k] = far_in[k]
        return c

    lax.fori_loop(0, HALO // 4, load, 0)
    clear(sources, 2 * HALO)
    clear((near_out, far_out), leaves)
    near_pass(near_ids, SPLIT, src, tgt, xw, near_out, near_dist)
    far_pass(far_ids, SPLIT, src_lo, src_hi, tgt_far, qw, far_out, far_dist)


def centred(block, centre):
    return augmented(coords(block, centre))


def finish_kernel(
    morton, box_far, sub_far, place,
    near, far, q1, gathered, box_skel, group_skel,
    basis, leaf_tr, box_tr, sub_tr,
    out, rows, pad, l1s,
    *, subs, groups, box_width, sub_width, near_factor, f0, f1, f2, f3,
):
    boxes = q1.shape[0]
    leaves = near.shape[0] - 1
    device, group = place[0], place[1]

    def tile(source8, target8):
        return profile(
            jnp.dot(
                source_rows(source8).T.astype(bf16),
                target_rows(target8).astype(bf16),
                preferred_element_type=f32,
            )
        )

    own = gathered[device, 64:72, :]
    centre = own[:, 0:1]
    target = centred(own, centre)[1]

    def sub_term(j, acc):
        entry = sub_far[j]
        m = jnp.maximum(entry, 0)
        source = centred(gathered[m, 64:72, :], centre)[0]
        term = hdot(gathered[m, 0:32, :], tile(source, target))
        return acc + jnp.where(entry >= 0, term, 0.0)

    many = 4 if sub_width % 4 == 0 else 1

    def sub_terms(g, acc):
        for j in range(many):
            acc = sub_term(g * many + j, acc)
        return acc

    z2 = lax.fori_loop(0, sub_width // many, sub_terms, jnp.zeros(gathered[0, 0:32, :].shape, f32))
    g_own = group_skel[group]
    g_centre = g_own[:, 0:1]
    g_target = centred(g_own, g_centre)[1]

    def group_term(h, acc):
        q3 = lax.fori_loop(
            0, subs, lambda s, t: t + gathered[h * subs + s, 32:64, :], jnp.zeros(z2.shape, f32)
        )
        source = centred(group_skel[h], g_centre)[0]
        return acc + jnp.where(h != group, hdot(q3, tile(source, g_target)), 0.0)

    z3 = jnp.zeros(z2.shape, f32)
    for h in range(groups):
        z3 = group_term(h, z3)
    l2 = z2 * f2 + hdot_nt(z3 * f3, sub_tr[0])

    def box_level(b, c):
        mine = box_skel[b]
        b_centre = mine[:, 0:1]
        b_target = centred(mine, b_centre)[1]

        def box_term(j, acc):
            entry = box_far[b * box_width + j]
            m = jnp.maximum(entry - device * boxes, 0)
            source = centred(box_skel[m], b_centre)[0]
            return acc + jnp.where(entry >= 0, hdot(q1[m], tile(source, b_target)), 0.0)

        z1 = jnp.zeros((32, P_SIZE), f32)
        for j in range(box_width):
            z1 = box_term(j, z1)
        l1s[b] = z1 * f1 + hdot_nt(l2, box_tr[b])
        return c

    def box_pair(g, c):
        for j in range(2):
            box_level(2 * g + j, c)
        return c

    lax.fori_loop(0, boxes // 2, box_pair, 0)

    pad[...] = jnp.zeros_like(pad)

    def down(b, c):
        l1 = l1s[b]
        for j in range(CH):
            i = b * CH + j
            turned = far[i].T
            l0 = (turned[0:32] + turned[32:64]) * f0 + hdot_nt(l1, leaf_tr[i])
            pad[j, 0:32, :] = near[i] * near_factor + hdot(l0, basis[i])
        for j in range(CH):
            pad[CH + j] = pad[j].T
        for j in range(CH):
            base = (b * CH + j) * P_SIZE
            for k in range(P_SIZE):
                rows[pl.ds(morton[base + k], 1), :] = pad[CH + j, k : k + 1, :]
        return c

    lax.fori_loop(0, boxes, down, 0)

    def flip(g, c):
        for j in range(4):
            at = pl.ds(pl.multiple_of((4 * g + j) * P_SIZE, P_SIZE), P_SIZE)
            out[:, at] = rows[at, :].T[0:32]
        return c

    lax.fori_loop(0, leaves // 4, flip, 0)


VMEM = pl.BlockSpec(memory_space=pltpu.VMEM)
SMEM = pl.BlockSpec(memory_space=pltpu.SMEM)
params = pltpu.CompilerParams(vmem_limit_bytes=56 * 2**20)


def body(
    points, probes, morton, near_list, leaf_far, box_far, subtree_far,
    leaf_skeleton, box_skeleton, subtree_skeleton, group_skeleton,
    leaf_basis, leaf_transfer, box_transfer, subtree_transfer,
):
    leaves = near_list.shape[0]
    count = points.shape[1]
    nv = probes.shape[0]
    boxes = box_far.shape[0]
    r0, r1 = leaf_basis.shape[1], box_transfer.shape[1]
    r2, r3 = subtree_transfer.shape[1:]
    device = lax.axis_index(("group", "sub"))
    group = lax.axis_index("group")
    subs, groups = lax.axis_size("sub"), lax.axis_size("group")

    i32 = jnp.int32
    geo, near_ids, far_ids, q1, q2, q3 = pl.pallas_call(
        arrange_kernel,
        out_shape=(
            jax.ShapeDtypeStruct((leaves, 56, P_SIZE), f32),
            jax.ShapeDtypeStruct((leaves + 8, P_SIZE), i32),
            jax.ShapeDtypeStruct((leaves + 8, P_SIZE), i32),
            jax.ShapeDtypeStruct((boxes, nv, r1), f32),
            jax.ShapeDtypeStruct((nv, r2), f32),
            jax.ShapeDtypeStruct((nv, r3), f32),
        ),
        in_specs=[SMEM] + [VMEM] * 9,
        out_specs=(VMEM,) * 6,
        scratch_shapes=[
            pltpu.VMEM((count, P_SIZE), f32),
            pltpu.VMEM((4, P_SIZE, P_SIZE), f32),
            pltpu.VMEM((CH, P_SIZE, P_SIZE), f32),
        ],
        compiler_params=params,
        name="arrange",
    )(morton, near_list, leaf_far, points, probes, leaf_skeleton, leaf_basis, leaf_transfer, box_transfer, subtree_transfer)

    both = ("group", "sub")
    ends = subs * groups - 1
    left = lax.ppermute(geo[leaves - HALO :], both, [(i, i + 1) for i in range(ends)])
    right = lax.ppermute(geo[:HALO], both, [(i + 1, i) for i in range(ends)])
    packed = jnp.concatenate(
        [q2, q3, subtree_skeleton[0], jnp.zeros((5, r2), f32)], axis=0
    )
    gathered = lax.all_gather(packed, both, axis=0)

    acc_shapes = (
        jax.ShapeDtypeStruct((leaves + 1, nv, P_SIZE), f32),
        jax.ShapeDtypeStruct((leaves + 1, r0, P_SIZE), f32),
    )
    tables = [
        pltpu.VMEM((2 * HALO + 1, P_SIZE, 64), bf16),
        pltpu.VMEM((2 * HALO + 1, 2 * nv, P_SIZE), bf16),
        pltpu.VMEM((2 * HALO + 1, 64, P_SIZE), bf16),
        pltpu.VMEM((2 * HALO + 1, 64, P_SIZE), bf16),
        pltpu.VMEM((2 * HALO + 1, 64, P_SIZE), bf16),
        pltpu.VMEM((NEAR_BATCH * NEAR_GROUP, P_SIZE, P_SIZE), f32),
        pltpu.VMEM((FAR_BATCH, 64, P_SIZE), f32),
    ]
    near, far, tgt, tgt_far = pl.pallas_call(
        inner_kernel,
        out_shape=acc_shapes
        + (
            jax.ShapeDtypeStruct((leaves + 1, 64, P_SIZE), bf16),
            jax.ShapeDtypeStruct((leaves + 1, 64, P_SIZE), bf16),
        ),
        in_specs=[SMEM] * 2 + [VMEM],
        out_specs=(VMEM,) * 4,
        scratch_shapes=tables,
        compiler_params=params,
        cost_estimate=pl.CostEstimate(flops=2 * 10**10, bytes_accessed=10**7, transcendentals=5 * 10**7),
        name="inner",
    )(near_ids, far_ids, geo)
    near, far = pl.pallas_call(
        outer_kernel,
        out_shape=acc_shapes,
        in_specs=[SMEM] * 2 + [VMEM] * 7,
        out_specs=(VMEM,) * 2,
        scratch_shapes=tables,
        compiler_params=params,
        name="outer",
    )(near_ids, far_ids, geo[:1], left, right, tgt, tgt_far, near, far)

    pad8 = lambda a: jnp.pad(a, ((0, 0), (0, 5), (0, 0)))
    return pl.pallas_call(
        functools.partial(
            finish_kernel,
            subs=subs,
            groups=groups,
            box_width=box_far.shape[1],
            sub_width=subtree_far.shape[1],
            near_factor=(P_SIZE * near_list.shape[1]) ** -0.5,
            f0=(r0 * leaf_far.shape[1]) ** -0.5,
            f1=(r1 * box_far.shape[1]) ** -0.5,
            f2=(r2 * subtree_far.shape[1]) ** -0.5,
            f3=r3**-0.5,
        ),
        out_shape=jax.ShapeDtypeStruct((nv, count), f32),
        in_specs=[SMEM] * 4 + [VMEM] * 10,
        out_specs=VMEM,
        scratch_shapes=[
            pltpu.VMEM((count, P_SIZE), f32),
            pltpu.VMEM((2 * CH, P_SIZE, P_SIZE), f32),
            pltpu.VMEM((boxes, nv, P_SIZE), f32),
        ],
        compiler_params=params,
        name="finish",
    )(
        morton, box_far.reshape(-1), subtree_far.reshape(-1),
        jnp.stack([device, group]).astype(jnp.int32),
        near, far, q1, gathered, pad8(box_skeleton), pad8(group_skeleton),
        leaf_basis, leaf_transfer, box_transfer, subtree_transfer,
    )


def solution(mesh):
    two = ("group", "sub")
    placed = (
        (P(None, two),) * 2
        + (P(two),)
        + (P(two, None),) * 4
        + (P(two, None, None),) * 3
        + (P(),)
        + (P(two, None, None),) * 4
    )
    return jax.shard_map(
        body, mesh=mesh, in_specs=placed, out_specs=P(None, two), check_vma=False
    )
```

```python
import functools
import math

import jax
import jax.numpy as jnp
from jax import lax
from jax.experimental import pallas as pl
from jax.experimental.pallas import tpu as pltpu
from jax.sharding import PartitionSpec as P

P_SIZE = 128
CH = 8
HALO = 32
SPLIT = 16
COUNT = 15
TOTAL = 14
NONE = 2 * HALO
RADIX = 128
NEAR_BATCH = 8
FAR_BATCH = 12

highest = lax.Precision.HIGHEST
scale = math.sqrt(3.0) / 12.0
soft = 0.0001 * scale * scale
log2e = math.log2(math.e)
f32 = jnp.float32
bf16 = jnp.bfloat16
NT = (((1,), (1,)), ((), ()))


def hdot(a, b):
    return jnp.dot(a, b, precision=highest, preferred_element_type=f32)


def hdot_nt(a, b):
    return lax.dot_general(a, b, NT, precision=highest, preferred_element_type=f32)


def profile(squared):
    squared = jnp.maximum(squared, soft)
    u = squared * lax.rsqrt(squared)
    return (1.0 + u) * jnp.exp2(u * -log2e)


def split3(v):
    high = v.astype(bf16).astype(f32)
    rest = v - high
    mid = rest.astype(bf16).astype(f32)
    return high, mid, rest - mid


def augmented(x):
    row = lax.broadcasted_iota(jnp.int32, x.shape, 0)
    norm = jnp.sum(x * x, axis=0, keepdims=True)
    source = jnp.where(row < 3, -2.0 * x, jnp.where(row == 3, 1.0, jnp.where(row == 4, norm + soft, 0.0)))
    target = jnp.where(row < 3, x, jnp.where(row == 3, norm, jnp.where(row == 4, 1.0, 0.0)))
    return source, target


def source_rows(v):
    h, m, lo = split3(v)
    return jnp.concatenate([h, m, h, m, lo, h, lo, m], axis=0)


def target_rows(v):
    h, m, lo = split3(v)
    return jnp.concatenate([h, h, m, m, h, lo, m, lo], axis=0)


def coords(block, centre):
    row = lax.broadcasted_iota(jnp.int32, block.shape, 0)
    return jnp.where(row < 3, (block - centre) * scale, 0.0)


def sort_list(ids_ref, out, wide, base):
    width, leaves = ids_ref.shape
    wide[...] = jnp.full(wide.shape, -1, jnp.int32)
    wide[0:width, 0:leaves] = ids_ref[...]
    ids = wide[...]
    shape = ids.shape
    place = ids - base
    valid = ids >= 0
    own = valid & (place >= 0) & (place < leaves)
    other = valid & jnp.logical_not(own)
    slot = jnp.where(own, place, jnp.where(place < 0, place + HALO, place - leaves + HALO))
    ones = jnp.concatenate([own.astype(f32), other.astype(f32)], axis=1)
    row = lax.broadcasted_iota(jnp.int32, shape, 0)
    lane = lax.broadcasted_iota(jnp.int32, shape, 1)
    square = (shape[0], shape[0])
    before = lax.broadcasted_iota(jnp.int32, square, 1) < lax.broadcasted_iota(jnp.int32, square, 0)
    rank = jnp.dot(
        before.astype(f32).astype(bf16), ones.astype(bf16), preferred_element_type=f32
    ).astype(jnp.int32)
    rank = jnp.where(own, rank[:, 0:P_SIZE], rank[:, P_SIZE:])
    goes = jnp.where(own, rank // 2, jnp.where(other, SPLIT + rank // 2, -1))
    value = jnp.where(rank % 2 == 1, slot * RADIX, slot).astype(f32)
    many = jnp.sum(ones, axis=0, keepdims=True).astype(jnp.int32)
    many = jnp.where(row < SPLIT, many[:, 0:P_SIZE], many[:, P_SIZE:])
    at = 2 * (row % SPLIT)
    table = jnp.where(many <= at, 1.0 * NONE, 0.0) + jnp.where(many <= at + 1, 1.0 * NONE * RADIX, 0.0)
    for j in range(width):
        table = table + jnp.where(row == goes[j : j + 1], value[j : j + 1], 0.0)
    groups = jnp.where(lane < leaves, jnp.maximum((many + 1) // 2, 1), 0).astype(f32)
    table = jnp.where(row % SPLIT == COUNT, groups, table)
    total = jnp.sum(groups, axis=1, keepdims=True)
    table = jnp.where((row % SPLIT == TOTAL) & (lane == leaves), total, table)
    square = jnp.concatenate([table, jnp.zeros((P_SIZE - shape[0], P_SIZE), f32)], axis=0).T
    out[...] = square[0 : out.shape[0]].astype(jnp.int32)


def row_of(morton, b, offset):
    return morton.at[pl.ds(offset, morton.shape[0] - CH * P_SIZE + 1)][b * (CH * P_SIZE)]


def fetch(pairs, sems):
    copies = [pltpu.make_async_copy(a, b, sems.at[i]) for i, (a, b) in enumerate(pairs)]
    for copy in copies:
        copy.start()
    return copies


def arrange_kernel(
    morton, near_list, leaf_far, points, probes, skel, sub_skel, basis_hbm, leaf_hbm, box_hbm, sub_hbm,
    geo_lo, geo_hi, near_ids, far_ids, q1_out, packed,
    rows, got, got_too, wide, basis, leaf_tr, box_tr, sub_tr, sems,
):
    copies = fetch(
        ((basis_hbm, basis), (leaf_hbm, leaf_tr), (box_hbm, box_tr), (sub_hbm, sub_tr)), sems
    )
    half = geo_lo.shape[0]
    leaves = 2 * half
    middle = q1_out.shape[0] // 2
    device = lax.axis_index("group") * lax.axis_size("sub") + lax.axis_index("sub")
    sort_list(near_list, near_ids, wide, device * leaves)
    sort_list(leaf_far, far_ids, wide, device * leaves)

    def flip(g, c):
        for j in range(8):
            at = pl.ds(pl.multiple_of((8 * g + j) * P_SIZE, P_SIZE), P_SIZE)
            both = jnp.concatenate(
                [probes[:, at], points[:, at], jnp.zeros((5, P_SIZE), f32)], axis=0
            )
            rows[at, 0:40] = both.T
        return c

    lax.fori_loop(0, leaves // 8, flip, 0)
    for copy in copies:
        copy.wait()

    def gather(b, into):
        for j in range(CH):
            for k in range(P_SIZE):
                into[j, k : k + 1, :] = rows[pl.ds(row_of(morton, b, j * P_SIZE + k), 1), :]

    def combine(b, start, held, geo):
        turned = [held[j].T for j in range(CH)]
        parts = []
        for j in range(CH):
            i = b * CH + j
            at = i - start
            geo[at, 0:40, :] = turned[j][0:40]
            for c in range(3):
                geo[at, 35 + c : 36 + c, 0:64] = skel[c, pl.ds(i, 1), :]
            q0 = hdot_nt(turned[j][0:32], basis[i])
            geo[at, 40:56, 0:64] = q0[0:16]
            geo[at, 40:56, 64:128] = q0[16:32]
            parts.append(q0)
        q1 = jnp.zeros(q1_out.shape[1:], f32)
        for j in range(0, CH, 2):
            two = jnp.concatenate([leaf_tr[b * CH + j], leaf_tr[b * CH + j + 1]], axis=0)
            q1 = q1 + hdot(jnp.concatenate(parts[j : j + 2], axis=1), two)
        q1_out[b] = q1
        return hdot(q1, box_tr[b])

    def two_boxes(g, q2):
        gather(g, got)
        late = combine(middle + jnp.maximum(g - 1, 0), half, got_too, geo_hi)
        gather(middle + g, got_too)
        return q2 + jnp.where(g > 0, late, 0.0) + combine(g, 0, got, geo_lo)

    q2 = lax.fori_loop(0, middle, two_boxes, jnp.zeros((32, packed.shape[1]), f32))
    q2 = q2 + combine(2 * middle - 1, half, got_too, geo_hi)
    packed[0:32, :] = q2
    packed[32:64, :] = hdot(q2, sub_tr[0])
    packed[64:72, :] = jnp.zeros((8, packed.shape[1]), f32)
    for c in range(3):
        packed[64 + c : 65 + c, :] = sub_skel[c]


def prepare_source(block, at, centre_pt, centre_sk, src, xw, src_lo, src_hi, qw):
    geo8 = block[32:40]
    s8, t8 = augmented(coords(geo8, centre_pt))
    src[at] = source_rows(s8).T.astype(bf16)
    turned = jnp.concatenate([geo8[3:8], geo8[0:3]], axis=0)
    ks8, kt8 = augmented(coords(turned, centre_sk))
    low = lax.broadcasted_iota(jnp.int32, (8, P_SIZE), 1) < 64
    ks8 = jnp.where(low, ks8, 0.0)
    src_lo[at] = source_rows(ks8).astype(bf16)
    src_hi[at] = source_rows(pltpu.roll(ks8, 64, 1)).astype(bf16)
    x = block[0:32]
    hi = x.astype(bf16)
    lo = (x - hi.astype(f32)).astype(bf16)
    xw[at] = jnp.concatenate([hi, lo], axis=0)
    q = block[40:56]
    q = jnp.concatenate([q, pltpu.roll(q, 64, 1)], axis=0)
    qhi = q.astype(bf16).astype(f32)
    four = jnp.concatenate([qhi, q - qhi, jnp.zeros((64, P_SIZE), f32)], axis=0)
    qw[at] = four.T[0:64].astype(bf16)
    return t8, kt8


def prepare_target(t8, kt8, at, tgt, tgt_far):
    tgt[at] = target_rows(t8).astype(bf16)
    far = target_rows(kt8)
    tgt_far[at] = jnp.concatenate([far, far], axis=0).T[0:64].astype(bf16)


def clear(refs, at):
    for ref in refs:
        ref[at] = jnp.zeros(ref.shape[1:], ref.dtype)


def batches(ids, lane0, leaves, batch, out, first, part):
    def follow(at):
        leaf, off = at
        more = off + 1 < ids[leaf, lane0 + COUNT]
        return (
            jnp.where(more, leaf, jnp.minimum(leaf + 1, leaves)),
            jnp.where(more, off + 1, 0),
        )

    def take(at):
        got = []
        for _ in range(batch):
            got.append(at)
            at = follow(at)
        return got, at

    def pair(at):
        word = ids[at[0], lane0 + at[1]]
        return at[0], word & (RADIX - 1), word >> 7

    now, at = take((jnp.int32(0), jnp.int32(0)))
    for j in range(batch):
        first(j, pair(now[j]))
    later, at = take(at)

    def one(i, c):
        now, later, at, leaf, acc = c
        for j in range(batch):
            more = part(j, pair(now[j]), pair(later[j]))
            acc = jnp.where(now[j][0] == leaf, acc, 0.0) + more
            leaf = now[j][0]
            out[leaf] = acc
        after, at = take(at)
        return later, after, at, leaf, acc

    total = ids[leaves, lane0 + TOTAL]
    lax.fori_loop(
        0, (total + batch - 1) // batch, one,
        (now, later, at, jnp.int32(0), jnp.zeros(out.shape[1:], f32)),
    )


def halves(k):
    hi = k.astype(bf16)
    return hi, (k - hi.astype(f32)).astype(bf16)


def near_pass(ids, lane0, src, tgt, xw, out, dist):
    def first(j, at):
        leaf, a, b = at
        target = tgt[leaf]
        dist[2 * j] = jnp.dot(src[a], target, preferred_element_type=f32)
        dist[2 * j + 1] = jnp.dot(src[b], target, preferred_element_type=f32)

    def part(j, at, ahead):
        tiles = [jnp.concatenate(halves(profile(dist[2 * j + u])), axis=1) for u in range(2)]
        first(j, ahead)
        acc = jnp.dot(
            jnp.concatenate([xw[at[1]], xw[at[2]]], axis=1),
            jnp.concatenate(tiles, axis=0),
            preferred_element_type=f32,
        )
        return acc[0:32, 0:128] + acc[0:32, 128:256] + acc[32:64, 0:128]

    batches(ids, lane0, tgt.shape[0] - 1, NEAR_BATCH, out, first, part)


def far_pass(ids, lane0, src_lo, src_hi, tgt, qw, out, dist):
    def first(j, at):
        leaf, a, b = at
        source = jnp.concatenate([src_lo[a], src_hi[b]], axis=0)
        dist[j] = jnp.dot(tgt[leaf], source, preferred_element_type=f32)

    def part(j, at, ahead):
        tile = jnp.concatenate(halves(profile(dist[j])), axis=1)
        first(j, ahead)
        a, b = qw[at[1]], qw[at[2]]
        return jnp.dot(
            tile, jnp.concatenate([a, b, a, b], axis=0), preferred_element_type=f32
        )

    batches(ids, lane0, tgt.shape[0] - 1, FAR_BATCH, out, first, part)


def inner_kernel(
    near_ids, far_ids, geo_lo, geo_hi,
    near_out, far_out, tgt, tgt_far, origin,
    src, xw, src_lo, src_hi, qw, near_dist, far_dist,
):
    half = geo_lo.shape[0]
    leaves = 2 * half
    first = geo_lo[0, 32:40, 0:1]
    origin[...] = geo_lo[0, 32:40, :]
    centre_sk = jnp.concatenate([first[3:8], first[0:3]], axis=0)
    sources = (src, xw, src_lo, src_hi, qw)

    def load(g, c):
        for geo, start in ((geo_lo, 0), (geo_hi, half)):
            for j in range(4):
                i = g * 4 + j
                t8, kt8 = prepare_source(geo[i], i + start, first, centre_sk, *sources)
                prepare_target(t8, kt8, i + start, tgt, tgt_far)
        return c

    lax.fori_loop(0, half // 4, load, 0)
    clear(sources, NONE)
    clear((tgt, tgt_far), leaves)
    near_pass(near_ids, 0, src, tgt, xw, near_out, near_dist)
    far_pass(far_ids, 0, src_lo, src_hi, tgt_far, qw, far_out, far_dist)


def centred(block, centre):
    return augmented(coords(block, centre))


def finish_kernel(
    morton, near_ids, far_ids, box_far, sub_far,
    origin, left, right, tgt, tgt_far, near_own, far_own,
    q1, gathered, box_skel3, group_skel3, basis_hbm, leaf_hbm, box_hbm, sub_hbm,
    out,
    near, far, src, xw, src_lo, src_hi, qw, near_dist, far_dist,
    box_skel, group_skel, rows, pad, tall, tall_too, l1s, basis, leaf_tr, box_tr, sub_tr, sems,
    *, subs, groups, box_width, sub_width, near_factor, f0, f1, f2, f3,
):
    copies = fetch(
        ((basis_hbm, basis), (leaf_hbm, leaf_tr), (box_hbm, box_tr), (sub_hbm, sub_tr)), sems
    )
    boxes = q1.shape[0]
    leaves = near.shape[0] - 1
    group = lax.axis_index("group")
    device = group * subs + lax.axis_index("sub")
    first = origin[:, 0:1]
    centre_sk = jnp.concatenate([first[3:8], first[0:3]], axis=0)
    sources = (src, xw, src_lo, src_hi, qw)

    def load(g, c):
        for block, start in ((left, 0), (right, HALO)):
            for j in range(4):
                i = g * 4 + j
                prepare_source(block[i], i + start, first, centre_sk, *sources)
        return c

    lax.fori_loop(0, HALO // 4, load, 0)
    clear(sources, NONE)
    near_pass(near_ids, SPLIT, src, tgt, xw, near, near_dist)
    far_pass(far_ids, SPLIT, src_lo, src_hi, tgt_far, qw, far, far_dist)
    for ref, ref3 in ((box_skel, box_skel3), (group_skel, group_skel3)):
        ref[...] = jnp.zeros_like(ref)
        for b in range(ref.shape[0]):
            for c in range(3):
                ref[b, c : c + 1, :] = ref3[c, b : b + 1, :]
    for copy in copies:
        copy.wait()

    def tile(source8, target8):
        return profile(
            jnp.dot(
                source_rows(source8).T.astype(bf16),
                target_rows(target8).astype(bf16),
                preferred_element_type=f32,
            )
        )

    own = gathered[device, 64:72, :]
    centre = own[:, 0:1]
    target = centred(own, centre)[1]

    def sub_term(j, acc):
        entry = sub_far[j]
        m = jnp.maximum(entry, 0)
        source = centred(gathered[m, 64:72, :], centre)[0]
        term = hdot(gathered[m, 0:32, :], tile(source, target))
        return acc + jnp.where(entry >= 0, term, 0.0)

    many = 4 if sub_width % 4 == 0 else 1

    def sub_terms(g, acc):
        for j in range(many):
            acc = sub_term(g * many + j, acc)
        return acc

    z2 = lax.fori_loop(0, sub_width // many, sub_terms, jnp.zeros(gathered[0, 0:32, :].shape, f32))
    g_own = group_skel[group]
    g_centre = g_own[:, 0:1]
    g_target = centred(g_own, g_centre)[1]

    def group_term(h, acc):
        q3 = lax.fori_loop(
            0, subs, lambda s, t: t + gathered[h * subs + s, 32:64, :], jnp.zeros(z2.shape, f32)
        )
        source = centred(group_skel[h], g_centre)[0]
        return acc + jnp.where(h != group, hdot(q3, tile(source, g_target)), 0.0)

    z3 = jnp.zeros(z2.shape, f32)
    for h in range(groups):
        z3 = group_term(h, z3)
    l2 = z2 * f2 + hdot_nt(z3 * f3, sub_tr[0])

    def box_level(b, c):
        mine = box_skel[b]
        b_centre = mine[:, 0:1]
        b_target = centred(mine, b_centre)[1]

        def box_term(j, acc):
            entry = box_far[j, b]
            m = jnp.maximum(entry - device * boxes, 0)
            source = centred(box_skel[m], b_centre)[0]
            return acc + jnp.where(entry >= 0, hdot(q1[m], tile(source, b_target)), 0.0)

        z1 = jnp.zeros((32, P_SIZE), f32)
        for j in range(box_width):
            z1 = box_term(j, z1)
        l1s[b] = z1 * f1 + hdot_nt(l2, box_tr[b])
        return c

    def box_pair(g, c):
        for j in range(2):
            box_level(2 * g + j, c)
        return c

    lax.fori_loop(0, boxes // 2, box_pair, 0)

    def down(b, into):
        l1 = l1s[b]
        for j in range(CH):
            i = b * CH + j
            turned = (far_own[i] + far[i]).T
            l0 = (turned[0:32] + turned[32:64]) * f0 + hdot_nt(l1, leaf_tr[i])
            pad[j, 0:32, :] = (near_own[i] + near[i]) * near_factor + hdot(l0, basis[i])
        for j in range(CH):
            into[j] = pad[j].T

    def scatter(b, held):
        for j in range(CH):
            for k in range(P_SIZE):
                rows[pl.ds(row_of(morton, b, j * P_SIZE + k), 1), :] = held[j, k : k + 1, :]

    pad[...] = jnp.zeros_like(pad)
    tall_too[...] = jnp.zeros_like(tall_too)

    def two_boxes(g, c):
        scatter(jnp.maximum(2 * g - 1, 1), tall_too)
        down(2 * g, tall)
        scatter(2 * g, tall)
        down(2 * g + 1, tall_too)
        return c

    lax.fori_loop(0, boxes // 2, two_boxes, 0)
    scatter(boxes - 1, tall_too)

    def flip(g, c):
        for j in range(8):
            at = pl.ds(pl.multiple_of((8 * g + j) * P_SIZE, P_SIZE), P_SIZE)
            out[:, at] = rows[at, :].T[0:32]
        return c

    lax.fori_loop(0, leaves // 8, flip, 0)


VMEM = pl.BlockSpec(memory_space=pltpu.VMEM)
SMEM = pl.BlockSpec(memory_space=pltpu.SMEM)
ANY = pl.BlockSpec(memory_space=pl.ANY)
params = pltpu.CompilerParams(vmem_limit_bytes=56 * 2**20)


def body(
    points, probes, morton, near_list, leaf_far, box_far, subtree_far,
    leaf_skeleton, box_skeleton, subtree_skeleton, group_skeleton,
    leaf_basis, leaf_transfer, box_transfer, subtree_transfer,
):
    leaves = near_list.shape[0]
    count = points.shape[1]
    nv = probes.shape[0]
    boxes = box_far.shape[0]
    r0, r1 = leaf_basis.shape[1], box_transfer.shape[1]
    r2, r3 = subtree_transfer.shape[1:]
    subs, groups = lax.axis_size("sub"), lax.axis_size("group")
    i32 = jnp.int32
    front = lambda a: jnp.transpose(a, (1, 0, 2))
    bases = (leaf_basis, leaf_transfer, box_transfer, subtree_transfer)
    held = [pltpu.VMEM(a.shape, f32) for a in bases]
    sems = pltpu.SemaphoreType.DMA((len(bases),))

    geo_lo, geo_hi, near_ids, far_ids, q1, packed = pl.pallas_call(
        arrange_kernel,
        out_shape=(
            jax.ShapeDtypeStruct((leaves // 2, 56, P_SIZE), f32),
            jax.ShapeDtypeStruct((leaves // 2, 56, P_SIZE), f32),
            jax.ShapeDtypeStruct((leaves + 8, P_SIZE), i32),
            jax.ShapeDtypeStruct((leaves + 8, P_SIZE), i32),
            jax.ShapeDtypeStruct((boxes, nv, r1), f32),
            jax.ShapeDtypeStruct((72, r2), f32),
        ),
        in_specs=[SMEM] + [VMEM] * 6 + [ANY] * 4,
        out_specs=(VMEM,) * 6,
        scratch_shapes=[
            pltpu.VMEM((count, P_SIZE), f32),
            pltpu.VMEM((CH, P_SIZE, P_SIZE), f32),
            pltpu.VMEM((CH, P_SIZE, P_SIZE), f32),
            pltpu.VMEM((2 * SPLIT, P_SIZE), i32),
        ]
        + held
        + [sems],
        compiler_params=params,
        name="arrange",
    )(
        morton, near_list.T, leaf_far.T, points, probes, front(leaf_skeleton),
        front(subtree_skeleton), *bases,
    )

    both = ("group", "sub")
    ends = subs * groups - 1
    left = lax.ppermute(geo_hi, both, [(i, i + 1) for i in range(ends)])
    right = lax.ppermute(geo_lo, both, [(i + 1, i) for i in range(ends)])
    gathered = lax.all_gather(packed, both, axis=0)

    acc_shapes = ((leaves + 1, nv, P_SIZE), (leaves + 1, r0, P_SIZE))
    tables = [
        pltpu.VMEM((NONE + 1, P_SIZE, 64), bf16),
        pltpu.VMEM((NONE + 1, 2 * nv, P_SIZE), bf16),
        pltpu.VMEM((NONE + 1, 64, P_SIZE), bf16),
        pltpu.VMEM((NONE + 1, 64, P_SIZE), bf16),
        pltpu.VMEM((NONE + 1, 64, P_SIZE), bf16),
        pltpu.VMEM((2 * NEAR_BATCH, P_SIZE, P_SIZE), f32),
        pltpu.VMEM((FAR_BATCH, 64, P_SIZE), f32),
    ]
    near, far, tgt, tgt_far, origin = pl.pallas_call(
        inner_kernel,
        out_shape=tuple(jax.ShapeDtypeStruct(a, f32) for a in acc_shapes)
        + (
            jax.ShapeDtypeStruct((leaves + 1, 64, P_SIZE), bf16),
            jax.ShapeDtypeStruct((leaves + 1, 64, P_SIZE), bf16),
            jax.ShapeDtypeStruct((8, P_SIZE), f32),
        ),
        in_specs=[SMEM] * 2 + [VMEM] * 2,
        out_specs=(VMEM,) * 5,
        scratch_shapes=tables,
        compiler_params=params,
        cost_estimate=pl.CostEstimate(flops=2 * 10**10, bytes_accessed=10**7, transcendentals=5 * 10**7),
        name="inner",
    )(near_ids, far_ids, geo_lo, geo_hi)

    return pl.pallas_call(
        functools.partial(
            finish_kernel,
            subs=subs,
            groups=groups,
            box_width=box_far.shape[1],
            sub_width=subtree_far.shape[1],
            near_factor=(P_SIZE * near_list.shape[1]) ** -0.5,
            f0=(r0 * leaf_far.shape[1]) ** -0.5,
            f1=(r1 * box_far.shape[1]) ** -0.5,
            f2=(r2 * subtree_far.shape[1]) ** -0.5,
            f3=r3**-0.5,
        ),
        out_shape=jax.ShapeDtypeStruct((nv, count), f32),
        in_specs=[SMEM] * 5 + [VMEM] * 11 + [ANY] * 4,
        out_specs=VMEM,
        scratch_shapes=[pltpu.VMEM(a, f32) for a in acc_shapes]
        + tables
        + [
            pltpu.VMEM((boxes, 8, r1), f32),
            pltpu.VMEM((groups, 8, r3), f32),
            pltpu.VMEM((count, P_SIZE), f32),
            pltpu.VMEM((CH, P_SIZE, P_SIZE), f32),
            pltpu.VMEM((CH, P_SIZE, P_SIZE), f32),
            pltpu.VMEM((CH, P_SIZE, P_SIZE), f32),
            pltpu.VMEM((boxes, nv, P_SIZE), f32),
        ]
        + held
        + [sems],
        compiler_params=params,
        name="finish",
    )(
        morton, near_ids, far_ids, box_far.T, subtree_far.reshape(-1),
        origin, left, right, tgt, tgt_far, near, far,
        q1, gathered, front(box_skeleton), front(group_skeleton), *bases,
    )


def solution(mesh):
    two = ("group", "sub")
    placed = (
        (P(None, two),) * 2
        + (P(two),)
        + (P(two, None),) * 4
        + (P(two, None, None),) * 3
        + (P(),)
        + (P(two, None, None),) * 4
    )
    return jax.shard_map(
        body, mesh=mesh, in_specs=placed, out_specs=P(None, two), check_vma=False
    )
```

```python
import functools
import math

import jax
import jax.numpy as jnp
from jax import lax
from jax.experimental import pallas as pl
from jax.experimental.pallas import tpu as pltpu
from jax.sharding import PartitionSpec as P

P_SIZE = 128
CH = 8
HALO = 32
SLOTS = 16
NONE = 2 * HALO
RADIX = 128
FLAT = 8 * P_SIZE
REACH = FLAT - 48
NEAR_BATCH = 16
FAR_BATCH = 14

highest = lax.Precision.HIGHEST
scale = math.sqrt(3.0) / 12.0
soft = 0.0001 * scale * scale
log2e = math.log2(math.e)
f32 = jnp.float32
bf16 = jnp.bfloat16
NT = (((1,), (1,)), ((), ()))


def hdot(a, b):
    return jnp.dot(a, b, precision=highest, preferred_element_type=f32)


def hdot_nt(a, b):
    return lax.dot_general(a, b, NT, precision=highest, preferred_element_type=f32)


def profile(squared):
    squared = jnp.maximum(squared, soft)
    u = squared * lax.rsqrt(squared)
    return (1.0 + u) * jnp.exp2(u * -log2e)


def split3(v):
    high = v.astype(bf16).astype(f32)
    rest = v - high
    mid = rest.astype(bf16).astype(f32)
    return high, mid, rest - mid


def augmented(x):
    row = lax.broadcasted_iota(jnp.int32, x.shape, 0)
    norm = jnp.sum(x * x, axis=0, keepdims=True)
    source = jnp.where(row < 3, -2.0 * x, jnp.where(row == 3, 1.0, jnp.where(row == 4, norm + soft, 0.0)))
    target = jnp.where(row < 3, x, jnp.where(row == 3, norm, jnp.where(row == 4, 1.0, 0.0)))
    return source, target


def source_rows(v):
    h, m, lo = split3(v)
    return jnp.concatenate([h, m, h, m, lo, h, lo, m], axis=0)


def target_rows(v):
    h, m, lo = split3(v)
    return jnp.concatenate([h, h, m, m, h, lo, m, lo], axis=0)


def coords(block, centre):
    row = lax.broadcasted_iota(jnp.int32, block.shape, 0)
    return jnp.where(row < 3, (block - centre) * scale, 0.0)


def sort_list(ids_ref, outs, wide, base):
    width, leaves = ids_ref.shape
    wide[...] = jnp.full(wide.shape, -1, jnp.int32)
    wide[0:width, 0:leaves] = ids_ref[...]
    ids = wide[...]
    shape = ids.shape
    place = ids - base
    valid = ids >= 0
    own = valid & (place >= 0) & (place < leaves)
    other = valid & jnp.logical_not(own)
    slot = jnp.where(own, place, jnp.where(place < 0, place + HALO, place - leaves + HALO))
    ones = jnp.concatenate([own.astype(f32), other.astype(f32)], axis=1)
    row = lax.broadcasted_iota(jnp.int32, shape, 0)
    lane = lax.broadcasted_iota(jnp.int32, shape, 1)
    square = (shape[0], shape[0])
    before = lax.broadcasted_iota(jnp.int32, square, 1) < lax.broadcasted_iota(jnp.int32, square, 0)
    rank = jnp.dot(
        before.astype(f32).astype(bf16), ones.astype(bf16), preferred_element_type=f32
    ).astype(jnp.int32)
    total = jnp.sum(ones, axis=0, keepdims=True).astype(jnp.int32)
    value = slot.astype(f32)
    square = (P_SIZE, P_SIZE)
    ahead = lax.broadcasted_iota(jnp.int32, square, 0) < lax.broadcasted_iota(jnp.int32, square, 1)
    ahead = ahead.astype(f32).astype(bf16)
    lane8 = lane[0:8]
    row8 = row[0:8]
    for part, out in enumerate(outs):
        mask = (own, other)[part]
        order = jnp.where(mask, rank[:, part * P_SIZE : (part + 1) * P_SIZE], -1)
        goes = jnp.where(order % 2 == 1, SLOTS + order // 2, order // 2)
        goes = jnp.where(mask, goes, -1)
        many = total[:, part * P_SIZE : (part + 1) * P_SIZE]
        at = jnp.where(row < SLOTS, 2 * row, 2 * (row - SLOTS) + 1)
        table = jnp.where(many <= at, 1.0 * NONE, 0.0)
        for j in range(width):
            table = table + jnp.where(row == goes[j : j + 1], value[j : j + 1], 0.0)
        groups = jnp.where(lane8 < leaves, jnp.maximum((many + 1) // 2, 1), 0)
        start = jnp.dot(
            groups.astype(f32).astype(bf16), ahead, preferred_element_type=f32
        ).astype(jnp.int32)
        stop = jnp.where(lane8 == leaves, FLAT, start + groups)
        extra = jnp.where(
            row8 == 0, start // 32, jnp.where(row8 == 1, start % 32, jnp.where(row8 == 2, lane8, 0))
        )
        look = jnp.concatenate([table, extra.astype(f32)], axis=0).astype(bf16)
        ends = jnp.concatenate(
            [jnp.where(row8 == 0, start, stop).astype(f32), jnp.zeros((P_SIZE - 8, P_SIZE), f32)],
            axis=0,
        ).T
        begin, end = ends[:, 0:1], ends[:, 1:2]
        spot = lax.broadcasted_iota(jnp.int32, square, 1).astype(f32)
        for t in range(FLAT // P_SIZE):
            here = spot + 1.0 * t * P_SIZE
            hot = ((begin <= here) & (here < end)).astype(f32).astype(bf16)
            found = jnp.dot(look, hot, preferred_element_type=f32)
            k = here[0:1] - (found[32:33] * 32.0 + found[33:34])
            pick = row[0:SLOTS].astype(f32) == k
            a = jnp.sum(jnp.where(pick, found[0:SLOTS], 0.0), axis=0, keepdims=True)
            b = jnp.sum(jnp.where(pick, found[SLOTS : 2 * SLOTS], 0.0), axis=0, keepdims=True)
            word = a + b * RADIX + found[34:35] * (RADIX * RADIX)
            out[t : t + 1, :] = word.astype(jnp.int32)
        count = start[0:1, leaves : leaves + 1]
        out[7:8, P_SIZE - 1 : P_SIZE] = count


def row_of(morton, b, offset):
    return morton.at[pl.ds(offset, morton.shape[0] - CH * P_SIZE + 1)][b * (CH * P_SIZE)]


def fetch(pairs, sems):
    copies = [pltpu.make_async_copy(a, b, sems.at[i]) for i, (a, b) in enumerate(pairs)]
    for copy in copies:
        copy.start()
    return copies


def arrange_kernel(
    morton, near_list, leaf_far, points, probes, skel, sub_skel, basis_hbm, leaf_hbm, box_hbm, sub_hbm,
    geo_lo, geo_hi, near_ids, near_ids_out, far_ids, far_ids_out, q1_out, packed,
    rows, got, got_too, wide, basis, leaf_tr, box_tr, sub_tr, sems,
):
    copies = fetch(
        ((basis_hbm, basis), (leaf_hbm, leaf_tr), (box_hbm, box_tr), (sub_hbm, sub_tr)), sems
    )
    half = geo_lo.shape[0]
    leaves = 2 * half
    middle = q1_out.shape[0] // 2
    device = lax.axis_index("group") * lax.axis_size("sub") + lax.axis_index("sub")
    sort_list(near_list, (near_ids, near_ids_out), wide, device * leaves)
    sort_list(leaf_far, (far_ids, far_ids_out), wide, device * leaves)

    def flip(g, c):
        for j in range(8):
            at = pl.ds(pl.multiple_of((8 * g + j) * P_SIZE, P_SIZE), P_SIZE)
            both = jnp.concatenate(
                [probes[:, at], points[:, at], jnp.zeros((5, P_SIZE), f32)], axis=0
            )
            rows[at, 0:40] = both.T
        return c

    lax.fori_loop(0, leaves // 8, flip, 0)
    for copy in copies:
        copy.wait()

    def gather(b, into):
        for j in range(CH):
            for k in range(P_SIZE):
                into[j, k : k + 1, :] = rows[pl.ds(row_of(morton, b, j * P_SIZE + k), 1), :]

    def combine(b, start, held, geo):
        turned = [held[j].T for j in range(CH)]
        parts = []
        for j in range(CH):
            i = b * CH + j
            at = i - start
            geo[at, 0:40, :] = turned[j][0:40]
            for c in range(3):
                geo[at, 35 + c : 36 + c, 0:64] = skel[c, pl.ds(i, 1), :]
            q0 = hdot_nt(turned[j][0:32], basis[i])
            geo[at, 40:56, 0:64] = q0[0:16]
            geo[at, 40:56, 64:128] = q0[16:32]
            parts.append(q0)
        q1 = jnp.zeros(q1_out.shape[1:], f32)
        for j in range(0, CH, 2):
            two = jnp.concatenate([leaf_tr[b * CH + j], leaf_tr[b * CH + j + 1]], axis=0)
            q1 = q1 + hdot(jnp.concatenate(parts[j : j + 2], axis=1), two)
        q1_out[b] = q1
        return hdot(q1, box_tr[b])

    def two_boxes(g, q2):
        gather(g, got)
        late = combine(middle + jnp.maximum(g - 1, 0), half, got_too, geo_hi)
        gather(middle + g, got_too)
        return q2 + jnp.where(g > 0, late, 0.0) + combine(g, 0, got, geo_lo)

    q2 = lax.fori_loop(0, middle, two_boxes, jnp.zeros((32, packed.shape[1]), f32))
    q2 = q2 + combine(2 * middle - 1, half, got_too, geo_hi)
    packed[0:32, :] = q2
    packed[32:64, :] = hdot(q2, sub_tr[0])
    packed[64:72, :] = jnp.zeros((8, packed.shape[1]), f32)
    for c in range(3):
        packed[64 + c : 65 + c, :] = sub_skel[c]


def prepare_source(block, at, centre_pt, centre_sk, src, xw, src_lo, src_hi, qw):
    geo8 = block[32:40]
    s8, t8 = augmented(coords(geo8, centre_pt))
    src[at] = source_rows(s8).T.astype(bf16)
    turned = jnp.concatenate([geo8[3:8], geo8[0:3]], axis=0)
    ks8, kt8 = augmented(coords(turned, centre_sk))
    low = lax.broadcasted_iota(jnp.int32, (8, P_SIZE), 1) < 64
    ks8 = jnp.where(low, ks8, 0.0)
    src_lo[at] = source_rows(ks8).astype(bf16)
    src_hi[at] = source_rows(pltpu.roll(ks8, 64, 1)).astype(bf16)
    x = block[0:32]
    hi = x.astype(bf16)
    lo = (x - hi.astype(f32)).astype(bf16)
    xw[at] = jnp.concatenate([hi, lo], axis=0)
    q = block[40:56]
    q = jnp.concatenate([q, pltpu.roll(q, 64, 1)], axis=0)
    qhi = q.astype(bf16).astype(f32)
    four = jnp.concatenate([qhi, q - qhi, jnp.zeros((64, P_SIZE), f32)], axis=0)
    qw[at] = four.T[0:64].astype(bf16)
    return t8, kt8


def prepare_target(t8, kt8, at, tgt, tgt_far):
    tgt[at] = target_rows(t8).astype(bf16)
    far = target_rows(kt8)
    tgt_far[at] = jnp.concatenate([far, far], axis=0).T[0:64].astype(bf16)


def clear(refs, at):
    for ref in refs:
        ref[at] = jnp.zeros(ref.shape[1:], ref.dtype)


def stream(ids, leaves, batch, out, first, part):
    def entry(i, j):
        word = ids.at[pl.ds(j, REACH)][i * batch]
        return word >> 14, word & (RADIX - 1), (word >> 7) & (RADIX - 1)

    def start():
        for j in range(batch):
            first(j, entry(0, j))
        return jnp.int32(0), jnp.zeros(out.shape[1:], f32)

    def steps(i, c):
        leaf, acc = c
        for j in range(batch):
            now = entry(i, j)
            more = part(j, now, entry(i, j + batch))
            acc = jnp.where(now[0] == leaf, acc, 0.0) + more
            leaf = now[0]
            out[leaf] = acc
            yield None
        yield leaf, acc

    trips = (ids[FLAT - 1] + batch - 1) // batch
    return start, steps, trips


def run(*streams):
    def one(i, c):
        work = [steps(i, held) for (_, steps, _), held in zip(streams, c)]
        done = [None] * len(work)
        while any(d is None for d in done):
            done = [next(w) if d is None else d for w, d in zip(work, done)]
        return tuple(done)

    trips = functools.reduce(jnp.maximum, [t for _, _, t in streams])
    lax.fori_loop(0, trips, one, tuple(start() for start, _, _ in streams))


def halves(k):
    hi = k.astype(bf16)
    return hi, (k - hi.astype(f32)).astype(bf16)


def near_pass(ids, src, tgt, xw, out, dist):
    def first(j, at):
        leaf, a, b = at
        target = tgt[leaf]
        dist[2 * j] = jnp.dot(src[a], target, preferred_element_type=f32)
        dist[2 * j + 1] = jnp.dot(src[b], target, preferred_element_type=f32)

    def part(j, at, ahead):
        tiles = [jnp.concatenate(halves(profile(dist[2 * j + u])), axis=1) for u in range(2)]
        first(j, ahead)
        acc = jnp.dot(
            jnp.concatenate([xw[at[1]], xw[at[2]]], axis=1),
            jnp.concatenate(tiles, axis=0),
            preferred_element_type=f32,
        )
        return acc[0:32, 0:128] + acc[0:32, 128:256] + acc[32:64, 0:128]

    return stream(ids, tgt.shape[0] - 1, NEAR_BATCH, out, first, part)


def far_pass(ids, src_lo, src_hi, tgt, qw, out, dist):
    def first(j, at):
        leaf, a, b = at
        source = jnp.concatenate([src_lo[a], src_hi[b]], axis=0)
        dist[j] = jnp.dot(tgt[leaf], source, preferred_element_type=f32)

    def part(j, at, ahead):
        tile = jnp.concatenate(halves(profile(dist[j])), axis=1)
        first(j, ahead)
        a, b = qw[at[1]], qw[at[2]]
        return jnp.dot(
            tile, jnp.concatenate([a, b, a, b], axis=0), preferred_element_type=f32
        )

    return stream(ids, tgt.shape[0] - 1, FAR_BATCH, out, first, part)


def inner_kernel(
    near_ids, far_ids, geo_lo, geo_hi,
    near_out, far_out, tgt, tgt_far, origin,
    src, xw, src_lo, src_hi, qw, near_dist, far_dist,
):
    half = geo_lo.shape[0]
    leaves = 2 * half
    first = geo_lo[0, 32:40, 0:1]
    origin[...] = geo_lo[0, 32:40, :]
    centre_sk = jnp.concatenate([first[3:8], first[0:3]], axis=0)
    sources = (src, xw, src_lo, src_hi, qw)

    def load(g, c):
        for geo, start in ((geo_lo, 0), (geo_hi, half)):
            for j in range(4):
                i = g * 4 + j
                t8, kt8 = prepare_source(geo[i], i + start, first, centre_sk, *sources)
                prepare_target(t8, kt8, i + start, tgt, tgt_far)
        return c

    lax.fori_loop(0, half // 4, load, 0)
    clear(sources, NONE)
    clear((tgt, tgt_far), leaves)
    run(
        near_pass(near_ids, src, tgt, xw, near_out, near_dist),
        far_pass(far_ids, src_lo, src_hi, tgt_far, qw, far_out, far_dist),
    )


def outer_kernel(
    near_ids, far_ids, origin, left, right, tgt, tgt_far,
    near_out, far_out,
    src, xw, src_lo, src_hi, qw, near_dist, far_dist,
):
    first = origin[:, 0:1]
    centre_sk = jnp.concatenate([first[3:8], first[0:3]], axis=0)
    sources = (src, xw, src_lo, src_hi, qw)

    def load(g, c):
        for block, start in ((left, 0), (right, HALO)):
            for j in range(4):
                i = g * 4 + j
                prepare_source(block[i], i + start, first, centre_sk, *sources)
        return c

    lax.fori_loop(0, HALO // 4, load, 0)
    clear(sources, NONE)
    run(
        near_pass(near_ids, src, tgt, xw, near_out, near_dist),
        far_pass(far_ids, src_lo, src_hi, tgt_far, qw, far_out, far_dist),
    )


def centred(block, centre):
    return augmented(coords(block, centre))


def finish_kernel(
    morton, box_far, sub_far, near_own, far_own, near, far,
    q1, family, tops, box_skel3, group_skel3, basis_hbm, leaf_hbm, box_hbm, sub_hbm,
    out,
    box_skel, group_skel, rows, pad, tall, tall_too, l1s, basis, leaf_tr, box_tr, sub_tr, sems,
    *, groups, box_width, sub_width, near_factor, f0, f1, f2, f3,
):
    copies = fetch(
        ((basis_hbm, basis), (leaf_hbm, leaf_tr), (box_hbm, box_tr), (sub_hbm, sub_tr)), sems
    )
    boxes = q1.shape[0]
    leaves = near.shape[0] - 1
    group = lax.axis_index("group")
    sub = lax.axis_index("sub")
    subs = lax.axis_size("sub")
    device = group * subs + sub
    for ref, ref3 in ((box_skel, box_skel3), (group_skel, group_skel3)):
        ref[...] = jnp.zeros_like(ref)
        for b in range(ref.shape[0]):
            for c in range(3):
                ref[b, c : c + 1, :] = ref3[c, b : b + 1, :]
    for copy in copies:
        copy.wait()

    def tile(source8, target8):
        return profile(
            jnp.dot(
                source_rows(source8).T.astype(bf16),
                target_rows(target8).astype(bf16),
                preferred_element_type=f32,
            )
        )

    own = family[sub, 64:72, :]
    centre = own[:, 0:1]
    target = centred(own, centre)[1]

    def sub_term(j, acc):
        entry = sub_far[j]
        m = jnp.maximum(entry - group * subs, 0)
        source = centred(family[m, 64:72, :], centre)[0]
        term = hdot(family[m, 0:32, :], tile(source, target))
        return acc + jnp.where(entry >= 0, term, 0.0)

    many = 4 if sub_width % 4 == 0 else 1

    def sub_terms(g, acc):
        for j in range(many):
            acc = sub_term(g * many + j, acc)
        return acc

    z2 = lax.fori_loop(0, sub_width // many, sub_terms, jnp.zeros((32, family.shape[2]), f32))
    g_own = group_skel[group]
    g_centre = g_own[:, 0:1]
    g_target = centred(g_own, g_centre)[1]

    def group_term(h, acc):
        source = centred(group_skel[h], g_centre)[0]
        return acc + jnp.where(h != group, hdot(tops[h], tile(source, g_target)), 0.0)

    z3 = jnp.zeros(z2.shape, f32)
    for h in range(groups):
        z3 = group_term(h, z3)
    l2 = z2 * f2 + hdot_nt(z3 * f3, sub_tr[0])

    def box_level(b, c):
        mine = box_skel[b]
        b_centre = mine[:, 0:1]
        b_target = centred(mine, b_centre)[1]

        def box_term(j, acc):
            entry = box_far[j, b]
            m = jnp.maximum(entry - device * boxes, 0)
            source = centred(box_skel[m], b_centre)[0]
            return acc + jnp.where(entry >= 0, hdot(q1[m], tile(source, b_target)), 0.0)

        z1 = jnp.zeros((32, P_SIZE), f32)
        for j in range(box_width):
            z1 = box_term(j, z1)
        l1s[b] = z1 * f1 + hdot_nt(l2, box_tr[b])
        return c

    def box_pair(g, c):
        for j in range(2):
            box_level(2 * g + j, c)
        return c

    lax.fori_loop(0, boxes // 2, box_pair, 0)

    def down(b, into):
        l1 = l1s[b]
        for j in range(CH):
            i = b * CH + j
            turned = (far_own[i] + far[i]).T
            l0 = (turned[0:32] + turned[32:64]) * f0 + hdot_nt(l1, leaf_tr[i])
            pad[j, 0:32, :] = (near_own[i] + near[i]) * near_factor + hdot(l0, basis[i])
        for j in range(CH):
            into[j] = pad[j].T

    def scatter(b, held):
        for j in range(CH):
            for k in range(P_SIZE):
                rows[pl.ds(row_of(morton, b, j * P_SIZE + k), 1), :] = held[j, k : k + 1, :]

    pad[...] = jnp.zeros_like(pad)
    tall_too[...] = jnp.zeros_like(tall_too)

    def two_boxes(g, c):
        scatter(jnp.maximum(2 * g - 1, 1), tall_too)
        down(2 * g, tall)
        scatter(2 * g, tall)
        down(2 * g + 1, tall_too)
        return c

    lax.fori_loop(0, boxes // 2, two_boxes, 0)
    scatter(boxes - 1, tall_too)

    def flip(g, c):
        for j in range(8):
            at = pl.ds(pl.multiple_of((8 * g + j) * P_SIZE, P_SIZE), P_SIZE)
            out[:, at] = rows[at, :].T[0:32]
        return c

    lax.fori_loop(0, leaves // 8, flip, 0)


VMEM = pl.BlockSpec(memory_space=pltpu.VMEM)
SMEM = pl.BlockSpec(memory_space=pltpu.SMEM)
ANY = pl.BlockSpec(memory_space=pl.ANY)
params = pltpu.CompilerParams(vmem_limit_bytes=56 * 2**20)


def body(
    points, probes, morton, near_list, leaf_far, box_far, subtree_far,
    leaf_skeleton, box_skeleton, subtree_skeleton, group_skeleton,
    leaf_basis, leaf_transfer, box_transfer, subtree_transfer,
):
    leaves = near_list.shape[0]
    count = points.shape[1]
    nv = probes.shape[0]
    boxes = box_far.shape[0]
    r0, r1 = leaf_basis.shape[1], box_transfer.shape[1]
    r2, r3 = subtree_transfer.shape[1:]
    subs, groups = lax.axis_size("sub"), lax.axis_size("group")
    i32 = jnp.int32
    front = lambda a: jnp.transpose(a, (1, 0, 2))
    bases = (leaf_basis, leaf_transfer, box_transfer, subtree_transfer)
    held = [pltpu.VMEM(a.shape, f32) for a in bases]
    sems = pltpu.SemaphoreType.DMA((len(bases),))

    geo_lo, geo_hi, near_ids, near_ids_out, far_ids, far_ids_out, q1, packed = pl.pallas_call(
        arrange_kernel,
        out_shape=(
            jax.ShapeDtypeStruct((leaves // 2, 56, P_SIZE), f32),
            jax.ShapeDtypeStruct((leaves // 2, 56, P_SIZE), f32),
            *[jax.ShapeDtypeStruct((FLAT // P_SIZE, P_SIZE), i32)] * 4,
            jax.ShapeDtypeStruct((boxes, nv, r1), f32),
            jax.ShapeDtypeStruct((72, r2), f32),
        ),
        in_specs=[SMEM] + [VMEM] * 6 + [ANY] * 4,
        out_specs=(VMEM,) * 8,
        scratch_shapes=[
            pltpu.VMEM((count, P_SIZE), f32),
            pltpu.VMEM((CH, P_SIZE, P_SIZE), f32),
            pltpu.VMEM((CH, P_SIZE, P_SIZE), f32),
            pltpu.VMEM((2 * SLOTS, P_SIZE), i32),
        ]
        + held
        + [sems],
        compiler_params=params,
        name="arrange",
    )(
        morton, near_list.T, leaf_far.T, points, probes, front(leaf_skeleton),
        front(subtree_skeleton), *bases,
    )

    both = ("group", "sub")
    ends = subs * groups - 1
    left = lax.ppermute(geo_hi, both, [(i, i + 1) for i in range(ends)])
    right = lax.ppermute(geo_lo, both, [(i + 1, i) for i in range(ends)])
    family = lax.all_gather(packed, "sub", axis=0)

    acc_shapes = ((leaves + 1, nv, P_SIZE), (leaves + 1, r0, P_SIZE))
    tables = [
        pltpu.VMEM((NONE + 1, P_SIZE, 64), bf16),
        pltpu.VMEM((NONE + 1, 2 * nv, P_SIZE), bf16),
        pltpu.VMEM((NONE + 1, 64, P_SIZE), bf16),
        pltpu.VMEM((NONE + 1, 64, P_SIZE), bf16),
        pltpu.VMEM((NONE + 1, 64, P_SIZE), bf16),
        pltpu.VMEM((2 * NEAR_BATCH, P_SIZE, P_SIZE), f32),
        pltpu.VMEM((FAR_BATCH, 64, P_SIZE), f32),
    ]
    near, far, tgt, tgt_far, origin = pl.pallas_call(
        inner_kernel,
        out_shape=tuple(jax.ShapeDtypeStruct(a, f32) for a in acc_shapes)
        + (
            jax.ShapeDtypeStruct((leaves + 1, 64, P_SIZE), bf16),
            jax.ShapeDtypeStruct((leaves + 1, 64, P_SIZE), bf16),
            jax.ShapeDtypeStruct((8, P_SIZE), f32),
        ),
        in_specs=[SMEM] * 2 + [VMEM] * 2,
        out_specs=(VMEM,) * 5,
        scratch_shapes=tables,
        compiler_params=params,
        cost_estimate=pl.CostEstimate(flops=2 * 10**10, bytes_accessed=10**7, transcendentals=5 * 10**7),
        name="inner",
    )(near_ids.reshape(-1), far_ids.reshape(-1), geo_lo, geo_hi)

    tops = lax.all_gather(jnp.sum(family[:, nv : 2 * nv, :], axis=0), "group", axis=0)
    near_halo, far_halo = pl.pallas_call(
        outer_kernel,
        out_shape=tuple(jax.ShapeDtypeStruct(a, f32) for a in acc_shapes),
        in_specs=[SMEM] * 2 + [VMEM] * 5,
        out_specs=(VMEM,) * 2,
        scratch_shapes=tables,
        compiler_params=params,
        cost_estimate=pl.CostEstimate(flops=10**10, bytes_accessed=10**7, transcendentals=3 * 10**7),
        name="outer",
    )(near_ids_out.reshape(-1), far_ids_out.reshape(-1), origin, left, right, tgt, tgt_far)

    return pl.pallas_call(
        functools.partial(
            finish_kernel,
            groups=groups,
            box_width=box_far.shape[1],
            sub_width=subtree_far.shape[1],
            near_factor=(P_SIZE * near_list.shape[1]) ** -0.5,
            f0=(r0 * leaf_far.shape[1]) ** -0.5,
            f1=(r1 * box_far.shape[1]) ** -0.5,
            f2=(r2 * subtree_far.shape[1]) ** -0.5,
            f3=r3**-0.5,
        ),
        out_shape=jax.ShapeDtypeStruct((nv, count), f32),
        in_specs=[SMEM] * 3 + [VMEM] * 9 + [ANY] * 4,
        out_specs=VMEM,
        scratch_shapes=[
            pltpu.VMEM((boxes, 8, r1), f32),
            pltpu.VMEM((groups, 8, r3), f32),
            pltpu.VMEM((count, P_SIZE), f32),
            pltpu.VMEM((CH, P_SIZE, P_SIZE), f32),
            pltpu.VMEM((CH, P_SIZE, P_SIZE), f32),
            pltpu.VMEM((CH, P_SIZE, P_SIZE), f32),
            pltpu.VMEM((boxes, nv, P_SIZE), f32),
        ]
        + held
        + [sems],
        compiler_params=params,
        name="finish",
    )(
        morton, box_far.T, subtree_far.reshape(-1), near, far, near_halo, far_halo,
        q1, family, tops, front(box_skeleton), front(group_skeleton), *bases,
    )


def solution(mesh):
    two = ("group", "sub")
    placed = (
        (P(None, two),) * 2
        + (P(two),)
        + (P(two, None),) * 4
        + (P(two, None, None),) * 3
        + (P(),)
        + (P(two, None, None),) * 4
    )
    return jax.shard_map(
        body, mesh=mesh, in_specs=placed, out_specs=P(None, two), check_vma=False
    )
```

```python
import functools
import math

import jax
import jax.numpy as jnp
from jax import lax
from jax.experimental import pallas as pl
from jax.experimental.pallas import tpu as pltpu
from jax.sharding import PartitionSpec as P

P_SIZE = 128
CH = 8
HALO = 32
SLOTS = 16
NONE = 2 * HALO
RADIX = 128
FLAT = 8 * P_SIZE
REACH = FLAT - 48
NEAR_BATCH = 16
FAR_BATCH = 14

scale = math.sqrt(3.0) / 12.0
soft = 0.0001 * scale * scale
log2e = math.log2(math.e)
f32 = jnp.float32
bf16 = jnp.bfloat16
NT = (((1,), (1,)), ((), ()))


def halves(k):
    hi = k.astype(bf16)
    return hi, (k - hi.astype(f32)).astype(bf16)


def hdot(a, b):
    ah, al = halves(a)
    bh, bl = halves(b)
    return jnp.dot(
        jnp.concatenate([ah, al, ah], axis=1),
        jnp.concatenate([bh, bh, bl], axis=0),
        preferred_element_type=f32,
    )


def hdot_nt(a, b):
    ah, al = halves(a)
    bh, bl = halves(b)
    return lax.dot_general(
        jnp.concatenate([ah, al, ah], axis=1),
        jnp.concatenate([bh, bh, bl], axis=1),
        NT,
        preferred_element_type=f32,
    )


def weigh(q, k):
    n = k.shape[1]
    both = jnp.dot(
        jnp.concatenate(halves(q), axis=0),
        jnp.concatenate(halves(k), axis=1),
        preferred_element_type=f32,
    )
    return both[0:32, 0:n] + both[0:32, n:] + both[32:64, 0:n]


def profile(squared):
    squared = jnp.maximum(squared, soft)
    u = squared * lax.rsqrt(squared)
    return (1.0 + u) * jnp.exp2(u * -log2e)


def split3(v):
    high = v.astype(bf16).astype(f32)
    rest = v - high
    mid = rest.astype(bf16).astype(f32)
    return high, mid, rest - mid


def augmented(x):
    row = lax.broadcasted_iota(jnp.int32, x.shape, 0)
    norm = jnp.sum(x * x, axis=0, keepdims=True)
    source = jnp.where(row < 3, -2.0 * x, jnp.where(row == 3, 1.0, jnp.where(row == 4, norm + soft, 0.0)))
    target = jnp.where(row < 3, x, jnp.where(row == 3, norm, jnp.where(row == 4, 1.0, 0.0)))
    return source, target


def source_rows(v):
    h, m, lo = split3(v)
    return jnp.concatenate([h, m, h, m, lo, h, lo, m], axis=0)


def target_rows(v):
    h, m, lo = split3(v)
    return jnp.concatenate([h, h, m, m, h, lo, m, lo], axis=0)


def coords(block, centre):
    row = lax.broadcasted_iota(jnp.int32, block.shape, 0)
    return jnp.where(row < 3, (block - centre) * scale, 0.0)


def sort_list(ids_ref, outs, wide, base):
    width, leaves = ids_ref.shape
    wide[...] = jnp.full(wide.shape, -1, jnp.int32)
    wide[0:width, 0:leaves] = ids_ref[...]
    ids = wide[...]
    shape = ids.shape
    place = ids - base
    valid = ids >= 0
    own = valid & (place >= 0) & (place < leaves)
    other = valid & jnp.logical_not(own)
    slot = jnp.where(own, place, jnp.where(place < 0, place + HALO, place - leaves + HALO))
    ones = jnp.concatenate([own.astype(f32), other.astype(f32)], axis=1)
    row = lax.broadcasted_iota(jnp.int32, shape, 0)
    lane = lax.broadcasted_iota(jnp.int32, shape, 1)
    square = (shape[0], shape[0])
    before = lax.broadcasted_iota(jnp.int32, square, 1) < lax.broadcasted_iota(jnp.int32, square, 0)
    rank = jnp.dot(
        before.astype(f32).astype(bf16), ones.astype(bf16), preferred_element_type=f32
    ).astype(jnp.int32)
    total = jnp.sum(ones, axis=0, keepdims=True).astype(jnp.int32)
    value = slot.astype(f32)
    square = (P_SIZE, P_SIZE)
    ahead = lax.broadcasted_iota(jnp.int32, square, 0) < lax.broadcasted_iota(jnp.int32, square, 1)
    ahead = ahead.astype(f32).astype(bf16)
    lane8 = lane[0:8]
    row8 = row[0:8]
    for part, out in enumerate(outs):
        mask = (own, other)[part]
        order = jnp.where(mask, rank[:, part * P_SIZE : (part + 1) * P_SIZE], -1)
        goes = jnp.where(order % 2 == 1, SLOTS + order // 2, order // 2)
        goes = jnp.where(mask, goes, -1)
        many = total[:, part * P_SIZE : (part + 1) * P_SIZE]
        at = jnp.where(row < SLOTS, 2 * row, 2 * (row - SLOTS) + 1)
        table = jnp.where(many <= at, 1.0 * NONE, 0.0)
        for j in range(width):
            table = table + jnp.where(row == goes[j : j + 1], value[j : j + 1], 0.0)
        groups = jnp.where(lane8 < leaves, jnp.maximum((many + 1) // 2, 1), 0)
        start = jnp.dot(
            groups.astype(f32).astype(bf16), ahead, preferred_element_type=f32
        ).astype(jnp.int32)
        stop = jnp.where(lane8 == leaves, FLAT, start + groups)
        extra = jnp.where(
            row8 == 0, start // 32, jnp.where(row8 == 1, start % 32, jnp.where(row8 == 2, lane8, 0))
        )
        look = jnp.concatenate([table, extra.astype(f32)], axis=0).astype(bf16)
        ends = jnp.concatenate(
            [jnp.where(row8 == 0, start, stop).astype(f32), jnp.zeros((P_SIZE - 8, P_SIZE), f32)],
            axis=0,
        ).T
        begin, end = ends[:, 0:1], ends[:, 1:2]
        spot = lax.broadcasted_iota(jnp.int32, square, 1).astype(f32)
        for t in range(FLAT // P_SIZE):
            here = spot + 1.0 * t * P_SIZE
            hot = ((begin <= here) & (here < end)).astype(f32).astype(bf16)
            found = jnp.dot(look, hot, preferred_element_type=f32)
            k = here[0:1] - (found[32:33] * 32.0 + found[33:34])
            pick = row[0:SLOTS].astype(f32) == k
            a = jnp.sum(jnp.where(pick, found[0:SLOTS], 0.0), axis=0, keepdims=True)
            b = jnp.sum(jnp.where(pick, found[SLOTS : 2 * SLOTS], 0.0), axis=0, keepdims=True)
            word = a + b * RADIX + found[34:35] * (RADIX * RADIX)
            out[t : t + 1, :] = word.astype(jnp.int32)
        count = start[0:1, leaves : leaves + 1]
        out[7:8, P_SIZE - 1 : P_SIZE] = count


def row_of(morton, b, offset):
    return morton.at[pl.ds(offset, morton.shape[0] - CH * P_SIZE + 1)][b * (CH * P_SIZE)]


def fetch(pairs, sems):
    copies = [pltpu.make_async_copy(a, b, sems.at[i]) for i, (a, b) in enumerate(pairs)]
    for copy in copies:
        copy.start()
    return copies


def arrange_kernel(
    morton, near_list, leaf_far, points, probes, skel, sub_skel, basis_hbm, leaf_hbm, box_hbm, sub_hbm,
    geo_lo, geo_hi, near_ids, near_ids_out, far_ids, far_ids_out, q1_out, packed,
    rows, got, got_too, wide, basis, leaf_tr, box_tr, sub_tr, sems,
):
    copies = fetch(
        ((basis_hbm, basis), (leaf_hbm, leaf_tr), (box_hbm, box_tr), (sub_hbm, sub_tr)), sems
    )
    half = geo_lo.shape[0]
    leaves = 2 * half
    middle = q1_out.shape[0] // 2
    device = lax.axis_index("group") * lax.axis_size("sub") + lax.axis_index("sub")
    sort_list(near_list, (near_ids, near_ids_out), wide, device * leaves)
    sort_list(leaf_far, (far_ids, far_ids_out), wide, device * leaves)

    def flip(g, c):
        for j in range(8):
            at = pl.ds(pl.multiple_of((8 * g + j) * P_SIZE, P_SIZE), P_SIZE)
            both = jnp.concatenate(
                [probes[:, at], points[:, at], jnp.zeros((5, P_SIZE), f32)], axis=0
            )
            rows[at, 0:40] = both.T
        return c

    lax.fori_loop(0, leaves // 8, flip, 0)
    for copy in copies:
        copy.wait()

    def gather(b, into):
        for j in range(CH):
            for k in range(P_SIZE):
                into[j, k : k + 1, :] = rows[pl.ds(row_of(morton, b, j * P_SIZE + k), 1), :]

    def combine(b, start, held, geo):
        turned = [held[j].T for j in range(CH)]
        parts = []
        for j in range(CH):
            i = b * CH + j
            at = i - start
            geo[at, 0:40, :] = turned[j][0:40]
            for c in range(3):
                geo[at, 35 + c : 36 + c, 0:64] = skel[c, pl.ds(i, 1), :]
            q0 = hdot_nt(turned[j][0:32], basis[i])
            geo[at, 40:56, 0:64] = q0[0:16]
            geo[at, 40:56, 64:128] = q0[16:32]
            parts.append(q0)
        q1 = jnp.zeros(q1_out.shape[1:], f32)
        for j in range(0, CH, 2):
            two = jnp.concatenate([leaf_tr[b * CH + j], leaf_tr[b * CH + j + 1]], axis=0)
            q1 = q1 + hdot(jnp.concatenate(parts[j : j + 2], axis=1), two)
        q1_out[b] = q1
        return hdot(q1, box_tr[b])

    def two_boxes(g, q2):
        gather(g, got)
        late = combine(middle + jnp.maximum(g - 1, 0), half, got_too, geo_hi)
        gather(middle + g, got_too)
        return q2 + jnp.where(g > 0, late, 0.0) + combine(g, 0, got, geo_lo)

    q2 = lax.fori_loop(0, middle, two_boxes, jnp.zeros((32, packed.shape[1]), f32))
    q2 = q2 + combine(2 * middle - 1, half, got_too, geo_hi)
    packed[0:32, :] = q2
    packed[32:64, :] = hdot(q2, sub_tr[0])
    packed[64:72, :] = jnp.zeros((8, packed.shape[1]), f32)
    for c in range(3):
        packed[64 + c : 65 + c, :] = sub_skel[c]


def prepare_source(block, at, centre_pt, centre_sk, src, xw, src_lo, src_hi, qw):
    geo8 = block[32:40]
    s8, t8 = augmented(coords(geo8, centre_pt))
    src[at] = source_rows(s8).T.astype(bf16)
    turned = jnp.concatenate([geo8[3:8], geo8[0:3]], axis=0)
    ks8, kt8 = augmented(coords(turned, centre_sk))
    low = lax.broadcasted_iota(jnp.int32, (8, P_SIZE), 1) < 64
    ks8 = jnp.where(low, ks8, 0.0)
    src_lo[at] = source_rows(ks8).astype(bf16)
    src_hi[at] = source_rows(pltpu.roll(ks8, 64, 1)).astype(bf16)
    x = block[0:32]
    hi = x.astype(bf16)
    lo = (x - hi.astype(f32)).astype(bf16)
    xw[at] = jnp.concatenate([hi, lo], axis=0)
    q = block[40:56]
    q = jnp.concatenate([q, pltpu.roll(q, 64, 1)], axis=0)
    qhi = q.astype(bf16).astype(f32)
    four = jnp.concatenate([qhi, q - qhi, jnp.zeros((64, P_SIZE), f32)], axis=0)
    qw[at] = four.T[0:64].astype(bf16)
    return t8, kt8


def prepare_target(t8, kt8, at, tgt, tgt_far):
    tgt[at] = target_rows(t8).astype(bf16)
    far = target_rows(kt8)
    tgt_far[at] = jnp.concatenate([far, far], axis=0).T[0:64].astype(bf16)


def clear(refs, at):
    for ref in refs:
        ref[at] = jnp.zeros(ref.shape[1:], ref.dtype)


def stream(ids, leaves, batch, out, first, part):
    def entry(i, j):
        word = ids.at[pl.ds(j, REACH)][i * batch]
        return word >> 14, word & (RADIX - 1), (word >> 7) & (RADIX - 1)

    def start():
        for j in range(batch):
            first(j, entry(0, j))
        return jnp.int32(0), jnp.zeros(out.shape[1:], f32)

    def steps(i, c):
        leaf, acc = c
        for j in range(batch):
            now = entry(i, j)
            more = part(j, now, entry(i, j + batch))
            acc = jnp.where(now[0] == leaf, acc, 0.0) + more
            leaf = now[0]
            out[leaf] = acc
            yield None
        yield leaf, acc

    trips = (ids[FLAT - 1] + batch - 1) // batch
    return start, steps, trips


def run(*streams):
    def one(i, c):
        work = [steps(i, held) for (_, steps, _), held in zip(streams, c)]
        done = [None] * len(work)
        while any(d is None for d in done):
            done = [next(w) if d is None else d for w, d in zip(work, done)]
        return tuple(done)

    trips = functools.reduce(jnp.maximum, [t for _, _, t in streams])
    lax.fori_loop(0, trips, one, tuple(start() for start, _, _ in streams))


def near_pass(ids, src, tgt, xw, out, dist):
    def first(j, at):
        leaf, a, b = at
        target = tgt[leaf]
        dist[2 * j] = jnp.dot(src[a], target, preferred_element_type=f32)
        dist[2 * j + 1] = jnp.dot(src[b], target, preferred_element_type=f32)

    def part(j, at, ahead):
        tiles = [jnp.concatenate(halves(profile(dist[2 * j + u])), axis=1) for u in range(2)]
        first(j, ahead)
        acc = jnp.dot(
            jnp.concatenate([xw[at[1]], xw[at[2]]], axis=1),
            jnp.concatenate(tiles, axis=0),
            preferred_element_type=f32,
        )
        return acc[0:32, 0:128] + acc[0:32, 128:256] + acc[32:64, 0:128]

    return stream(ids, tgt.shape[0] - 1, NEAR_BATCH, out, first, part)


def far_pass(ids, src_lo, src_hi, tgt, qw, out, dist):
    def first(j, at):
        leaf, a, b = at
        source = jnp.concatenate([src_lo[a], src_hi[b]], axis=0)
        dist[j] = jnp.dot(tgt[leaf], source, preferred_element_type=f32)

    def part(j, at, ahead):
        tile = jnp.concatenate(halves(profile(dist[j])), axis=1)
        first(j, ahead)
        a, b = qw[at[1]], qw[at[2]]
        return jnp.dot(
            tile, jnp.concatenate([a, b, a, b], axis=0), preferred_element_type=f32
        )

    return stream(ids, tgt.shape[0] - 1, FAR_BATCH, out, first, part)


def centred(block, centre):
    return augmented(coords(block, centre))


def distances(source8, target8):
    return jnp.dot(
        source_rows(source8).T.astype(bf16),
        target_rows(target8).astype(bf16),
        preferred_element_type=f32,
    )


def inner_kernel(
    near_ids, far_ids, geo_lo, geo_hi,
    near_out, far_out, tgt, tgt_far, origin,
    src, xw, src_lo, src_hi, qw, near_dist, far_dist,
):
    half = geo_lo.shape[0]
    leaves = 2 * half
    first = geo_lo[0, 32:40, 0:1]
    origin[...] = geo_lo[0, 32:40, :]
    centre_sk = jnp.concatenate([first[3:8], first[0:3]], axis=0)
    sources = (src, xw, src_lo, src_hi, qw)

    def load(g, c):
        for geo, start in ((geo_lo, 0), (geo_hi, half)):
            for j in range(4):
                i = g * 4 + j
                t8, kt8 = prepare_source(geo[i], i + start, first, centre_sk, *sources)
                prepare_target(t8, kt8, i + start, tgt, tgt_far)
        return c

    lax.fori_loop(0, half // 4, load, 0)
    clear(sources, NONE)
    clear((tgt, tgt_far), leaves)
    run(
        near_pass(near_ids, src, tgt, xw, near_out, near_dist),
        far_pass(far_ids, src_lo, src_hi, tgt_far, qw, far_out, far_dist),
    )


def outer_kernel(
    near_ids, far_ids, box_far, origin, left, right, tgt, tgt_far, q1, box_skel3,
    near_out, far_out, z1,
    src, xw, src_lo, src_hi, qw, near_dist, far_dist, box_skel,
):
    boxes, box_width = q1.shape[0], box_far.shape[0]
    device = lax.axis_index("group") * lax.axis_size("sub") + lax.axis_index("sub")
    box_skel[...] = jnp.zeros_like(box_skel)
    for b in range(boxes):
        for c in range(3):
            box_skel[b, c : c + 1, :] = box_skel3[c, b : b + 1, :]

    def box_level(b):
        mine = box_skel[b]
        centre = mine[:, 0:1]
        blocks, weights = [], []
        for j in range(box_width):
            entry = box_far[j, b]
            m = jnp.maximum(entry - device * boxes, 0)
            blocks.append(box_skel[m])
            weights.append(jnp.where(entry >= 0, q1[m], 0.0))
        source = centred(jnp.concatenate(blocks, axis=1), centre)[0]
        k = distances(source, centred(mine, centre)[1])
        z1[b] = weigh(jnp.concatenate(weights, axis=1), profile(k))

    def two_levels(g, c):
        box_level(2 * g)
        box_level(2 * g + 1)
        return c

    lax.fori_loop(0, boxes // 2, two_levels, 0)
    first = origin[:, 0:1]
    centre_sk = jnp.concatenate([first[3:8], first[0:3]], axis=0)
    sources = (src, xw, src_lo, src_hi, qw)

    def load(g, c):
        for block, start in ((left, 0), (right, HALO)):
            for j in range(4):
                i = g * 4 + j
                prepare_source(block[i], i + start, first, centre_sk, *sources)
        return c

    lax.fori_loop(0, HALO // 4, load, 0)
    clear(sources, NONE)
    run(
        near_pass(near_ids, src, tgt, xw, near_out, near_dist),
        far_pass(far_ids, src_lo, src_hi, tgt_far, qw, far_out, far_dist),
    )


def finish_kernel(
    morton, sub_far, near_own, far_own, near, far,
    z1, gathered, group_skel3, basis_hbm, leaf_hbm, box_hbm, sub_hbm,
    out,
    group_skel, rows, pad, tall, tall_too, l1s, basis, leaf_tr, box_tr, sub_tr, sems,
    *, groups, sub_width, near_factor, f0, f1, f2, f3,
):
    copies = fetch(
        ((basis_hbm, basis), (leaf_hbm, leaf_tr), (box_hbm, box_tr), (sub_hbm, sub_tr)), sems
    )
    boxes = z1.shape[0]
    leaves = near.shape[0] - 1
    group = lax.axis_index("group")
    subs = lax.axis_size("sub")
    device = group * subs + lax.axis_index("sub")
    group_skel[...] = jnp.zeros_like(group_skel)
    for b in range(groups):
        for c in range(3):
            group_skel[b, c : c + 1, :] = group_skel3[c, b : b + 1, :]

    own = gathered[device, 64:72, :]
    centre = own[:, 0:1]
    target = centred(own, centre)[1]

    def sub_term(j, acc):
        entry = sub_far[j]
        m = jnp.maximum(entry, 0)
        source = centred(gathered[m, 64:72, :], centre)[0]
        q2 = jnp.where(entry >= 0, gathered[m, 0:32, :], 0.0)
        return acc + weigh(q2, profile(distances(source, target)))

    many = 4 if sub_width % 4 == 0 else 1

    def sub_terms(g, acc):
        for j in range(many):
            acc = sub_term(g * many + j, acc)
        return acc

    none = jnp.zeros((32, gathered.shape[2]), f32)
    z2 = lax.fori_loop(0, sub_width // many, sub_terms, none)
    g_own = group_skel[group]
    g_centre = g_own[:, 0:1]
    g_target = centred(g_own, g_centre)[1]
    z3 = none
    for step in range(1, groups):
        h = lax.rem(group + step, groups)

        def eight(s, t):
            for k in range(8):
                t = t + gathered[h * subs + s * 8 + k, 32:64, :]
            return t

        q3 = lax.fori_loop(0, subs // 8, eight, none)
        source = centred(group_skel[h], g_centre)[0]
        z3 = z3 + weigh(q3, profile(distances(source, g_target)))
    for copy in copies:
        copy.wait()
    l2 = z2 * f2 + hdot_nt(z3 * f3, sub_tr[0])
    for b in range(boxes):
        l1s[b] = z1[b] * f1 + hdot_nt(l2, box_tr[b])

    def down(b, into):
        l1 = l1s[b]
        for j in range(CH):
            i = b * CH + j
            turned = (far_own[i] + far[i]).T
            l0 = (turned[0:32] + turned[32:64]) * f0 + hdot_nt(l1, leaf_tr[i])
            pad[j, 0:32, :] = (near_own[i] + near[i]) * near_factor + hdot(l0, basis[i])
        for j in range(CH):
            into[j] = pad[j].T

    def scatter(b, held):
        for j in range(CH):
            for k in range(P_SIZE):
                rows[pl.ds(row_of(morton, b, j * P_SIZE + k), 1), :] = held[j, k : k + 1, :]

    pad[...] = jnp.zeros_like(pad)
    tall_too[...] = jnp.zeros_like(tall_too)

    def two_boxes(g, c):
        scatter(jnp.maximum(2 * g - 1, 1), tall_too)
        down(2 * g, tall)
        scatter(2 * g, tall)
        down(2 * g + 1, tall_too)
        return c

    lax.fori_loop(0, boxes // 2, two_boxes, 0)
    scatter(boxes - 1, tall_too)

    def flip(g, c):
        for j in range(8):
            at = pl.ds(pl.multiple_of((8 * g + j) * P_SIZE, P_SIZE), P_SIZE)
            out[:, at] = rows[at, :].T[0:32]
        return c

    lax.fori_loop(0, leaves // 8, flip, 0)


VMEM = pl.BlockSpec(memory_space=pltpu.VMEM)
SMEM = pl.BlockSpec(memory_space=pltpu.SMEM)
ANY = pl.BlockSpec(memory_space=pl.ANY)
params = pltpu.CompilerParams(vmem_limit_bytes=56 * 2**20)


def body(
    points, probes, morton, near_list, leaf_far, box_far, subtree_far,
    leaf_skeleton, box_skeleton, subtree_skeleton, group_skeleton,
    leaf_basis, leaf_transfer, box_transfer, subtree_transfer,
):
    leaves = near_list.shape[0]
    count = points.shape[1]
    nv = probes.shape[0]
    boxes = box_far.shape[0]
    r0, r1 = leaf_basis.shape[1], box_transfer.shape[1]
    r2, r3 = subtree_transfer.shape[1:]
    subs, groups = lax.axis_size("sub"), lax.axis_size("group")
    i32 = jnp.int32
    front = lambda a: jnp.transpose(a, (1, 0, 2))
    bases = (leaf_basis, leaf_transfer, box_transfer, subtree_transfer)
    held = [pltpu.VMEM(a.shape, f32) for a in bases]
    sems = pltpu.SemaphoreType.DMA((len(bases),))

    geo_lo, geo_hi, near_ids, near_ids_out, far_ids, far_ids_out, q1, packed = pl.pallas_call(
        arrange_kernel,
        out_shape=(
            jax.ShapeDtypeStruct((leaves // 2, 56, P_SIZE), f32),
            jax.ShapeDtypeStruct((leaves // 2, 56, P_SIZE), f32),
            *[jax.ShapeDtypeStruct((FLAT // P_SIZE, P_SIZE), i32)] * 4,
            jax.ShapeDtypeStruct((boxes, nv, r1), f32),
            jax.ShapeDtypeStruct((72, r2), f32),
        ),
        in_specs=[SMEM] + [VMEM] * 6 + [ANY] * 4,
        out_specs=(VMEM,) * 8,
        scratch_shapes=[
            pltpu.VMEM((count, P_SIZE), f32),
            pltpu.VMEM((CH, P_SIZE, P_SIZE), f32),
            pltpu.VMEM((CH, P_SIZE, P_SIZE), f32),
            pltpu.VMEM((2 * SLOTS, P_SIZE), i32),
        ]
        + held
        + [sems],
        compiler_params=params,
        name="arrange",
    )(
        morton, near_list.T, leaf_far.T, points, probes, front(leaf_skeleton),
        front(subtree_skeleton), *bases,
    )

    both = ("group", "sub")
    ends = subs * groups - 1
    left = lax.ppermute(geo_hi, both, [(i, i + 1) for i in range(ends)])
    right = lax.ppermute(geo_lo, both, [(i + 1, i) for i in range(ends)])
    gathered = lax.all_gather(packed, both, axis=0)

    acc_shapes = ((leaves + 1, nv, P_SIZE), (leaves + 1, r0, P_SIZE))
    tables = [
        pltpu.VMEM((NONE + 1, P_SIZE, 64), bf16),
        pltpu.VMEM((NONE + 1, 2 * nv, P_SIZE), bf16),
        pltpu.VMEM((NONE + 1, 64, P_SIZE), bf16),
        pltpu.VMEM((NONE + 1, 64, P_SIZE), bf16),
        pltpu.VMEM((NONE + 1, 64, P_SIZE), bf16),
        pltpu.VMEM((2 * NEAR_BATCH, P_SIZE, P_SIZE), f32),
        pltpu.VMEM((FAR_BATCH, 64, P_SIZE), f32),
    ]
    near, far, tgt, tgt_far, origin = pl.pallas_call(
        inner_kernel,
        out_shape=tuple(jax.ShapeDtypeStruct(a, f32) for a in acc_shapes)
        + (
            jax.ShapeDtypeStruct((leaves + 1, 64, P_SIZE), bf16),
            jax.ShapeDtypeStruct((leaves + 1, 64, P_SIZE), bf16),
            jax.ShapeDtypeStruct((8, P_SIZE), f32),
        ),
        in_specs=[SMEM] * 2 + [VMEM] * 2,
        out_specs=(VMEM,) * 5,
        scratch_shapes=tables,
        compiler_params=params,
        cost_estimate=pl.CostEstimate(flops=2 * 10**10, bytes_accessed=10**7, transcendentals=5 * 10**7),
        name="inner",
    )(near_ids.reshape(-1), far_ids.reshape(-1), geo_lo, geo_hi)

    near_halo, far_halo, z1 = pl.pallas_call(
        outer_kernel,
        out_shape=tuple(
            jax.ShapeDtypeStruct(a, f32) for a in acc_shapes + ((boxes, nv, r1),)
        ),
        in_specs=[SMEM] * 3 + [VMEM] * 7,
        out_specs=(VMEM,) * 3,
        scratch_shapes=tables + [pltpu.VMEM((boxes, 8, r1), f32)],
        compiler_params=params,
        cost_estimate=pl.CostEstimate(flops=10**10, bytes_accessed=10**7, transcendentals=3 * 10**7),
        name="outer",
    )(
        near_ids_out.reshape(-1), far_ids_out.reshape(-1), box_far.T,
        origin, left, right, tgt, tgt_far, q1, front(box_skeleton),
    )

    return pl.pallas_call(
        functools.partial(
            finish_kernel,
            groups=groups,
            sub_width=subtree_far.shape[1],
            near_factor=(P_SIZE * near_list.shape[1]) ** -0.5,
            f0=(r0 * leaf_far.shape[1]) ** -0.5,
            f1=(r1 * box_far.shape[1]) ** -0.5,
            f2=(r2 * subtree_far.shape[1]) ** -0.5,
            f3=r3**-0.5,
        ),
        out_shape=jax.ShapeDtypeStruct((nv, count), f32),
        in_specs=[SMEM] * 2 + [VMEM] * 7 + [ANY] * 4,
        out_specs=VMEM,
        scratch_shapes=[
            pltpu.VMEM((groups, 8, r3), f32),
            pltpu.VMEM((count, P_SIZE), f32),
            pltpu.VMEM((CH, P_SIZE, P_SIZE), f32),
            pltpu.VMEM((CH, P_SIZE, P_SIZE), f32),
            pltpu.VMEM((CH, P_SIZE, P_SIZE), f32),
            pltpu.VMEM((boxes, nv, P_SIZE), f32),
        ]
        + held
        + [sems],
        compiler_params=params,
        name="finish",
    )(
        morton, subtree_far.reshape(-1), near, far, near_halo, far_halo,
        z1, gathered, front(group_skeleton), *bases,
    )


def solution(mesh):
    two = ("group", "sub")
    placed = (
        (P(None, two),) * 2
        + (P(two),)
        + (P(two, None),) * 4
        + (P(two, None, None),) * 3
        + (P(),)
        + (P(two, None, None),) * 4
    )
    return jax.shard_map(
        body, mesh=mesh, in_specs=placed, out_specs=P(None, two), check_vma=False
    )
```

```python
import functools
import math

import jax
import jax.numpy as jnp
from jax import lax
from jax.experimental import pallas as pl
from jax.experimental.pallas import tpu as pltpu
from jax.sharding import PartitionSpec as P

P_SIZE = 128
CH = 8
HALO = 32
SLOTS = 16
NONE = 2 * HALO
RADIX = 128
FLAT = 8 * P_SIZE
REACH = FLAT - 48
NEAR_BATCH = 16
FAR_BATCH = 14

scale = math.sqrt(3.0) / 12.0
soft = 0.0001 * scale * scale
log2e = math.log2(math.e)
f32 = jnp.float32
bf16 = jnp.bfloat16
NT = (((1,), (1,)), ((), ()))


def halves(k):
    hi = k.astype(bf16)
    return hi, (k - hi.astype(f32)).astype(bf16)


def hdot(a, b):
    ah, al = halves(a)
    bh, bl = halves(b)
    return jnp.dot(
        jnp.concatenate([ah, al, ah], axis=1),
        jnp.concatenate([bh, bh, bl], axis=0),
        preferred_element_type=f32,
    )


def hdot_nt(a, b):
    ah, al = halves(a)
    bh, bl = halves(b)
    return lax.dot_general(
        jnp.concatenate([ah, al, ah], axis=1),
        jnp.concatenate([bh, bh, bl], axis=1),
        NT,
        preferred_element_type=f32,
    )


def weigh(q, k):
    n = k.shape[1]
    both = jnp.dot(
        jnp.concatenate(halves(q), axis=0),
        jnp.concatenate(halves(k), axis=1),
        preferred_element_type=f32,
    )
    return both[0:32, 0:n] + both[0:32, n:] + both[32:64, 0:n]


def profile(squared):
    squared = jnp.maximum(squared, soft)
    u = squared * lax.rsqrt(squared)
    return (1.0 + u) * jnp.exp2(u * -log2e)


def split3(v):
    high = v.astype(bf16).astype(f32)
    rest = v - high
    mid = rest.astype(bf16).astype(f32)
    return high, mid, rest - mid


def augmented(x):
    row = lax.broadcasted_iota(jnp.int32, x.shape, 0)
    norm = jnp.sum(x * x, axis=0, keepdims=True)
    source = jnp.where(row < 3, -2.0 * x, jnp.where(row == 3, 1.0, jnp.where(row == 4, norm + soft, 0.0)))
    target = jnp.where(row < 3, x, jnp.where(row == 3, norm, jnp.where(row == 4, 1.0, 0.0)))
    return source, target


def source_rows(v):
    h, m, lo = split3(v)
    return jnp.concatenate([h, m, h, m, lo, h, lo, m], axis=0)


def target_rows(v):
    h, m, lo = split3(v)
    return jnp.concatenate([h, h, m, m, h, lo, m, lo], axis=0)


def coords(block, centre):
    row = lax.broadcasted_iota(jnp.int32, block.shape, 0)
    return jnp.where(row < 3, (block - centre) * scale, 0.0)


def sort_list(ids_ref, outs, wide, base):
    width, leaves = ids_ref.shape
    wide[...] = jnp.full(wide.shape, -1, jnp.int32)
    wide[0:width, 0:leaves] = ids_ref[...]
    ids = wide[...]
    shape = ids.shape
    place = ids - base
    valid = ids >= 0
    own = valid & (place >= 0) & (place < leaves)
    other = valid & jnp.logical_not(own)
    slot = jnp.where(own, place, jnp.where(place < 0, place + HALO, place - leaves + HALO))
    ones = jnp.concatenate([own.astype(f32), other.astype(f32)], axis=1)
    row = lax.broadcasted_iota(jnp.int32, shape, 0)
    lane = lax.broadcasted_iota(jnp.int32, shape, 1)
    square = (shape[0], shape[0])
    before = lax.broadcasted_iota(jnp.int32, square, 1) < lax.broadcasted_iota(jnp.int32, square, 0)
    rank = jnp.dot(
        before.astype(f32).astype(bf16), ones.astype(bf16), preferred_element_type=f32
    ).astype(jnp.int32)
    total = jnp.sum(ones, axis=0, keepdims=True).astype(jnp.int32)
    value = slot.astype(f32)
    square = (P_SIZE, P_SIZE)
    ahead = lax.broadcasted_iota(jnp.int32, square, 0) < lax.broadcasted_iota(jnp.int32, square, 1)
    ahead = ahead.astype(f32).astype(bf16)
    lane8 = lane[0:8]
    row8 = row[0:8]
    for part, out in enumerate(outs):
        mask = (own, other)[part]
        order = jnp.where(mask, rank[:, part * P_SIZE : (part + 1) * P_SIZE], -1)
        goes = jnp.where(order % 2 == 1, SLOTS + order // 2, order // 2)
        goes = jnp.where(mask, goes, -1)
        many = total[:, part * P_SIZE : (part + 1) * P_SIZE]
        at = jnp.where(row < SLOTS, 2 * row, 2 * (row - SLOTS) + 1)
        table = jnp.where(many <= at, 1.0 * NONE, 0.0)
        for j in range(width):
            table = table + jnp.where(row == goes[j : j + 1], value[j : j + 1], 0.0)
        groups = jnp.where(lane8 < leaves, jnp.maximum((many + 1) // 2, 1), 0)
        start = jnp.dot(
            groups.astype(f32).astype(bf16), ahead, preferred_element_type=f32
        ).astype(jnp.int32)
        stop = jnp.where(lane8 == leaves, FLAT, start + groups)
        extra = jnp.where(
            row8 == 0, start // 32, jnp.where(row8 == 1, start % 32, jnp.where(row8 == 2, lane8, 0))
        )
        look = jnp.concatenate([table, extra.astype(f32)], axis=0).astype(bf16)
        ends = jnp.concatenate(
            [jnp.where(row8 == 0, start, stop).astype(f32), jnp.zeros((P_SIZE - 8, P_SIZE), f32)],
            axis=0,
        ).T
        begin, end = ends[:, 0:1], ends[:, 1:2]
        spot = lax.broadcasted_iota(jnp.int32, square, 1).astype(f32)
        for t in range(FLAT // P_SIZE):
            here = spot + 1.0 * t * P_SIZE
            hot = ((begin <= here) & (here < end)).astype(f32).astype(bf16)
            found = jnp.dot(look, hot, preferred_element_type=f32)
            k = here[0:1] - (found[32:33] * 32.0 + found[33:34])
            pick = row[0:SLOTS].astype(f32) == k
            a = jnp.sum(jnp.where(pick, found[0:SLOTS], 0.0), axis=0, keepdims=True)
            b = jnp.sum(jnp.where(pick, found[SLOTS : 2 * SLOTS], 0.0), axis=0, keepdims=True)
            word = a + b * RADIX + found[34:35] * (RADIX * RADIX)
            out[t : t + 1, :] = word.astype(jnp.int32)
        count = start[0:1, leaves : leaves + 1]
        out[7:8, P_SIZE - 1 : P_SIZE] = count


def row_of(morton, b, offset):
    return morton.at[pl.ds(offset, morton.shape[0] - CH * P_SIZE + 1)][b * (CH * P_SIZE)]


def fetch(pairs, sems):
    copies = [pltpu.make_async_copy(a, b, sems.at[i]) for i, (a, b) in enumerate(pairs)]
    for copy in copies:
        copy.start()
    return copies


def arrange_kernel(
    morton, near_list, leaf_far, points, probes, skel, sub_skel, basis_hbm, leaf_hbm, box_hbm, sub_hbm,
    geo_lo, geo_hi, near_ids, near_ids_out, far_ids, far_ids_out, q1_out, packed,
    rows, got, got_too, wide, basis, leaf_tr, box_tr, sub_tr, sems,
):
    copies = fetch(
        ((basis_hbm, basis), (leaf_hbm, leaf_tr), (box_hbm, box_tr), (sub_hbm, sub_tr)), sems
    )
    half = geo_lo.shape[0]
    leaves = 2 * half
    middle = q1_out.shape[0] // 2
    device = lax.axis_index("group") * lax.axis_size("sub") + lax.axis_index("sub")
    sort_list(near_list, (near_ids, near_ids_out), wide, device * leaves)
    sort_list(leaf_far, (far_ids, far_ids_out), wide, device * leaves)

    def flip(g, c):
        for j in range(8):
            at = pl.ds(pl.multiple_of((8 * g + j) * P_SIZE, P_SIZE), P_SIZE)
            both = jnp.concatenate(
                [probes[:, at], points[:, at], jnp.zeros((5, P_SIZE), f32)], axis=0
            )
            rows[at, 0:40] = both.T
        return c

    lax.fori_loop(0, leaves // 8, flip, 0)
    for copy in copies:
        copy.wait()

    def gather(b, into):
        for j in range(CH):
            for k in range(P_SIZE):
                into[j, k : k + 1, :] = rows[pl.ds(row_of(morton, b, j * P_SIZE + k), 1), :]

    def combine(b, start, held, geo):
        turned = [held[j].T for j in range(CH)]
        parts = []
        for j in range(CH):
            i = b * CH + j
            at = i - start
            geo[at, 0:40, :] = turned[j][0:40]
            for c in range(3):
                geo[at, 35 + c : 36 + c, 0:64] = skel[c, pl.ds(i, 1), :]
            q0 = hdot_nt(turned[j][0:32], basis[i])
            geo[at, 40:56, 0:64] = q0[0:16]
            geo[at, 40:56, 64:128] = q0[16:32]
            parts.append(q0)
        q1 = jnp.zeros(q1_out.shape[1:], f32)
        for j in range(0, CH, 2):
            two = jnp.concatenate([leaf_tr[b * CH + j], leaf_tr[b * CH + j + 1]], axis=0)
            q1 = q1 + hdot(jnp.concatenate(parts[j : j + 2], axis=1), two)
        q1_out[b] = q1
        return hdot(q1, box_tr[b])

    def two_boxes(g, q2):
        gather(g, got)
        late = combine(middle + jnp.maximum(g - 1, 0), half, got_too, geo_hi)
        gather(middle + g, got_too)
        return q2 + jnp.where(g > 0, late, 0.0) + combine(g, 0, got, geo_lo)

    q2 = lax.fori_loop(0, middle, two_boxes, jnp.zeros((32, packed.shape[1]), f32))
    q2 = q2 + combine(2 * middle - 1, half, got_too, geo_hi)
    packed[0:32, :] = q2
    packed[32:64, :] = hdot(q2, sub_tr[0])
    packed[64:72, :] = jnp.zeros((8, packed.shape[1]), f32)
    for c in range(3):
        packed[64 + c : 65 + c, :] = sub_skel[c]


def prepare_source(block, at, centre_pt, centre_sk, src, xw, src_lo, src_hi, qw):
    geo8 = block[32:40]
    s8, t8 = augmented(coords(geo8, centre_pt))
    src[at] = source_rows(s8).T.astype(bf16)
    turned = jnp.concatenate([geo8[3:8], geo8[0:3]], axis=0)
    ks8, kt8 = augmented(coords(turned, centre_sk))
    low = lax.broadcasted_iota(jnp.int32, (8, P_SIZE), 1) < 64
    ks8 = jnp.where(low, ks8, 0.0)
    src_lo[at] = source_rows(ks8).astype(bf16)
    src_hi[at] = source_rows(pltpu.roll(ks8, 64, 1)).astype(bf16)
    x = block[0:32]
    hi = x.astype(bf16)
    lo = (x - hi.astype(f32)).astype(bf16)
    xw[at] = jnp.concatenate([hi, lo], axis=0)
    q = block[40:56]
    q = jnp.concatenate([q, pltpu.roll(q, 64, 1)], axis=0)
    qhi = q.astype(bf16).astype(f32)
    four = jnp.concatenate([qhi, q - qhi, jnp.zeros((64, P_SIZE), f32)], axis=0)
    qw[at] = four.T[0:64].astype(bf16)
    return t8, kt8


def prepare_target(t8, kt8, at, tgt, tgt_far):
    tgt[at] = target_rows(t8).astype(bf16)
    far = target_rows(kt8)
    tgt_far[at] = jnp.concatenate([far, far], axis=0).T[0:64].astype(bf16)


def clear(refs, at):
    for ref in refs:
        ref[at] = jnp.zeros(ref.shape[1:], ref.dtype)


def stream(ids, leaves, batch, out, first, part):
    def entry(i, j):
        word = ids.at[pl.ds(j, REACH)][i * batch]
        return word >> 14, word & (RADIX - 1), (word >> 7) & (RADIX - 1)

    def start():
        for j in range(batch):
            first(j, entry(0, j))
        return jnp.int32(0), jnp.zeros(out.shape[1:], f32)

    def steps(i, c):
        leaf, acc = c
        for j in range(batch):
            now = entry(i, j)
            more = part(j, now, entry(i, j + batch))
            acc = jnp.where(now[0] == leaf, acc, 0.0) + more
            leaf = now[0]
            out[leaf] = acc
            yield None
        yield leaf, acc

    trips = (ids[FLAT - 1] + batch - 1) // batch
    return start, steps, trips


def run(*streams):
    def one(i, c):
        work = [steps(i, held) for (_, steps, _), held in zip(streams, c)]
        done = [None] * len(work)
        while any(d is None for d in done):
            done = [next(w) if d is None else d for w, d in zip(work, done)]
        return tuple(done)

    trips = functools.reduce(jnp.maximum, [t for _, _, t in streams])
    lax.fori_loop(0, trips, one, tuple(start() for start, _, _ in streams))


def near_pass(ids, src, tgt, xw, out, dist):
    def first(j, at):
        leaf, a, b = at
        target = tgt[leaf]
        dist[2 * j] = jnp.dot(src[a], target, preferred_element_type=f32)
        dist[2 * j + 1] = jnp.dot(src[b], target, preferred_element_type=f32)

    def part(j, at, ahead):
        tiles = [jnp.concatenate(halves(profile(dist[2 * j + u])), axis=1) for u in range(2)]
        first(j, ahead)
        acc = jnp.dot(
            jnp.concatenate([xw[at[1]], xw[at[2]]], axis=1),
            jnp.concatenate(tiles, axis=0),
            preferred_element_type=f32,
        )
        return acc[0:32, 0:128] + acc[0:32, 128:256] + acc[32:64, 0:128]

    return stream(ids, tgt.shape[0] - 1, NEAR_BATCH, out, first, part)


def far_pass(ids, src_lo, src_hi, tgt, qw, out, dist):
    def first(j, at):
        leaf, a, b = at
        source = jnp.concatenate([src_lo[a], src_hi[b]], axis=0)
        dist[j] = jnp.dot(tgt[leaf], source, preferred_element_type=f32)

    def part(j, at, ahead):
        tile = jnp.concatenate(halves(profile(dist[j])), axis=1)
        first(j, ahead)
        a, b = qw[at[1]], qw[at[2]]
        return jnp.dot(
            tile, jnp.concatenate([a, b, a, b], axis=0), preferred_element_type=f32
        )

    return stream(ids, tgt.shape[0] - 1, FAR_BATCH, out, first, part)


def centred(block, centre):
    return augmented(coords(block, centre))


def distances(source8, target8):
    return jnp.dot(
        source_rows(source8).T.astype(bf16),
        target_rows(target8).astype(bf16),
        preferred_element_type=f32,
    )


def inner_kernel(
    near_ids, far_ids, geo_lo, geo_hi,
    near_out, far_out, tgt, tgt_far, origin,
    src, xw, src_lo, src_hi, qw, near_dist, far_dist,
):
    half = geo_lo.shape[0]
    leaves = 2 * half
    first = geo_lo[0, 32:40, 0:1]
    origin[...] = geo_lo[0, 32:40, :]
    centre_sk = jnp.concatenate([first[3:8], first[0:3]], axis=0)
    sources = (src, xw, src_lo, src_hi, qw)

    def load(g, c):
        for geo, start in ((geo_lo, 0), (geo_hi, half)):
            for j in range(4):
                i = g * 4 + j
                t8, kt8 = prepare_source(geo[i], i + start, first, centre_sk, *sources)
                prepare_target(t8, kt8, i + start, tgt, tgt_far)
        return c

    lax.fori_loop(0, half // 4, load, 0)
    clear(sources, NONE)
    clear((tgt, tgt_far), leaves)
    run(
        near_pass(near_ids, src, tgt, xw, near_out, near_dist),
        far_pass(far_ids, src_lo, src_hi, tgt_far, qw, far_out, far_dist),
    )


def outer_kernel(
    near_ids, far_ids, box_far, origin, left, right, tgt, tgt_far, q1, box_skel3,
    near_out, far_out, z1,
    src, xw, src_lo, src_hi, qw, near_dist, far_dist, box_skel,
):
    boxes, box_width = q1.shape[0], box_far.shape[0]
    device = lax.axis_index("group") * lax.axis_size("sub") + lax.axis_index("sub")
    box_skel[...] = jnp.zeros_like(box_skel)
    for b in range(boxes):
        for c in range(3):
            box_skel[b, c : c + 1, :] = box_skel3[c, b : b + 1, :]

    def box_level(b):
        mine = box_skel[b]
        centre = mine[:, 0:1]
        blocks, weights = [], []
        for j in range(box_width):
            entry = box_far[j, b]
            m = jnp.maximum(entry - device * boxes, 0)
            blocks.append(box_skel[m])
            weights.append(jnp.where(entry >= 0, q1[m], 0.0))
        source = centred(jnp.concatenate(blocks, axis=1), centre)[0]
        k = distances(source, centred(mine, centre)[1])
        z1[b] = weigh(jnp.concatenate(weights, axis=1), profile(k))

    def two_levels(g, c):
        box_level(2 * g)
        box_level(2 * g + 1)
        return c

    lax.fori_loop(0, boxes // 2, two_levels, 0)
    first = origin[:, 0:1]
    centre_sk = jnp.concatenate([first[3:8], first[0:3]], axis=0)
    sources = (src, xw, src_lo, src_hi, qw)

    def load(g, c):
        for block, start in ((left, 0), (right, HALO)):
            for j in range(4):
                i = g * 4 + j
                prepare_source(block[i], i + start, first, centre_sk, *sources)
        return c

    lax.fori_loop(0, HALO // 4, load, 0)
    clear(sources, NONE)
    run(
        near_pass(near_ids, src, tgt, xw, near_out, near_dist),
        far_pass(far_ids, src_lo, src_hi, tgt_far, qw, far_out, far_dist),
    )


def finish_kernel(
    morton, sub_far, near_own, far_own, near, far,
    z1, gathered, group_skel3, basis_hbm, leaf_hbm, box_hbm, sub_hbm,
    out,
    group_skel, rows, pad, tall, tall_too, l1s, basis, leaf_tr, box_tr, sub_tr, sems,
    *, groups, sub_width, near_factor, f0, f1, f2, f3,
):
    copies = fetch(
        ((basis_hbm, basis), (leaf_hbm, leaf_tr), (box_hbm, box_tr), (sub_hbm, sub_tr)), sems
    )
    boxes = z1.shape[0]
    leaves = near.shape[0] - 1
    group = lax.axis_index("group")
    subs = lax.axis_size("sub")
    device = group * subs + lax.axis_index("sub")
    group_skel[...] = jnp.zeros_like(group_skel)
    for b in range(groups):
        for c in range(3):
            group_skel[b, c : c + 1, :] = group_skel3[c, b : b + 1, :]

    own = gathered[device, 64:72, :]
    centre = own[:, 0:1]
    target = centred(own, centre)[1]

    def sub_term(j, acc):
        entry = sub_far[j]
        m = jnp.maximum(entry, 0)
        source = centred(gathered[m, 64:72, :], centre)[0]
        q2 = jnp.where(entry >= 0, gathered[m, 0:32, :], 0.0)
        return acc + weigh(q2, profile(distances(source, target)))

    many = 4 if sub_width % 4 == 0 else 1

    def sub_terms(g, acc):
        for j in range(many):
            acc = sub_term(g * many + j, acc)
        return acc

    none = jnp.zeros((32, gathered.shape[2]), f32)
    z2 = lax.fori_loop(0, sub_width // many, sub_terms, none)
    g_own = group_skel[group]
    g_centre = g_own[:, 0:1]
    g_target = centred(g_own, g_centre)[1]
    z3 = none
    for step in range(1, groups):
        h = lax.rem(group + step, groups)

        def eight(s, t):
            for k in range(8):
                t = t + gathered[h * subs + s * 8 + k, 32:64, :]
            return t

        q3 = lax.fori_loop(0, subs // 8, eight, none)
        source = centred(group_skel[h], g_centre)[0]
        z3 = z3 + weigh(q3, profile(distances(source, g_target)))
    for copy in copies:
        copy.wait()
    l2 = z2 * f2 + hdot_nt(z3 * f3, sub_tr[0])
    for b in range(boxes):
        l1s[b] = z1[b] * f1 + hdot_nt(l2, box_tr[b])

    def down(b, into):
        l1 = l1s[b]
        for j in range(CH):
            i = b * CH + j
            turned = (far_own[i] + far[i]).T
            l0 = (turned[0:32] + turned[32:64]) * f0 + hdot_nt(l1, leaf_tr[i])
            pad[j, 0:32, :] = (near_own[i] + near[i]) * near_factor + hdot(l0, basis[i])
        for j in range(CH):
            into[j] = pad[j].T

    def scatter(b, held):
        for j in range(CH):
            for k in range(P_SIZE):
                rows[pl.ds(row_of(morton, b, j * P_SIZE + k), 1), :] = held[j, k : k + 1, :]

    pad[...] = jnp.zeros_like(pad)
    tall_too[...] = jnp.zeros_like(tall_too)

    def two_boxes(g, c):
        scatter(jnp.maximum(2 * g - 1, 1), tall_too)
        down(2 * g, tall)
        scatter(2 * g, tall)
        down(2 * g + 1, tall_too)
        return c

    lax.fori_loop(0, boxes // 2, two_boxes, 0)
    scatter(boxes - 1, tall_too)

    def flip(g, c):
        for j in range(8):
            at = pl.ds(pl.multiple_of((8 * g + j) * P_SIZE, P_SIZE), P_SIZE)
            out[:, at] = rows[at, :].T[0:32]
        return c

    lax.fori_loop(0, leaves // 8, flip, 0)


VMEM = pl.BlockSpec(memory_space=pltpu.VMEM)
SMEM = pl.BlockSpec(memory_space=pltpu.SMEM)
ANY = pl.BlockSpec(memory_space=pl.ANY)
params = pltpu.CompilerParams(vmem_limit_bytes=36 * 2**20)


def body(
    points, probes, morton, near_list, leaf_far, box_far, subtree_far,
    leaf_skeleton, box_skeleton, subtree_skeleton, group_skeleton,
    leaf_basis, leaf_transfer, box_transfer, subtree_transfer,
):
    leaves = near_list.shape[0]
    count = points.shape[1]
    nv = probes.shape[0]
    boxes = box_far.shape[0]
    r0, r1 = leaf_basis.shape[1], box_transfer.shape[1]
    r2, r3 = subtree_transfer.shape[1:]
    subs, groups = lax.axis_size("sub"), lax.axis_size("group")
    i32 = jnp.int32
    front = lambda a: jnp.transpose(a, (1, 0, 2))
    bases = (leaf_basis, leaf_transfer, box_transfer, subtree_transfer)
    held = [pltpu.VMEM(a.shape, f32) for a in bases]
    sems = pltpu.SemaphoreType.DMA((len(bases),))

    geo_lo, geo_hi, near_ids, near_ids_out, far_ids, far_ids_out, q1, packed = pl.pallas_call(
        arrange_kernel,
        out_shape=(
            jax.ShapeDtypeStruct((leaves // 2, 56, P_SIZE), f32),
            jax.ShapeDtypeStruct((leaves // 2, 56, P_SIZE), f32),
            *[jax.ShapeDtypeStruct((FLAT // P_SIZE, P_SIZE), i32)] * 4,
            jax.ShapeDtypeStruct((boxes, nv, r1), f32),
            jax.ShapeDtypeStruct((72, r2), f32),
        ),
        in_specs=[SMEM] + [VMEM] * 6 + [ANY] * 4,
        out_specs=(VMEM,) * 8,
        scratch_shapes=[
            pltpu.VMEM((count, P_SIZE), f32),
            pltpu.VMEM((CH, P_SIZE, P_SIZE), f32),
            pltpu.VMEM((CH, P_SIZE, P_SIZE), f32),
            pltpu.VMEM((2 * SLOTS, P_SIZE), i32),
        ]
        + held
        + [sems],
        compiler_params=params,
        name="arrange",
    )(
        morton, near_list.T, leaf_far.T, points, probes, front(leaf_skeleton),
        front(subtree_skeleton), *bases,
    )

    both = ("group", "sub")
    ends = subs * groups - 1
    left = lax.ppermute(geo_hi, both, [(i, i + 1) for i in range(ends)])
    right = lax.ppermute(geo_lo, both, [(i + 1, i) for i in range(ends)])
    gathered = lax.all_gather(packed, both, axis=0)

    acc_shapes = ((leaves + 1, nv, P_SIZE), (leaves + 1, r0, P_SIZE))
    tables = [
        pltpu.VMEM((NONE + 1, P_SIZE, 64), bf16),
        pltpu.VMEM((NONE + 1, 2 * nv, P_SIZE), bf16),
        pltpu.VMEM((NONE + 1, 64, P_SIZE), bf16),
        pltpu.VMEM((NONE + 1, 64, P_SIZE), bf16),
        pltpu.VMEM((NONE + 1, 64, P_SIZE), bf16),
        pltpu.VMEM((2 * NEAR_BATCH, P_SIZE, P_SIZE), f32),
        pltpu.VMEM((FAR_BATCH, 64, P_SIZE), f32),
    ]
    near, far, tgt, tgt_far, origin = pl.pallas_call(
        inner_kernel,
        out_shape=tuple(jax.ShapeDtypeStruct(a, f32) for a in acc_shapes)
        + (
            jax.ShapeDtypeStruct((leaves + 1, 64, P_SIZE), bf16),
            jax.ShapeDtypeStruct((leaves + 1, 64, P_SIZE), bf16),
            jax.ShapeDtypeStruct((8, P_SIZE), f32),
        ),
        in_specs=[SMEM] * 2 + [VMEM] * 2,
        out_specs=(VMEM,) * 5,
        scratch_shapes=tables,
        compiler_params=params,
        cost_estimate=pl.CostEstimate(flops=2 * 10**10, bytes_accessed=10**7, transcendentals=5 * 10**7),
        name="inner",
    )(near_ids.reshape(-1), far_ids.reshape(-1), geo_lo, geo_hi)

    near_halo, far_halo, z1 = pl.pallas_call(
        outer_kernel,
        out_shape=tuple(
            jax.ShapeDtypeStruct(a, f32) for a in acc_shapes + ((boxes, nv, r1),)
        ),
        in_specs=[SMEM] * 3 + [VMEM] * 7,
        out_specs=(VMEM,) * 3,
        scratch_shapes=tables + [pltpu.VMEM((boxes, 8, r1), f32)],
        compiler_params=params,
        cost_estimate=pl.CostEstimate(flops=10**10, bytes_accessed=10**7, transcendentals=3 * 10**7),
        name="outer",
    )(
        near_ids_out.reshape(-1), far_ids_out.reshape(-1), box_far.T,
        origin, left, right, tgt, tgt_far, q1, front(box_skeleton),
    )

    return pl.pallas_call(
        functools.partial(
            finish_kernel,
            groups=groups,
            sub_width=subtree_far.shape[1],
            near_factor=(P_SIZE * near_list.shape[1]) ** -0.5,
            f0=(r0 * leaf_far.shape[1]) ** -0.5,
            f1=(r1 * box_far.shape[1]) ** -0.5,
            f2=(r2 * subtree_far.shape[1]) ** -0.5,
            f3=r3**-0.5,
        ),
        out_shape=jax.ShapeDtypeStruct((nv, count), f32),
        in_specs=[SMEM] * 2 + [VMEM] * 7 + [ANY] * 4,
        out_specs=VMEM,
        scratch_shapes=[
            pltpu.VMEM((groups, 8, r3), f32),
            pltpu.VMEM((count, P_SIZE), f32),
            pltpu.VMEM((CH, P_SIZE, P_SIZE), f32),
            pltpu.VMEM((CH, P_SIZE, P_SIZE), f32),
            pltpu.VMEM((CH, P_SIZE, P_SIZE), f32),
            pltpu.VMEM((boxes, nv, P_SIZE), f32),
        ]
        + held
        + [sems],
        compiler_params=params,
        name="finish",
    )(
        morton, subtree_far.reshape(-1), near, far, near_halo, far_halo,
        z1, gathered, front(group_skeleton), *bases,
    )


def solution(mesh):
    two = ("group", "sub")
    placed = (
        (P(None, two),) * 2
        + (P(two),)
        + (P(two, None),) * 4
        + (P(two, None, None),) * 3
        + (P(),)
        + (P(two, None, None),) * 4
    )
    return jax.shard_map(
        body, mesh=mesh, in_specs=placed, out_specs=P(None, two), check_vma=False
    )
```

```python
import functools
import math

import jax
import jax.numpy as jnp
from jax import lax
from jax.experimental import pallas as pl
from jax.experimental.pallas import tpu as pltpu
from jax.sharding import PartitionSpec as P

P_SIZE = 128
CH = 8
HALO = 32
SLOTS = 16
NONE = 2 * HALO
RADIX = 128
FLAT = 8 * P_SIZE
REACH = FLAT - 48
NEAR_BATCH = 16
FAR_BATCH = 14

scale = math.sqrt(3.0) / 12.0
soft = 0.0001 * scale * scale
log2e = math.log2(math.e)
f32 = jnp.float32
bf16 = jnp.bfloat16
NT = (((1,), (1,)), ((), ()))


def halves(k):
    hi = k.astype(bf16)
    return hi, (k - hi.astype(f32)).astype(bf16)


def hdot(a, b):
    ah, al = halves(a)
    bh, bl = halves(b)
    return jnp.dot(
        jnp.concatenate([ah, al, ah], axis=1),
        jnp.concatenate([bh, bh, bl], axis=0),
        preferred_element_type=f32,
    )


def hdot_nt(a, b):
    ah, al = halves(a)
    bh, bl = halves(b)
    return lax.dot_general(
        jnp.concatenate([ah, al, ah], axis=1),
        jnp.concatenate([bh, bh, bl], axis=1),
        NT,
        preferred_element_type=f32,
    )


def weigh(q, k):
    n = k.shape[1]
    both = jnp.dot(
        jnp.concatenate(halves(q), axis=0),
        jnp.concatenate(halves(k), axis=1),
        preferred_element_type=f32,
    )
    return both[0:32, 0:n] + both[0:32, n:] + both[32:64, 0:n]


def profile(squared):
    squared = jnp.maximum(squared, soft)
    u = squared * lax.rsqrt(squared)
    return (1.0 + u) * jnp.exp2(u * -log2e)


def split3(v):
    high = v.astype(bf16).astype(f32)
    rest = v - high
    mid = rest.astype(bf16).astype(f32)
    return high, mid, rest - mid


def augmented(x):
    row = lax.broadcasted_iota(jnp.int32, x.shape, 0)
    norm = jnp.sum(x * x, axis=0, keepdims=True)
    source = jnp.where(row < 3, -2.0 * x, jnp.where(row == 3, 1.0, jnp.where(row == 4, norm + soft, 0.0)))
    target = jnp.where(row < 3, x, jnp.where(row == 3, norm, jnp.where(row == 4, 1.0, 0.0)))
    return source, target


def source_rows(v):
    h, m, lo = split3(v)
    return jnp.concatenate([h, m, h, m, lo, h, lo, m], axis=0)


def target_rows(v):
    h, m, lo = split3(v)
    return jnp.concatenate([h, h, m, m, h, lo, m, lo], axis=0)


def coords(block, centre):
    row = lax.broadcasted_iota(jnp.int32, block.shape, 0)
    return jnp.where(row < 3, (block - centre) * scale, 0.0)


def sort_list(ids_ref, outs, wide, base):
    width, leaves = ids_ref.shape
    wide[...] = jnp.full(wide.shape, -1, jnp.int32)
    wide[0:width, 0:leaves] = ids_ref[...]
    ids = wide[...]
    shape = ids.shape
    place = ids - base
    valid = ids >= 0
    own = valid & (place >= 0) & (place < leaves)
    other = valid & jnp.logical_not(own)
    slot = jnp.where(own, place, jnp.where(place < 0, place + HALO, place - leaves + HALO))
    ones = jnp.concatenate([own.astype(f32), other.astype(f32)], axis=1)
    row = lax.broadcasted_iota(jnp.int32, shape, 0)
    lane = lax.broadcasted_iota(jnp.int32, shape, 1)
    square = (shape[0], shape[0])
    before = lax.broadcasted_iota(jnp.int32, square, 1) < lax.broadcasted_iota(jnp.int32, square, 0)
    rank = jnp.dot(
        before.astype(f32).astype(bf16), ones.astype(bf16), preferred_element_type=f32
    ).astype(jnp.int32)
    total = jnp.sum(ones, axis=0, keepdims=True).astype(jnp.int32)
    value = slot.astype(f32)
    square = (P_SIZE, P_SIZE)
    ahead = lax.broadcasted_iota(jnp.int32, square, 0) < lax.broadcasted_iota(jnp.int32, square, 1)
    ahead = ahead.astype(f32).astype(bf16)
    lane8 = lane[0:8]
    row8 = row[0:8]
    for part, out in enumerate(outs):
        mask = (own, other)[part]
        order = jnp.where(mask, rank[:, part * P_SIZE : (part + 1) * P_SIZE], -1)
        goes = jnp.where(order % 2 == 1, SLOTS + order // 2, order // 2)
        goes = jnp.where(mask, goes, -1)
        many = total[:, part * P_SIZE : (part + 1) * P_SIZE]
        at = jnp.where(row < SLOTS, 2 * row, 2 * (row - SLOTS) + 1)
        table = jnp.where(many <= at, 1.0 * NONE, 0.0)
        for j in range(width):
            table = table + jnp.where(row == goes[j : j + 1], value[j : j + 1], 0.0)
        groups = jnp.where(lane8 < leaves, jnp.maximum((many + 1) // 2, 1), 0)
        start = jnp.dot(
            groups.astype(f32).astype(bf16), ahead, preferred_element_type=f32
        ).astype(jnp.int32)
        stop = jnp.where(lane8 == leaves, FLAT, start + groups)
        extra = jnp.where(
            row8 == 0, start // 32, jnp.where(row8 == 1, start % 32, jnp.where(row8 == 2, lane8, 0))
        )
        look = jnp.concatenate([table, extra.astype(f32)], axis=0).astype(bf16)
        ends = jnp.concatenate(
            [jnp.where(row8 == 0, start, stop).astype(f32), jnp.zeros((P_SIZE - 8, P_SIZE), f32)],
            axis=0,
        ).T
        begin, end = ends[:, 0:1], ends[:, 1:2]
        spot = lax.broadcasted_iota(jnp.int32, square, 1).astype(f32)
        for t in range(FLAT // P_SIZE):
            here = spot + 1.0 * t * P_SIZE
            hot = ((begin <= here) & (here < end)).astype(f32).astype(bf16)
            found = jnp.dot(look, hot, preferred_element_type=f32)
            k = here[0:1] - (found[32:33] * 32.0 + found[33:34])
            pick = row[0:SLOTS].astype(f32) == k
            a = jnp.sum(jnp.where(pick, found[0:SLOTS], 0.0), axis=0, keepdims=True)
            b = jnp.sum(jnp.where(pick, found[SLOTS : 2 * SLOTS], 0.0), axis=0, keepdims=True)
            word = a + b * RADIX + found[34:35] * (RADIX * RADIX)
            out[t : t + 1, :] = word.astype(jnp.int32)
        count = start[0:1, leaves : leaves + 1]
        out[7:8, P_SIZE - 1 : P_SIZE] = count


def row_of(morton, b, offset):
    return morton.at[pl.ds(offset, morton.shape[0] - CH * P_SIZE + 1)][b * (CH * P_SIZE)]


def fetch(pairs, sems):
    copies = [pltpu.make_async_copy(a, b, sems.at[i]) for i, (a, b) in enumerate(pairs)]
    for copy in copies:
        copy.start()
    return copies


def arrange_kernel(
    morton, near_list, leaf_far, points, probes, skel, sub_skel, basis_hbm, leaf_hbm, box_hbm, sub_hbm,
    geo_lo, geo_hi, near_ids, near_ids_out, far_ids, far_ids_out, q1_out, packed,
    rows, got, got_too, wide, basis, leaf_tr, box_tr, sub_tr, sems,
):
    copies = fetch(
        ((basis_hbm, basis), (leaf_hbm, leaf_tr), (box_hbm, box_tr), (sub_hbm, sub_tr)), sems
    )
    half = geo_lo.shape[0]
    leaves = 2 * half
    middle = q1_out.shape[0] // 2
    device = lax.axis_index("group") * lax.axis_size("sub") + lax.axis_index("sub")
    sort_list(near_list, (near_ids, near_ids_out), wide, device * leaves)
    sort_list(leaf_far, (far_ids, far_ids_out), wide, device * leaves)

    def flip(g, c):
        for j in range(8):
            at = pl.ds(pl.multiple_of((8 * g + j) * P_SIZE, P_SIZE), P_SIZE)
            both = jnp.concatenate(
                [probes[:, at], points[:, at], jnp.zeros((5, P_SIZE), f32)], axis=0
            )
            rows[at, 0:40] = both.T
        return c

    lax.fori_loop(0, leaves // 8, flip, 0)
    for copy in copies:
        copy.wait()

    def work(b, start, held, geo, new, into):
        parts = []
        for j in range(CH):
            i = b * CH + j
            at = i - start
            turned = held[j].T
            for k in range(P_SIZE if into is not None else 0):
                into[j, k : k + 1, :] = rows[pl.ds(row_of(morton, new, j * P_SIZE + k), 1), :]
            geo[at, 0:40, :] = turned[0:40]
            for c in range(3):
                geo[at, 35 + c : 36 + c, 0:64] = skel[c, pl.ds(i, 1), :]
            q0 = hdot_nt(turned[0:32], basis[i])
            geo[at, 40:56, 0:64] = q0[0:16]
            geo[at, 40:56, 64:128] = q0[16:32]
            parts.append(q0)
        q1 = jnp.zeros(q1_out.shape[1:], f32)
        for j in range(0, CH, 2):
            two = jnp.concatenate([leaf_tr[b * CH + j], leaf_tr[b * CH + j + 1]], axis=0)
            q1 = q1 + hdot(jnp.concatenate(parts[j : j + 2], axis=1), two)
        q1_out[b] = q1
        return hdot(q1, box_tr[b])

    def two_boxes(g, q2):
        late = work(middle + jnp.maximum(g - 1, 0), half, got_too, geo_hi, g, got)
        return q2 + jnp.where(g > 0, late, 0.0) + work(g, 0, got, geo_lo, middle + g, got_too)

    q2 = lax.fori_loop(0, middle, two_boxes, jnp.zeros((32, packed.shape[1]), f32))
    q2 = q2 + work(2 * middle - 1, half, got_too, geo_hi, None, None)
    packed[0:32, :] = q2
    packed[32:64, :] = hdot(q2, sub_tr[0])
    packed[64:72, :] = jnp.zeros((8, packed.shape[1]), f32)
    for c in range(3):
        packed[64 + c : 65 + c, :] = sub_skel[c]


def prepare_source(block, at, centre_pt, centre_sk, src, xw, src_lo, src_hi, qw):
    geo8 = block[32:40]
    s8, t8 = augmented(coords(geo8, centre_pt))
    src[at] = source_rows(s8).T.astype(bf16)
    turned = jnp.concatenate([geo8[3:8], geo8[0:3]], axis=0)
    ks8, kt8 = augmented(coords(turned, centre_sk))
    low = lax.broadcasted_iota(jnp.int32, (8, P_SIZE), 1) < 64
    ks8 = jnp.where(low, ks8, 0.0)
    src_lo[at] = source_rows(ks8).astype(bf16)
    src_hi[at] = source_rows(pltpu.roll(ks8, 64, 1)).astype(bf16)
    x = block[0:32]
    hi = x.astype(bf16)
    lo = (x - hi.astype(f32)).astype(bf16)
    xw[at] = jnp.concatenate([hi, lo], axis=0)
    q = block[40:56]
    q = jnp.concatenate([q, pltpu.roll(q, 64, 1)], axis=0)
    qhi = q.astype(bf16).astype(f32)
    four = jnp.concatenate([qhi, q - qhi, jnp.zeros((64, P_SIZE), f32)], axis=0)
    qw[at] = four.T[0:64].astype(bf16)
    return t8, kt8


def prepare_target(t8, kt8, at, tgt, tgt_far):
    tgt[at] = target_rows(t8).astype(bf16)
    far = target_rows(kt8)
    tgt_far[at] = jnp.concatenate([far, far], axis=0).T[0:64].astype(bf16)


def clear(refs, at):
    for ref in refs:
        ref[at] = jnp.zeros(ref.shape[1:], ref.dtype)


def stream(ids, leaves, batch, out, first, part):
    def entry(i, j):
        word = ids.at[pl.ds(j, REACH)][i * batch]
        return word >> 14, word & (RADIX - 1), (word >> 7) & (RADIX - 1)

    def start():
        for j in range(batch):
            first(j, entry(0, j))
        return jnp.int32(0), jnp.zeros(out.shape[1:], f32)

    def steps(i, c):
        leaf, acc = c
        for j in range(batch):
            now = entry(i, j)
            more = part(j, now, entry(i, j + batch))
            acc = jnp.where(now[0] == leaf, acc, 0.0) + more
            leaf = now[0]
            out[leaf] = acc
            yield None
        yield leaf, acc

    trips = (ids[FLAT - 1] + batch - 1) // batch
    return start, steps, trips


def run(*streams):
    def one(i, c):
        work = [steps(i, held) for (_, steps, _), held in zip(streams, c)]
        done = [None] * len(work)
        while any(d is None for d in done):
            done = [next(w) if d is None else d for w, d in zip(work, done)]
        return tuple(done)

    trips = functools.reduce(jnp.maximum, [t for _, _, t in streams])
    lax.fori_loop(0, trips, one, tuple(start() for start, _, _ in streams))


def near_pass(ids, src, tgt, xw, out, dist):
    def first(j, at):
        leaf, a, b = at
        target = tgt[leaf]
        dist[2 * j] = jnp.dot(src[a], target, preferred_element_type=f32)
        dist[2 * j + 1] = jnp.dot(src[b], target, preferred_element_type=f32)

    def part(j, at, ahead):
        tiles = [jnp.concatenate(halves(profile(dist[2 * j + u])), axis=1) for u in range(2)]
        first(j, ahead)
        acc = jnp.dot(
            jnp.concatenate([xw[at[1]], xw[at[2]]], axis=1),
            jnp.concatenate(tiles, axis=0),
            preferred_element_type=f32,
        )
        return acc[0:32, 0:128] + acc[0:32, 128:256] + acc[32:64, 0:128]

    return stream(ids, tgt.shape[0] - 1, NEAR_BATCH, out, first, part)


def far_pass(ids, src_lo, src_hi, tgt, qw, out, dist):
    def first(j, at):
        leaf, a, b = at
        source = jnp.concatenate([src_lo[a], src_hi[b]], axis=0)
        dist[j] = jnp.dot(tgt[leaf], source, preferred_element_type=f32)

    def part(j, at, ahead):
        tile = jnp.concatenate(halves(profile(dist[j])), axis=1)
        first(j, ahead)
        a, b = qw[at[1]], qw[at[2]]
        return jnp.dot(
            tile, jnp.concatenate([a, b, a, b], axis=0), preferred_element_type=f32
        )

    return stream(ids, tgt.shape[0] - 1, FAR_BATCH, out, first, part)


def centred(block, centre):
    return augmented(coords(block, centre))


def distances(source8, target8):
    return jnp.dot(
        source_rows(source8).T.astype(bf16),
        target_rows(target8).astype(bf16),
        preferred_element_type=f32,
    )


def inner_kernel(
    near_ids, far_ids, geo_lo, geo_hi,
    near_out, far_out, tgt, tgt_far, origin,
    src, xw, src_lo, src_hi, qw, near_dist, far_dist,
):
    half = geo_lo.shape[0]
    leaves = 2 * half
    first = geo_lo[0, 32:40, 0:1]
    origin[...] = geo_lo[0, 32:40, :]
    centre_sk = jnp.concatenate([first[3:8], first[0:3]], axis=0)
    sources = (src, xw, src_lo, src_hi, qw)

    def load(g, c):
        for geo, start in ((geo_lo, 0), (geo_hi, half)):
            for j in range(8):
                i = g * 8 + j
                t8, kt8 = prepare_source(geo[i], i + start, first, centre_sk, *sources)
                prepare_target(t8, kt8, i + start, tgt, tgt_far)
        return c

    lax.fori_loop(0, half // 8, load, 0)
    clear(sources, NONE)
    clear((tgt, tgt_far), leaves)
    run(
        near_pass(near_ids, src, tgt, xw, near_out, near_dist),
        far_pass(far_ids, src_lo, src_hi, tgt_far, qw, far_out, far_dist),
    )


def outer_kernel(
    near_ids, far_ids, box_far, origin, left, right, tgt, tgt_far, q1, box_skel3,
    near_out, far_out, z1,
    src, xw, src_lo, src_hi, qw, near_dist, far_dist, box_skel,
):
    boxes, box_width = q1.shape[0], box_far.shape[0]
    device = lax.axis_index("group") * lax.axis_size("sub") + lax.axis_index("sub")
    box_skel[...] = jnp.zeros_like(box_skel)
    for b in range(boxes):
        for c in range(3):
            box_skel[b, c : c + 1, :] = box_skel3[c, b : b + 1, :]

    def box_level(b):
        mine = box_skel[b]
        centre = mine[:, 0:1]
        blocks, weights = [], []
        for j in range(box_width):
            entry = box_far[j, b]
            m = jnp.maximum(entry - device * boxes, 0)
            blocks.append(box_skel[m])
            weights.append(jnp.where(entry >= 0, q1[m], 0.0))
        source = centred(jnp.concatenate(blocks, axis=1), centre)[0]
        k = distances(source, centred(mine, centre)[1])
        z1[b] = weigh(jnp.concatenate(weights, axis=1), profile(k))

    def two_levels(g, c):
        box_level(2 * g)
        box_level(2 * g + 1)
        return c

    lax.fori_loop(0, boxes // 2, two_levels, 0)
    first = origin[:, 0:1]
    centre_sk = jnp.concatenate([first[3:8], first[0:3]], axis=0)
    sources = (src, xw, src_lo, src_hi, qw)

    def load(g, c):
        for block, start in ((left, 0), (right, HALO)):
            for j in range(8):
                i = g * 8 + j
                prepare_source(block[i], i + start, first, centre_sk, *sources)
        return c

    lax.fori_loop(0, HALO // 8, load, 0)
    clear(sources, NONE)
    run(
        near_pass(near_ids, src, tgt, xw, near_out, near_dist),
        far_pass(far_ids, src_lo, src_hi, tgt_far, qw, far_out, far_dist),
    )


def finish_kernel(
    morton, sub_far, z1, gathered, group_skel3, *rest,
    groups, sub_width, near_factor, f0, f1, f2, f3,
):
    fetched = rest[:8]
    out, group_skel, rows, pad, tall, tall_too, l1s = rest[8:15]
    held, sems = rest[15:23], rest[23]
    near_own, far_own, near, far, basis, leaf_tr, box_tr, sub_tr = held
    copies = fetch(tuple(zip(fetched, held))[::-1], sems)
    boxes = z1.shape[0]
    leaves = near.shape[0] - 1
    group = lax.axis_index("group")
    subs = lax.axis_size("sub")
    device = group * subs + lax.axis_index("sub")
    group_skel[...] = jnp.zeros_like(group_skel)
    for b in range(groups):
        for c in range(3):
            group_skel[b, c : c + 1, :] = group_skel3[c, b : b + 1, :]

    own = gathered[device, 64:72, :]
    centre = own[:, 0:1]
    target = centred(own, centre)[1]

    def sub_term(j, acc):
        entry = sub_far[j]
        m = jnp.maximum(entry, 0)
        source = centred(gathered[m, 64:72, :], centre)[0]
        q2 = jnp.where(entry >= 0, gathered[m, 0:32, :], 0.0)
        return acc + weigh(q2, profile(distances(source, target)))

    many = 4 if sub_width % 4 == 0 else 1

    def sub_terms(g, acc):
        for j in range(many):
            acc = sub_term(g * many + j, acc)
        return acc

    none = jnp.zeros((32, gathered.shape[2]), f32)
    z2 = lax.fori_loop(0, sub_width // many, sub_terms, none)
    g_own = group_skel[group]
    g_centre = g_own[:, 0:1]
    g_target = centred(g_own, g_centre)[1]
    z3 = none
    for step in range(1, groups):
        h = lax.rem(group + step, groups)

        def eight(s, t):
            for k in range(8):
                t = t + gathered[h * subs + s * 8 + k, 32:64, :]
            return t

        q3 = lax.fori_loop(0, subs // 8, eight, none)
        source = centred(group_skel[h], g_centre)[0]
        z3 = z3 + weigh(q3, profile(distances(source, g_target)))
    for copy in copies:
        copy.wait()
    l2 = z2 * f2 + hdot_nt(z3 * f3, sub_tr[0])
    for b in range(boxes):
        l1s[b] = z1[b] * f1 + hdot_nt(l2, box_tr[b])

    def work(b, into, old, held):
        l1 = l1s[b]
        for j in range(CH):
            for k in range(P_SIZE):
                rows[pl.ds(row_of(morton, old, j * P_SIZE + k), 1), :] = held[j, k : k + 1, :]
            i = b * CH + j
            turned = (far_own[i] + far[i]).T
            l0 = (turned[0:32] + turned[32:64]) * f0 + hdot_nt(l1, leaf_tr[i])
            pad[j, 0:32, :] = (near_own[i] + near[i]) * near_factor + hdot(l0, basis[i])
            into[j] = pad[j].T

    def scatter(b, held):
        for j in range(CH):
            for k in range(P_SIZE):
                rows[pl.ds(row_of(morton, b, j * P_SIZE + k), 1), :] = held[j, k : k + 1, :]

    pad[...] = jnp.zeros_like(pad)
    tall_too[...] = jnp.zeros_like(tall_too)

    def two_boxes(g, c):
        work(2 * g, tall, jnp.maximum(2 * g - 1, 1), tall_too)
        work(2 * g + 1, tall_too, 2 * g, tall)
        return c

    lax.fori_loop(0, boxes // 2, two_boxes, 0)
    scatter(boxes - 1, tall_too)

    def flip(g, c):
        for j in range(8):
            at = pl.ds(pl.multiple_of((8 * g + j) * P_SIZE, P_SIZE), P_SIZE)
            out[:, at] = rows[at, :].T[0:32]
        return c

    lax.fori_loop(0, leaves // 8, flip, 0)


VMEM = pl.BlockSpec(memory_space=pltpu.VMEM)
SMEM = pl.BlockSpec(memory_space=pltpu.SMEM)
ANY = pl.BlockSpec(memory_space=pl.ANY)
params = pltpu.CompilerParams(vmem_limit_bytes=56 * 2**20)


def body(
    points, probes, morton, near_list, leaf_far, box_far, subtree_far,
    leaf_skeleton, box_skeleton, subtree_skeleton, group_skeleton,
    leaf_basis, leaf_transfer, box_transfer, subtree_transfer,
):
    leaves = near_list.shape[0]
    count = points.shape[1]
    nv = probes.shape[0]
    boxes = box_far.shape[0]
    r0, r1 = leaf_basis.shape[1], box_transfer.shape[1]
    r2, r3 = subtree_transfer.shape[1:]
    subs, groups = lax.axis_size("sub"), lax.axis_size("group")
    i32 = jnp.int32
    front = lambda a: jnp.transpose(a, (1, 0, 2))
    bases = (leaf_basis, leaf_transfer, box_transfer, subtree_transfer)
    held = [pltpu.VMEM(a.shape, f32) for a in bases]
    sems = pltpu.SemaphoreType.DMA((len(bases),))

    geo_lo, geo_hi, near_ids, near_ids_out, far_ids, far_ids_out, q1, packed = pl.pallas_call(
        arrange_kernel,
        out_shape=(
            jax.ShapeDtypeStruct((leaves // 2, 56, P_SIZE), f32),
            jax.ShapeDtypeStruct((leaves // 2, 56, P_SIZE), f32),
            *[jax.ShapeDtypeStruct((FLAT // P_SIZE, P_SIZE), i32)] * 4,
            jax.ShapeDtypeStruct((boxes, nv, r1), f32),
            jax.ShapeDtypeStruct((72, r2), f32),
        ),
        in_specs=[SMEM] + [VMEM] * 6 + [ANY] * 4,
        out_specs=(VMEM,) * 8,
        scratch_shapes=[
            pltpu.VMEM((count, P_SIZE), f32),
            pltpu.VMEM((CH, P_SIZE, P_SIZE), f32),
            pltpu.VMEM((CH, P_SIZE, P_SIZE), f32),
            pltpu.VMEM((2 * SLOTS, P_SIZE), i32),
        ]
        + held
        + [sems],
        compiler_params=params,
        name="arrange",
    )(
        morton, near_list.T, leaf_far.T, points, probes, front(leaf_skeleton),
        front(subtree_skeleton), *bases,
    )

    both = ("group", "sub")
    ends = subs * groups - 1
    left = lax.ppermute(geo_hi, both, [(i, i + 1) for i in range(ends)])
    right = lax.ppermute(geo_lo, both, [(i + 1, i) for i in range(ends)])
    gathered = lax.all_gather(packed, both, axis=0)

    acc_shapes = ((leaves + 1, nv, P_SIZE), (leaves + 1, r0, P_SIZE))
    tables = [
        pltpu.VMEM((NONE + 1, P_SIZE, 64), bf16),
        pltpu.VMEM((NONE + 1, 2 * nv, P_SIZE), bf16),
        pltpu.VMEM((NONE + 1, 64, P_SIZE), bf16),
        pltpu.VMEM((NONE + 1, 64, P_SIZE), bf16),
        pltpu.VMEM((NONE + 1, 64, P_SIZE), bf16),
        pltpu.VMEM((2 * NEAR_BATCH, P_SIZE, P_SIZE), f32),
        pltpu.VMEM((FAR_BATCH, 64, P_SIZE), f32),
    ]
    near, far, tgt, tgt_far, origin = pl.pallas_call(
        inner_kernel,
        out_shape=tuple(jax.ShapeDtypeStruct(a, f32) for a in acc_shapes)
        + (
            jax.ShapeDtypeStruct((leaves + 1, 64, P_SIZE), bf16),
            jax.ShapeDtypeStruct((leaves + 1, 64, P_SIZE), bf16),
            jax.ShapeDtypeStruct((8, P_SIZE), f32),
        ),
        in_specs=[SMEM] * 2 + [VMEM] * 2,
        out_specs=(VMEM,) * 5,
        scratch_shapes=tables,
        compiler_params=params,
        cost_estimate=pl.CostEstimate(flops=2 * 10**10, bytes_accessed=10**7, transcendentals=5 * 10**7),
        name="inner",
    )(near_ids.reshape(-1), far_ids.reshape(-1), geo_lo, geo_hi)

    near_halo, far_halo, z1 = pl.pallas_call(
        outer_kernel,
        out_shape=tuple(
            jax.ShapeDtypeStruct(a, f32) for a in acc_shapes + ((boxes, nv, r1),)
        ),
        in_specs=[SMEM] * 3 + [VMEM] * 7,
        out_specs=(VMEM,) * 3,
        scratch_shapes=tables + [pltpu.VMEM((boxes, 8, r1), f32)],
        compiler_params=params,
        cost_estimate=pl.CostEstimate(flops=10**10, bytes_accessed=10**7, transcendentals=3 * 10**7),
        name="outer",
    )(
        near_ids_out.reshape(-1), far_ids_out.reshape(-1), box_far.T,
        origin, left, right, tgt, tgt_far, q1, front(box_skeleton),
    )

    return pl.pallas_call(
        functools.partial(
            finish_kernel,
            groups=groups,
            sub_width=subtree_far.shape[1],
            near_factor=(P_SIZE * near_list.shape[1]) ** -0.5,
            f0=(r0 * leaf_far.shape[1]) ** -0.5,
            f1=(r1 * box_far.shape[1]) ** -0.5,
            f2=(r2 * subtree_far.shape[1]) ** -0.5,
            f3=r3**-0.5,
        ),
        out_shape=jax.ShapeDtypeStruct((nv, count), f32),
        in_specs=[SMEM] * 2 + [VMEM] * 3 + [ANY] * 8,
        out_specs=VMEM,
        scratch_shapes=[
            pltpu.VMEM((groups, 8, r3), f32),
            pltpu.VMEM((count, P_SIZE), f32),
            pltpu.VMEM((CH, P_SIZE, P_SIZE), f32),
            pltpu.VMEM((CH, P_SIZE, P_SIZE), f32),
            pltpu.VMEM((CH, P_SIZE, P_SIZE), f32),
            pltpu.VMEM((boxes, nv, P_SIZE), f32),
        ]
        + [pltpu.VMEM(a, f32) for a in acc_shapes * 2]
        + held
        + [pltpu.SemaphoreType.DMA((8,))],
        compiler_params=params,
        name="finish",
    )(
        morton, subtree_far.reshape(-1), z1, gathered, front(group_skeleton),
        near, far, near_halo, far_halo, *bases,
    )


def solution(mesh):
    two = ("group", "sub")
    placed = (
        (P(None, two),) * 2
        + (P(two),)
        + (P(two, None),) * 4
        + (P(two, None, None),) * 3
        + (P(),)
        + (P(two, None, None),) * 4
    )
    return jax.shard_map(
        body, mesh=mesh, in_specs=placed, out_specs=P(None, two), check_vma=False
    )
```

```python
import functools
import math

import jax
import jax.numpy as jnp
from jax import lax
from jax.experimental import pallas as pl
from jax.experimental.pallas import tpu as pltpu
from jax.sharding import PartitionSpec as P

P_SIZE = 128
CH = 8
HALO = 32
SLOTS = 16
NONE = 2 * HALO
RADIX = 128
FLAT = 8 * P_SIZE
REACH = FLAT - 48
NEAR_BATCH = 16
FAR_BATCH = 14

scale = math.sqrt(3.0) / 12.0
soft = 0.0001 * scale * scale
log2e = math.log2(math.e)
f32 = jnp.float32
bf16 = jnp.bfloat16
NT = (((1,), (1,)), ((), ()))


def halves(k):
    hi = k.astype(bf16)
    return hi, (k - hi.astype(f32)).astype(bf16)


def hdot(a, b):
    ah, al = halves(a)
    bh, bl = halves(b)
    return jnp.dot(
        jnp.concatenate([ah, al, ah], axis=1),
        jnp.concatenate([bh, bh, bl], axis=0),
        preferred_element_type=f32,
    )


def hdot_nt(a, b):
    ah, al = halves(a)
    bh, bl = halves(b)
    return lax.dot_general(
        jnp.concatenate([ah, al, ah], axis=1),
        jnp.concatenate([bh, bh, bl], axis=1),
        NT,
        preferred_element_type=f32,
    )


def weigh(q, k):
    n = k.shape[1]
    both = jnp.dot(
        jnp.concatenate(halves(q), axis=0),
        jnp.concatenate(halves(k), axis=1),
        preferred_element_type=f32,
    )
    return both[0:32, 0:n] + both[0:32, n:] + both[32:64, 0:n]


def profile(squared):
    squared = jnp.maximum(squared, soft)
    u = squared * lax.rsqrt(squared)
    return (1.0 + u) * jnp.exp2(u * -log2e)


def split3(v):
    high = v.astype(bf16).astype(f32)
    rest = v - high
    mid = rest.astype(bf16).astype(f32)
    return high, mid, rest - mid


def augmented(x):
    row = lax.broadcasted_iota(jnp.int32, x.shape, 0)
    norm = jnp.sum(x * x, axis=0, keepdims=True)
    source = jnp.where(row < 3, -2.0 * x, jnp.where(row == 3, 1.0, jnp.where(row == 4, norm + soft, 0.0)))
    target = jnp.where(row < 3, x, jnp.where(row == 3, norm, jnp.where(row == 4, 1.0, 0.0)))
    return source, target


def source_rows(v):
    h, m, lo = split3(v)
    return jnp.concatenate([h, m, h, m, lo, h, lo, m], axis=0)


def target_rows(v):
    h, m, lo = split3(v)
    return jnp.concatenate([h, h, m, m, h, lo, m, lo], axis=0)


def coords(block, centre):
    row = lax.broadcasted_iota(jnp.int32, block.shape, 0)
    return jnp.where(row < 3, (block - centre) * scale, 0.0)


def sort_list(ids_ref, outs, wide, base):
    width, leaves = ids_ref.shape
    wide[...] = jnp.full(wide.shape, -1, jnp.int32)
    wide[0:width, 0:leaves] = ids_ref[...]
    ids = wide[...]
    shape = ids.shape
    place = ids - base
    valid = ids >= 0
    own = valid & (place >= 0) & (place < leaves)
    other = valid & jnp.logical_not(own)
    slot = jnp.where(own, place, jnp.where(place < 0, place + HALO, place - leaves + HALO))
    ones = jnp.concatenate([own.astype(f32), other.astype(f32)], axis=1)
    row = lax.broadcasted_iota(jnp.int32, shape, 0)
    lane = lax.broadcasted_iota(jnp.int32, shape, 1)
    square = (shape[0], shape[0])
    before = lax.broadcasted_iota(jnp.int32, square, 1) < lax.broadcasted_iota(jnp.int32, square, 0)
    rank = jnp.dot(
        before.astype(f32).astype(bf16), ones.astype(bf16), preferred_element_type=f32
    ).astype(jnp.int32)
    total = jnp.sum(ones, axis=0, keepdims=True).astype(jnp.int32)
    value = slot.astype(f32)
    square = (P_SIZE, P_SIZE)
    ahead = lax.broadcasted_iota(jnp.int32, square, 0) < lax.broadcasted_iota(jnp.int32, square, 1)
    ahead = ahead.astype(f32).astype(bf16)
    lane8 = lane[0:8]
    row8 = row[0:8]
    for part, out in enumerate(outs):
        mask = (own, other)[part]
        order = jnp.where(mask, rank[:, part * P_SIZE : (part + 1) * P_SIZE], -1)
        goes = jnp.where(order % 2 == 1, SLOTS + order // 2, order // 2)
        goes = jnp.where(mask, goes, -1)
        many = total[:, part * P_SIZE : (part + 1) * P_SIZE]
        at = jnp.where(row < SLOTS, 2 * row, 2 * (row - SLOTS) + 1)
        table = jnp.where(many <= at, 1.0 * NONE, 0.0)
        for j in range(width):
            table = table + jnp.where(row == goes[j : j + 1], value[j : j + 1], 0.0)
        groups = jnp.where(lane8 < leaves, jnp.maximum((many + 1) // 2, 1), 0)
        start = jnp.dot(
            groups.astype(f32).astype(bf16), ahead, preferred_element_type=f32
        ).astype(jnp.int32)
        stop = jnp.where(lane8 == leaves, FLAT, start + groups)
        extra = jnp.where(
            row8 == 0, start // 32, jnp.where(row8 == 1, start % 32, jnp.where(row8 == 2, lane8, 0))
        )
        look = jnp.concatenate([table, extra.astype(f32)], axis=0).astype(bf16)
        ends = jnp.concatenate(
            [jnp.where(row8 == 0, start, stop).astype(f32), jnp.zeros((P_SIZE - 8, P_SIZE), f32)],
            axis=0,
        ).T
        begin, end = ends[:, 0:1], ends[:, 1:2]
        spot = lax.broadcasted_iota(jnp.int32, square, 1).astype(f32)
        for t in range(FLAT // P_SIZE):
            here = spot + 1.0 * t * P_SIZE
            hot = ((begin <= here) & (here < end)).astype(f32).astype(bf16)
            found = jnp.dot(look, hot, preferred_element_type=f32)
            k = here[0:1] - (found[32:33] * 32.0 + found[33:34])
            pick = row[0:SLOTS].astype(f32) == k
            a = jnp.sum(jnp.where(pick, found[0:SLOTS], 0.0), axis=0, keepdims=True)
            b = jnp.sum(jnp.where(pick, found[SLOTS : 2 * SLOTS], 0.0), axis=0, keepdims=True)
            word = a + b * RADIX + found[34:35] * (RADIX * RADIX)
            out[t : t + 1, :] = word.astype(jnp.int32)
        count = start[0:1, leaves : leaves + 1]
        out[7:8, P_SIZE - 1 : P_SIZE] = count


def row_of(morton, b, offset):
    return morton.at[pl.ds(offset, morton.shape[0] - CH * P_SIZE + 1)][b * (CH * P_SIZE)]


def fetch(pairs, sems):
    copies = [pltpu.make_async_copy(a, b, sems.at[i]) for i, (a, b) in enumerate(pairs)]
    for copy in copies:
        copy.start()
    return copies


def arrange_kernel(
    morton, near_list, leaf_far, points, probes, skel, sub_skel, basis_hbm, leaf_hbm, box_hbm, sub_hbm,
    geo_lo, geo_hi, near_ids, near_ids_out, far_ids, far_ids_out, q1_out, packed,
    rows, got, got_too, wide, basis, leaf_tr, box_tr, sub_tr, sems,
):
    copies = fetch(
        ((basis_hbm, basis), (leaf_hbm, leaf_tr), (box_hbm, box_tr), (sub_hbm, sub_tr)), sems
    )
    half = geo_lo.shape[0]
    leaves = 2 * half
    middle = q1_out.shape[0] // 2
    device = lax.axis_index("group") * lax.axis_size("sub") + lax.axis_index("sub")
    sort_list(near_list, (near_ids, near_ids_out), wide, device * leaves)
    sort_list(leaf_far, (far_ids, far_ids_out), wide, device * leaves)

    def flip(g, c):
        for j in range(8):
            at = pl.ds(pl.multiple_of((8 * g + j) * P_SIZE, P_SIZE), P_SIZE)
            both = jnp.concatenate(
                [probes[:, at], points[:, at], jnp.zeros((5, P_SIZE), f32)], axis=0
            )
            rows[at, 0:40] = both.T
        return c

    lax.fori_loop(0, leaves // 8, flip, 0)
    for copy in copies:
        copy.wait()

    def work(b, start, held, geo, new, into):
        parts = []
        for j in range(CH):
            i = b * CH + j
            at = i - start
            turned = held[j].T
            for k in range(P_SIZE if into is not None else 0):
                into[j, k : k + 1, :] = rows[pl.ds(row_of(morton, new, j * P_SIZE + k), 1), :]
            geo[at, 0:40, :] = turned[0:40]
            for c in range(3):
                geo[at, 35 + c : 36 + c, 0:64] = skel[c, pl.ds(i, 1), :]
            q0 = hdot_nt(turned[0:32], basis[i])
            geo[at, 40:56, 0:64] = q0[0:16]
            geo[at, 40:56, 64:128] = q0[16:32]
            parts.append(q0)
        q1 = jnp.zeros(q1_out.shape[1:], f32)
        for j in range(0, CH, 2):
            two = jnp.concatenate([leaf_tr[b * CH + j], leaf_tr[b * CH + j + 1]], axis=0)
            q1 = q1 + hdot(jnp.concatenate(parts[j : j + 2], axis=1), two)
        q1_out[b] = q1
        return hdot(q1, box_tr[b])

    def two_boxes(g, q2):
        late = work(middle + jnp.maximum(g - 1, 0), half, got_too, geo_hi, g, got)
        return q2 + jnp.where(g > 0, late, 0.0) + work(g, 0, got, geo_lo, middle + g, got_too)

    q2 = lax.fori_loop(0, middle, two_boxes, jnp.zeros((32, packed.shape[1]), f32))
    q2 = q2 + work(2 * middle - 1, half, got_too, geo_hi, None, None)
    packed[0:32, :] = q2
    packed[32:64, :] = hdot(q2, sub_tr[0])
    packed[64:72, :] = jnp.zeros((8, packed.shape[1]), f32)
    for c in range(3):
        packed[64 + c : 65 + c, :] = sub_skel[c]


def prepare_source(block, at, centre_pt, centre_sk, src, xw, src_lo, src_hi, qw):
    geo8 = block[32:40]
    s8, t8 = augmented(coords(geo8, centre_pt))
    src[at] = source_rows(s8).T.astype(bf16)
    turned = jnp.concatenate([geo8[3:8], geo8[0:3]], axis=0)
    ks8, kt8 = augmented(coords(turned, centre_sk))
    low = lax.broadcasted_iota(jnp.int32, (8, P_SIZE), 1) < 64
    ks8 = jnp.where(low, ks8, 0.0)
    src_lo[at] = source_rows(ks8).astype(bf16)
    src_hi[at] = source_rows(pltpu.roll(ks8, 64, 1)).astype(bf16)
    x = block[0:32]
    hi = x.astype(bf16)
    lo = (x - hi.astype(f32)).astype(bf16)
    xw[at] = jnp.concatenate([hi, lo], axis=0)
    q = block[40:56]
    q = jnp.concatenate([q, pltpu.roll(q, 64, 1)], axis=0)
    qhi = q.astype(bf16).astype(f32)
    four = jnp.concatenate([qhi, q - qhi, jnp.zeros((64, P_SIZE), f32)], axis=0)
    qw[at] = four.T[0:64].astype(bf16)
    return t8, kt8


def prepare_target(t8, kt8, at, tgt, tgt_far):
    tgt[at] = target_rows(t8).astype(bf16)
    far = target_rows(kt8)
    tgt_far[at] = jnp.concatenate([far, far], axis=0).T[0:64].astype(bf16)


def clear(refs, at):
    for ref in refs:
        ref[at] = jnp.zeros(ref.shape[1:], ref.dtype)


def stream(ids, leaves, batch, out, first, part):
    def entry(i, j):
        word = ids.at[pl.ds(j, REACH)][i * batch]
        return word >> 14, word & (RADIX - 1), (word >> 7) & (RADIX - 1)

    def start():
        for j in range(batch):
            first(j, entry(0, j))
        return jnp.int32(0), jnp.zeros(out.shape[1:], f32)

    def steps(i, c):
        leaf, acc = c
        for j in range(batch):
            now = entry(i, j)
            more = part(j, now, entry(i, j + batch))
            acc = jnp.where(now[0] == leaf, acc, 0.0) + more
            leaf = now[0]
            out[leaf] = acc
            yield None
        yield leaf, acc

    trips = (ids[FLAT - 1] + batch - 1) // batch
    return start, steps, trips


def run(*streams):
    def one(i, c):
        work = [steps(i, held) for (_, steps, _), held in zip(streams, c)]
        done = [None] * len(work)
        while any(d is None for d in done):
            done = [next(w) if d is None else d for w, d in zip(work, done)]
        return tuple(done)

    trips = functools.reduce(jnp.maximum, [t for _, _, t in streams])
    lax.fori_loop(0, trips, one, tuple(start() for start, _, _ in streams))


def near_pass(ids, src, tgt, xw, out, dist):
    def first(j, at):
        leaf, a, b = at
        target = tgt[leaf]
        dist[2 * j] = jnp.dot(src[a], target, preferred_element_type=f32)
        dist[2 * j + 1] = jnp.dot(src[b], target, preferred_element_type=f32)

    def part(j, at, ahead):
        tiles = [jnp.concatenate(halves(profile(dist[2 * j + u])), axis=1) for u in range(2)]
        first(j, ahead)
        acc = jnp.dot(
            jnp.concatenate([xw[at[1]], xw[at[2]]], axis=1),
            jnp.concatenate(tiles, axis=0),
            preferred_element_type=f32,
        )
        return acc[0:32, 0:128] + acc[0:32, 128:256] + acc[32:64, 0:128]

    return stream(ids, tgt.shape[0] - 1, NEAR_BATCH, out, first, part)


def far_pass(ids, src_lo, src_hi, tgt, qw, out, dist):
    def first(j, at):
        leaf, a, b = at
        source = jnp.concatenate([src_lo[a], src_hi[b]], axis=0)
        dist[j] = jnp.dot(tgt[leaf], source, preferred_element_type=f32)

    def part(j, at, ahead):
        tile = jnp.concatenate(halves(profile(dist[j])), axis=1)
        first(j, ahead)
        a, b = qw[at[1]], qw[at[2]]
        return jnp.dot(
            tile, jnp.concatenate([a, b, a, b], axis=0), preferred_element_type=f32
        )

    return stream(ids, tgt.shape[0] - 1, FAR_BATCH, out, first, part)


def centred(block, centre):
    return augmented(coords(block, centre))


def distances(source8, target8):
    return jnp.dot(
        source_rows(source8).T.astype(bf16),
        target_rows(target8).astype(bf16),
        preferred_element_type=f32,
    )


def inner_kernel(
    near_ids, far_ids, geo_lo, geo_hi,
    near_out, far_out, tgt, tgt_far, origin,
    src, xw, src_lo, src_hi, qw, near_dist, far_dist,
):
    half = geo_lo.shape[0]
    leaves = 2 * half
    first = geo_lo[0, 32:40, 0:1]
    origin[...] = geo_lo[0, 32:40, :]
    centre_sk = jnp.concatenate([first[3:8], first[0:3]], axis=0)
    sources = (src, xw, src_lo, src_hi, qw)

    def load(g, c):
        for geo, start in ((geo_lo, 0), (geo_hi, half)):
            for j in range(8):
                i = g * 8 + j
                t8, kt8 = prepare_source(geo[i], i + start, first, centre_sk, *sources)
                prepare_target(t8, kt8, i + start, tgt, tgt_far)
        return c

    lax.fori_loop(0, half // 8, load, 0)
    clear(sources, NONE)
    clear((tgt, tgt_far), leaves)
    run(
        near_pass(near_ids, src, tgt, xw, near_out, near_dist),
        far_pass(far_ids, src_lo, src_hi, tgt_far, qw, far_out, far_dist),
    )


def outer_kernel(
    near_ids, far_ids, box_far, origin, left, right, tgt, tgt_far, q1, box_skel3,
    near_hbm, far_hbm,
    near_sum, far_sum, z1,
    src, xw, src_lo, src_hi, qw, near_dist, far_dist, box_skel,
    near_out, far_out, near_own, far_own, sems,
    *, near_factor, f0,
):
    copies = fetch(((near_hbm, near_own), (far_hbm, far_own)), sems)
    boxes, box_width = q1.shape[0], box_far.shape[0]
    device = lax.axis_index("group") * lax.axis_size("sub") + lax.axis_index("sub")
    box_skel[...] = jnp.zeros_like(box_skel)
    for b in range(boxes):
        for c in range(3):
            box_skel[b, c : c + 1, :] = box_skel3[c, b : b + 1, :]

    def box_level(b):
        mine = box_skel[b]
        centre = mine[:, 0:1]
        blocks, weights = [], []
        for j in range(box_width):
            entry = box_far[j, b]
            m = jnp.maximum(entry - device * boxes, 0)
            blocks.append(box_skel[m])
            weights.append(jnp.where(entry >= 0, q1[m], 0.0))
        source = centred(jnp.concatenate(blocks, axis=1), centre)[0]
        k = distances(source, centred(mine, centre)[1])
        z1[b] = weigh(jnp.concatenate(weights, axis=1), profile(k))

    def two_levels(g, c):
        box_level(2 * g)
        box_level(2 * g + 1)
        return c

    lax.fori_loop(0, boxes // 2, two_levels, 0)
    first = origin[:, 0:1]
    centre_sk = jnp.concatenate([first[3:8], first[0:3]], axis=0)
    sources = (src, xw, src_lo, src_hi, qw)

    def load(g, c):
        for block, start in ((left, 0), (right, HALO)):
            for j in range(8):
                i = g * 8 + j
                prepare_source(block[i], i + start, first, centre_sk, *sources)
        return c

    lax.fori_loop(0, HALO // 8, load, 0)
    clear(sources, NONE)
    run(
        near_pass(near_ids, src, tgt, xw, near_out, near_dist),
        far_pass(far_ids, src_lo, src_hi, tgt_far, qw, far_out, far_dist),
    )
    for copy in copies:
        copy.wait()

    def combine(g, c):
        for j in range(4):
            parts = []
            for half in range(2):
                i = 8 * g + 2 * j + half
                near_sum[i] = (near_own[i] + near_out[i]) * near_factor
                turned = (far_own[i] + far_out[i]).T
                parts.append((turned[0:32] + turned[32:64]) * f0)
            far_sum[4 * g + j] = jnp.concatenate(parts, axis=1)
        return c

    lax.fori_loop(0, near_sum.shape[0] // 8, combine, 0)


def finish_kernel(
    morton, sub_far, near, far, z1, gathered, group_skel3, *rest,
    groups, sub_width, f1, f2, f3,
):
    fetched = rest[:4]
    out, group_skel, rows, pad, tall, tall_too, l1s = rest[4:11]
    held, sems = rest[11:15], rest[15]
    basis, leaf_tr, box_tr, sub_tr = held
    copies = fetch(tuple(zip(fetched, held))[::-1], sems)
    boxes = z1.shape[0]
    leaves = near.shape[0]
    group = lax.axis_index("group")
    subs = lax.axis_size("sub")
    device = group * subs + lax.axis_index("sub")
    group_skel[...] = jnp.zeros_like(group_skel)
    for b in range(groups):
        for c in range(3):
            group_skel[b, c : c + 1, :] = group_skel3[c, b : b + 1, :]

    own = gathered[device, 64:72, :]
    centre = own[:, 0:1]
    target = centred(own, centre)[1]

    def sub_term(j, acc):
        entry = sub_far[j]
        m = jnp.maximum(entry, 0)
        source = centred(gathered[m, 64:72, :], centre)[0]
        q2 = jnp.where(entry >= 0, gathered[m, 0:32, :], 0.0)
        return acc + weigh(q2, profile(distances(source, target)))

    many = 4 if sub_width % 4 == 0 else 1

    def sub_terms(g, acc):
        for j in range(many):
            acc = sub_term(g * many + j, acc)
        return acc

    none = jnp.zeros((32, gathered.shape[2]), f32)
    z2 = lax.fori_loop(0, sub_width // many, sub_terms, none)
    g_own = group_skel[group]
    g_centre = g_own[:, 0:1]
    g_target = centred(g_own, g_centre)[1]
    z3 = none
    for step in range(1, groups):
        h = lax.rem(group + step, groups)

        def eight(s, t):
            for k in range(8):
                t = t + gathered[h * subs + s * 8 + k, 32:64, :]
            return t

        q3 = lax.fori_loop(0, subs // 8, eight, none)
        source = centred(group_skel[h], g_centre)[0]
        z3 = z3 + weigh(q3, profile(distances(source, g_target)))
    for copy in copies:
        copy.wait()
    l2 = z2 * f2 + hdot_nt(z3 * f3, sub_tr[0])
    for b in range(boxes):
        l1s[b] = z1[b] * f1 + hdot_nt(l2, box_tr[b])

    def work(b, into, old, held):
        l1 = l1s[b]
        for j in range(CH):
            for k in range(P_SIZE):
                rows[pl.ds(row_of(morton, old, j * P_SIZE + k), 1), :] = held[j, k : k + 1, :]
            i = b * CH + j
            side = 64 * (j % 2)
            l0 = far[b * (CH // 2) + j // 2, :, side : side + 64] + hdot_nt(l1, leaf_tr[i])
            pad[j, 0:32, :] = near[i] + hdot(l0, basis[i])
            into[j] = pad[j].T

    def scatter(b, held):
        for j in range(CH):
            for k in range(P_SIZE):
                rows[pl.ds(row_of(morton, b, j * P_SIZE + k), 1), :] = held[j, k : k + 1, :]

    pad[...] = jnp.zeros_like(pad)
    tall_too[...] = jnp.zeros_like(tall_too)

    def two_boxes(g, c):
        work(2 * g, tall, jnp.maximum(2 * g - 1, 1), tall_too)
        work(2 * g + 1, tall_too, 2 * g, tall)
        return c

    lax.fori_loop(0, boxes // 2, two_boxes, 0)
    scatter(boxes - 1, tall_too)

    def flip(g, c):
        for j in range(8):
            at = pl.ds(pl.multiple_of((8 * g + j) * P_SIZE, P_SIZE), P_SIZE)
            out[:, at] = rows[at, :].T[0:32]
        return c

    lax.fori_loop(0, leaves // 8, flip, 0)


VMEM = pl.BlockSpec(memory_space=pltpu.VMEM)
SMEM = pl.BlockSpec(memory_space=pltpu.SMEM)
ANY = pl.BlockSpec(memory_space=pl.ANY)
params = pltpu.CompilerParams(vmem_limit_bytes=56 * 2**20)


def body(
    points, probes, morton, near_list, leaf_far, box_far, subtree_far,
    leaf_skeleton, box_skeleton, subtree_skeleton, group_skeleton,
    leaf_basis, leaf_transfer, box_transfer, subtree_transfer,
):
    leaves = near_list.shape[0]
    count = points.shape[1]
    nv = probes.shape[0]
    boxes = box_far.shape[0]
    r0, r1 = leaf_basis.shape[1], box_transfer.shape[1]
    r2, r3 = subtree_transfer.shape[1:]
    subs, groups = lax.axis_size("sub"), lax.axis_size("group")
    i32 = jnp.int32
    front = lambda a: jnp.transpose(a, (1, 0, 2))
    bases = (leaf_basis, leaf_transfer, box_transfer, subtree_transfer)
    held = [pltpu.VMEM(a.shape, f32) for a in bases]
    sems = pltpu.SemaphoreType.DMA((len(bases),))

    geo_lo, geo_hi, near_ids, near_ids_out, far_ids, far_ids_out, q1, packed = pl.pallas_call(
        arrange_kernel,
        out_shape=(
            jax.ShapeDtypeStruct((leaves // 2, 56, P_SIZE), f32),
            jax.ShapeDtypeStruct((leaves // 2, 56, P_SIZE), f32),
            *[jax.ShapeDtypeStruct((FLAT // P_SIZE, P_SIZE), i32)] * 4,
            jax.ShapeDtypeStruct((boxes, nv, r1), f32),
            jax.ShapeDtypeStruct((72, r2), f32),
        ),
        in_specs=[SMEM] + [VMEM] * 6 + [ANY] * 4,
        out_specs=(VMEM,) * 8,
        scratch_shapes=[
            pltpu.VMEM((count, P_SIZE), f32),
            pltpu.VMEM((CH, P_SIZE, P_SIZE), f32),
            pltpu.VMEM((CH, P_SIZE, P_SIZE), f32),
            pltpu.VMEM((2 * SLOTS, P_SIZE), i32),
        ]
        + held
        + [sems],
        compiler_params=params,
        name="arrange",
    )(
        morton, near_list.T, leaf_far.T, points, probes, front(leaf_skeleton),
        front(subtree_skeleton), *bases,
    )

    both = ("group", "sub")
    ends = subs * groups - 1
    left = lax.ppermute(geo_hi, both, [(i, i + 1) for i in range(ends)])
    right = lax.ppermute(geo_lo, both, [(i + 1, i) for i in range(ends)])
    gathered = lax.all_gather(packed, both, axis=0)

    acc_shapes = ((leaves + 1, nv, P_SIZE), (leaves + 1, r0, P_SIZE))
    tables = [
        pltpu.VMEM((NONE + 1, P_SIZE, 64), bf16),
        pltpu.VMEM((NONE + 1, 2 * nv, P_SIZE), bf16),
        pltpu.VMEM((NONE + 1, 64, P_SIZE), bf16),
        pltpu.VMEM((NONE + 1, 64, P_SIZE), bf16),
        pltpu.VMEM((NONE + 1, 64, P_SIZE), bf16),
        pltpu.VMEM((2 * NEAR_BATCH, P_SIZE, P_SIZE), f32),
        pltpu.VMEM((FAR_BATCH, 64, P_SIZE), f32),
    ]
    near, far, tgt, tgt_far, origin = pl.pallas_call(
        inner_kernel,
        out_shape=tuple(jax.ShapeDtypeStruct(a, f32) for a in acc_shapes)
        + (
            jax.ShapeDtypeStruct((leaves + 1, 64, P_SIZE), bf16),
            jax.ShapeDtypeStruct((leaves + 1, 64, P_SIZE), bf16),
            jax.ShapeDtypeStruct((8, P_SIZE), f32),
        ),
        in_specs=[SMEM] * 2 + [VMEM] * 2,
        out_specs=(VMEM,) * 5,
        scratch_shapes=tables,
        compiler_params=params,
        cost_estimate=pl.CostEstimate(flops=2 * 10**10, bytes_accessed=10**7, transcendentals=5 * 10**7),
        name="inner",
    )(near_ids.reshape(-1), far_ids.reshape(-1), geo_lo, geo_hi)

    near, far, z1 = pl.pallas_call(
        functools.partial(
            outer_kernel,
            near_factor=(P_SIZE * near_list.shape[1]) ** -0.5,
            f0=(r0 * leaf_far.shape[1]) ** -0.5,
        ),
        out_shape=(
            jax.ShapeDtypeStruct((leaves, nv, P_SIZE), f32),
            jax.ShapeDtypeStruct((leaves // 2, nv, 2 * r0), f32),
            jax.ShapeDtypeStruct((boxes, nv, r1), f32),
        ),
        in_specs=[SMEM] * 3 + [VMEM] * 7 + [ANY] * 2,
        out_specs=(VMEM,) * 3,
        scratch_shapes=tables
        + [pltpu.VMEM((boxes, 8, r1), f32)]
        + [pltpu.VMEM(a, f32) for a in acc_shapes * 2]
        + [pltpu.SemaphoreType.DMA((2,))],
        compiler_params=params,
        cost_estimate=pl.CostEstimate(flops=10**10, bytes_accessed=10**7, transcendentals=3 * 10**7),
        name="outer",
    )(
        near_ids_out.reshape(-1), far_ids_out.reshape(-1), box_far.T,
        origin, left, right, tgt, tgt_far, q1, front(box_skeleton), near, far,
    )

    return pl.pallas_call(
        functools.partial(
            finish_kernel,
            groups=groups,
            sub_width=subtree_far.shape[1],
            f1=(r1 * box_far.shape[1]) ** -0.5,
            f2=(r2 * subtree_far.shape[1]) ** -0.5,
            f3=r3**-0.5,
        ),
        out_shape=jax.ShapeDtypeStruct((nv, count), f32),
        in_specs=[SMEM] * 2 + [VMEM] * 5 + [ANY] * 4,
        out_specs=VMEM,
        scratch_shapes=[
            pltpu.VMEM((groups, 8, r3), f32),
            pltpu.VMEM((count, P_SIZE), f32),
            pltpu.VMEM((CH, P_SIZE, P_SIZE), f32),
            pltpu.VMEM((CH, P_SIZE, P_SIZE), f32),
            pltpu.VMEM((CH, P_SIZE, P_SIZE), f32),
            pltpu.VMEM((boxes, nv, P_SIZE), f32),
        ]
        + held
        + [sems],
        compiler_params=params,
        name="finish",
    )(
        morton, subtree_far.reshape(-1), near, far, z1, gathered, front(group_skeleton), *bases,
    )


def solution(mesh):
    two = ("group", "sub")
    placed = (
        (P(None, two),) * 2
        + (P(two),)
        + (P(two, None),) * 4
        + (P(two, None, None),) * 3
        + (P(),)
        + (P(two, None, None),) * 4
    )
    return jax.shard_map(
        body, mesh=mesh, in_specs=placed, out_specs=P(None, two), check_vma=False
    )
```

```python
import functools
import math

import jax
import jax.numpy as jnp
from jax import lax
from jax.experimental import pallas as pl
from jax.experimental.pallas import tpu as pltpu
from jax.sharding import PartitionSpec as P

P_SIZE = 128
CH = 8
HALO = 32
SLOTS = 16
NONE = 2 * HALO
RADIX = 128
FLAT = 8 * P_SIZE
REACH = FLAT - 48
NEAR_BATCH = 16
FAR_BATCH = 14

scale = math.sqrt(3.0) / 12.0
soft = 0.0001 * scale * scale
log2e = math.log2(math.e)
f32 = jnp.float32
bf16 = jnp.bfloat16
NT = (((1,), (1,)), ((), ()))


def halves(k):
    hi = k.astype(bf16)
    return hi, (k - hi.astype(f32)).astype(bf16)


def hdot(a, b):
    ah, al = halves(a)
    bh, bl = halves(b)
    return jnp.dot(
        jnp.concatenate([ah, al, ah], axis=1),
        jnp.concatenate([bh, bh, bl], axis=0),
        preferred_element_type=f32,
    )


def hdot_nt(a, b):
    ah, al = halves(a)
    bh, bl = halves(b)
    return lax.dot_general(
        jnp.concatenate([ah, al, ah], axis=1),
        jnp.concatenate([bh, bh, bl], axis=1),
        NT,
        preferred_element_type=f32,
    )


def weigh(q, k):
    n = k.shape[1]
    both = jnp.dot(
        jnp.concatenate(halves(q), axis=0),
        jnp.concatenate(halves(k), axis=1),
        preferred_element_type=f32,
    )
    return both[0:32, 0:n] + both[0:32, n:] + both[32:64, 0:n]


def profile(squared):
    squared = jnp.maximum(squared, soft)
    u = squared * lax.rsqrt(squared)
    return (1.0 + u) * jnp.exp2(u * -log2e)


def split3(v):
    high = v.astype(bf16).astype(f32)
    rest = v - high
    mid = rest.astype(bf16).astype(f32)
    return high, mid, rest - mid


def augmented(x):
    row = lax.broadcasted_iota(jnp.int32, x.shape, 0)
    norm = jnp.sum(x * x, axis=0, keepdims=True)
    source = jnp.where(row < 3, -2.0 * x, jnp.where(row == 3, 1.0, jnp.where(row == 4, norm + soft, 0.0)))
    target = jnp.where(row < 3, x, jnp.where(row == 3, norm, jnp.where(row == 4, 1.0, 0.0)))
    return source, target


def source_rows(v):
    h, m, lo = split3(v)
    return jnp.concatenate([h, m, h, m, lo, h, lo, m], axis=0)


def target_rows(v):
    h, m, lo = split3(v)
    return jnp.concatenate([h, h, m, m, h, lo, m, lo], axis=0)


def coords(block, centre):
    row = lax.broadcasted_iota(jnp.int32, block.shape, 0)
    return jnp.where(row < 3, (block - centre) * scale, 0.0)


def sort_list(ids_ref, outs, wide, base):
    width, leaves = ids_ref.shape
    wide[...] = jnp.full(wide.shape, -1, jnp.int32)
    wide[0:width, 0:leaves] = ids_ref[...]
    ids = wide[...]
    shape = ids.shape
    place = ids - base
    valid = ids >= 0
    own = valid & (place >= 0) & (place < leaves)
    other = valid & jnp.logical_not(own)
    slot = jnp.where(own, place, jnp.where(place < 0, place + HALO, place - leaves + HALO))
    ones = jnp.concatenate([own.astype(f32), other.astype(f32)], axis=1)
    row = lax.broadcasted_iota(jnp.int32, shape, 0)
    lane = lax.broadcasted_iota(jnp.int32, shape, 1)
    square = (shape[0], shape[0])
    before = lax.broadcasted_iota(jnp.int32, square, 1) < lax.broadcasted_iota(jnp.int32, square, 0)
    rank = jnp.dot(
        before.astype(f32).astype(bf16), ones.astype(bf16), preferred_element_type=f32
    ).astype(jnp.int32)
    total = jnp.sum(ones, axis=0, keepdims=True).astype(jnp.int32)
    value = slot.astype(f32)
    square = (P_SIZE, P_SIZE)
    ahead = lax.broadcasted_iota(jnp.int32, square, 0) < lax.broadcasted_iota(jnp.int32, square, 1)
    ahead = ahead.astype(f32).astype(bf16)
    lane8 = lane[0:8]
    row8 = row[0:8]
    for part, out in enumerate(outs):
        mask = (own, other)[part]
        order = jnp.where(mask, rank[:, part * P_SIZE : (part + 1) * P_SIZE], -1)
        goes = jnp.where(order % 2 == 1, SLOTS + order // 2, order // 2)
        goes = jnp.where(mask, goes, -1)
        many = total[:, part * P_SIZE : (part + 1) * P_SIZE]
        at = jnp.where(row < SLOTS, 2 * row, 2 * (row - SLOTS) + 1)
        table = jnp.where(many <= at, 1.0 * NONE, 0.0)
        for j in range(width):
            table = table + jnp.where(row == goes[j : j + 1], value[j : j + 1], 0.0)
        groups = jnp.where(lane8 < leaves, jnp.maximum((many + 1) // 2, 1), 0)
        start = jnp.dot(
            groups.astype(f32).astype(bf16), ahead, preferred_element_type=f32
        ).astype(jnp.int32)
        stop = jnp.where(lane8 == leaves, FLAT, start + groups)
        extra = jnp.where(
            row8 == 0, start // 32, jnp.where(row8 == 1, start % 32, jnp.where(row8 == 2, lane8, 0))
        )
        look = jnp.concatenate([table, extra.astype(f32)], axis=0).astype(bf16)
        ends = jnp.concatenate(
            [jnp.where(row8 == 0, start, stop).astype(f32), jnp.zeros((P_SIZE - 8, P_SIZE), f32)],
            axis=0,
        ).T
        begin, end = ends[:, 0:1], ends[:, 1:2]
        spot = lax.broadcasted_iota(jnp.int32, square, 1).astype(f32)
        for t in range(FLAT // P_SIZE):
            here = spot + 1.0 * t * P_SIZE
            hot = ((begin <= here) & (here < end)).astype(f32).astype(bf16)
            found = jnp.dot(look, hot, preferred_element_type=f32)
            k = here[0:1] - (found[32:33] * 32.0 + found[33:34])
            pick = row[0:SLOTS].astype(f32) == k
            a = jnp.sum(jnp.where(pick, found[0:SLOTS], 0.0), axis=0, keepdims=True)
            b = jnp.sum(jnp.where(pick, found[SLOTS : 2 * SLOTS], 0.0), axis=0, keepdims=True)
            word = a + b * RADIX + found[34:35] * (RADIX * RADIX)
            out[t : t + 1, :] = word.astype(jnp.int32)
        count = start[0:1, leaves : leaves + 1]
        out[7:8, P_SIZE - 1 : P_SIZE] = count


def row_of(morton, b, offset):
    return morton.at[pl.ds(offset, morton.shape[0] - CH * P_SIZE + 1)][b * (CH * P_SIZE)]


def fetch(pairs, sems):
    copies = [pltpu.make_async_copy(a, b, sems.at[i]) for i, (a, b) in enumerate(pairs)]
    for copy in copies:
        copy.start()
    return copies


def arrange_kernel(
    morton, near_list, leaf_far, points, probes, skel, sub_skel, basis_hbm, leaf_hbm, box_hbm, sub_hbm,
    geo_lo, geo_hi, near_ids, near_ids_out, far_ids, far_ids_out, q1_out, packed,
    rows, got, got_too, wide, basis, leaf_tr, box_tr, sub_tr, sems,
):
    copies = fetch(
        ((basis_hbm, basis), (leaf_hbm, leaf_tr), (box_hbm, box_tr), (sub_hbm, sub_tr)), sems
    )
    half = geo_lo.shape[0]
    leaves = 2 * half
    middle = q1_out.shape[0] // 2
    device = lax.axis_index("group") * lax.axis_size("sub") + lax.axis_index("sub")
    sort_list(near_list, (near_ids, near_ids_out), wide, device * leaves)
    sort_list(leaf_far, (far_ids, far_ids_out), wide, device * leaves)

    def flip(g, c):
        for j in range(8):
            at = pl.ds(pl.multiple_of((8 * g + j) * P_SIZE, P_SIZE), P_SIZE)
            both = jnp.concatenate(
                [probes[:, at], points[:, at], jnp.zeros((5, P_SIZE), f32)], axis=0
            )
            rows[at, 0:40] = both.T
        return c

    lax.fori_loop(0, leaves // 8, flip, 0)
    for copy in copies:
        copy.wait()

    def gather(b, into):
        for j in range(CH):
            for k in range(P_SIZE):
                into[j, k : k + 1, :] = rows[pl.ds(row_of(morton, b, j * P_SIZE + k), 1), :]

    def combine(b, start, held, geo):
        turned = [held[j].T for j in range(CH)]
        parts = []
        for j in range(CH):
            i = b * CH + j
            at = i - start
            geo[at, 0:40, :] = turned[j][0:40]
            for c in range(3):
                geo[at, 35 + c : 36 + c, 0:64] = skel[c, pl.ds(i, 1), :]
            q0 = hdot_nt(turned[j][0:32], basis[i])
            geo[at, 40:56, 0:64] = q0[0:16]
            geo[at, 40:56, 64:128] = q0[16:32]
            parts.append(q0)
        q1 = jnp.zeros(q1_out.shape[1:], f32)
        for j in range(0, CH, 2):
            two = jnp.concatenate([leaf_tr[b * CH + j], leaf_tr[b * CH + j + 1]], axis=0)
            q1 = q1 + hdot(jnp.concatenate(parts[j : j + 2], axis=1), two)
        q1_out[b] = q1
        return hdot(q1, box_tr[b])

    def two_boxes(g, q2):
        gather(g, got)
        late = combine(middle + jnp.maximum(g - 1, 0), half, got_too, geo_hi)
        gather(middle + g, got_too)
        return q2 + jnp.where(g > 0, late, 0.0) + combine(g, 0, got, geo_lo)

    q2 = lax.fori_loop(0, middle, two_boxes, jnp.zeros((32, packed.shape[1]), f32))
    q2 = q2 + combine(2 * middle - 1, half, got_too, geo_hi)
    packed[0:32, :] = q2
    packed[32:64, :] = hdot(q2, sub_tr[0])
    packed[64:72, :] = jnp.zeros((8, packed.shape[1]), f32)
    for c in range(3):
        packed[64 + c : 65 + c, :] = sub_skel[c]


def prepare_source(block, at, centre_pt, centre_sk, src, xw, src_lo, src_hi, qw):
    geo8 = block[32:40]
    s8, t8 = augmented(coords(geo8, centre_pt))
    src[at] = source_rows(s8).T.astype(bf16)
    turned = jnp.concatenate([geo8[3:8], geo8[0:3]], axis=0)
    ks8, kt8 = augmented(coords(turned, centre_sk))
    low = lax.broadcasted_iota(jnp.int32, (8, P_SIZE), 1) < 64
    ks8 = jnp.where(low, ks8, 0.0)
    src_lo[at] = source_rows(ks8).astype(bf16)
    src_hi[at] = source_rows(pltpu.roll(ks8, 64, 1)).astype(bf16)
    x = block[0:32]
    hi = x.astype(bf16)
    lo = (x - hi.astype(f32)).astype(bf16)
    xw[at] = jnp.concatenate([hi, lo], axis=0)
    q = block[40:56]
    q = jnp.concatenate([q, pltpu.roll(q, 64, 1)], axis=0)
    qhi = q.astype(bf16).astype(f32)
    four = jnp.concatenate([qhi, q - qhi, jnp.zeros((64, P_SIZE), f32)], axis=0)
    qw[at] = four.T[0:64].astype(bf16)
    return t8, kt8


def prepare_target(t8, kt8, at, tgt, tgt_far):
    tgt[at] = target_rows(t8).astype(bf16)
    far = target_rows(kt8)
    tgt_far[at] = jnp.concatenate([far, far], axis=0).T[0:64].astype(bf16)


def clear(refs, at):
    for ref in refs:
        ref[at] = jnp.zeros(ref.shape[1:], ref.dtype)


def stream(ids, leaves, batch, out, first, part):
    def entry(i, j):
        word = ids.at[pl.ds(j, REACH)][i * batch]
        return word >> 14, word & (RADIX - 1), (word >> 7) & (RADIX - 1)

    def start():
        for j in range(batch):
            first(j, entry(0, j))
        return jnp.int32(0), jnp.zeros(out.shape[1:], f32)

    def steps(i, c):
        leaf, acc = c
        for j in range(batch):
            now = entry(i, j)
            more = part(j, now, entry(i, j + batch))
            acc = jnp.where(now[0] == leaf, acc, 0.0) + more
            leaf = now[0]
            out[leaf] = acc
            yield None
        yield leaf, acc

    trips = (ids[FLAT - 1] + batch - 1) // batch
    return start, steps, trips


def run(*streams):
    def one(i, c):
        work = [steps(i, held) for (_, steps, _), held in zip(streams, c)]
        done = [None] * len(work)
        while any(d is None for d in done):
            done = [next(w) if d is None else d for w, d in zip(work, done)]
        return tuple(done)

    trips = functools.reduce(jnp.maximum, [t for _, _, t in streams])
    lax.fori_loop(0, trips, one, tuple(start() for start, _, _ in streams))


def near_pass(ids, src, tgt, xw, out, dist):
    def first(j, at):
        leaf, a, b = at
        target = tgt[leaf]
        dist[2 * j] = jnp.dot(src[a], target, preferred_element_type=f32)
        dist[2 * j + 1] = jnp.dot(src[b], target, preferred_element_type=f32)

    def part(j, at, ahead):
        tiles = [jnp.concatenate(halves(profile(dist[2 * j + u])), axis=1) for u in range(2)]
        first(j, ahead)
        acc = jnp.dot(
            jnp.concatenate([xw[at[1]], xw[at[2]]], axis=1),
            jnp.concatenate(tiles, axis=0),
            preferred_element_type=f32,
        )
        return acc[0:32, 0:128] + acc[0:32, 128:256] + acc[32:64, 0:128]

    return stream(ids, tgt.shape[0] - 1, NEAR_BATCH, out, first, part)


def far_pass(ids, src_lo, src_hi, tgt, qw, out, dist):
    def first(j, at):
        leaf, a, b = at
        source = jnp.concatenate([src_lo[a], src_hi[b]], axis=0)
        dist[j] = jnp.dot(tgt[leaf], source, preferred_element_type=f32)

    def part(j, at, ahead):
        tile = jnp.concatenate(halves(profile(dist[j])), axis=1)
        first(j, ahead)
        a, b = qw[at[1]], qw[at[2]]
        return jnp.dot(
            tile, jnp.concatenate([a, b, a, b], axis=0), preferred_element_type=f32
        )

    return stream(ids, tgt.shape[0] - 1, FAR_BATCH, out, first, part)


def centred(block, centre):
    return augmented(coords(block, centre))


def distances(source8, target8):
    return jnp.dot(
        source_rows(source8).T.astype(bf16),
        target_rows(target8).astype(bf16),
        preferred_element_type=f32,
    )


def inner_kernel(
    near_ids, far_ids, geo_lo, geo_hi,
    near_out, far_out, tgt, tgt_far, origin,
    src, xw, src_lo, src_hi, qw, near_dist, far_dist,
):
    half = geo_lo.shape[0]
    leaves = 2 * half
    first = geo_lo[0, 32:40, 0:1]
    origin[...] = geo_lo[0, 32:40, :]
    centre_sk = jnp.concatenate([first[3:8], first[0:3]], axis=0)
    sources = (src, xw, src_lo, src_hi, qw)

    def load(g, c):
        for geo, start in ((geo_lo, 0), (geo_hi, half)):
            for j in range(8):
                i = g * 8 + j
                t8, kt8 = prepare_source(geo[i], i + start, first, centre_sk, *sources)
                prepare_target(t8, kt8, i + start, tgt, tgt_far)
        return c

    lax.fori_loop(0, half // 8, load, 0)
    clear(sources, NONE)
    clear((tgt, tgt_far), leaves)
    run(
        near_pass(near_ids, src, tgt, xw, near_out, near_dist),
        far_pass(far_ids, src_lo, src_hi, tgt_far, qw, far_out, far_dist),
    )


def outer_kernel(
    near_ids, far_ids, box_far, origin, left, right, tgt, tgt_far, q1, box_skel3,
    near_out, far_out, z1,
    src, xw, src_lo, src_hi, qw, near_dist, far_dist, box_skel,
):
    boxes, box_width = q1.shape[0], box_far.shape[0]
    device = lax.axis_index("group") * lax.axis_size("sub") + lax.axis_index("sub")
    box_skel[...] = jnp.zeros_like(box_skel)
    for b in range(boxes):
        for c in range(3):
            box_skel[b, c : c + 1, :] = box_skel3[c, b : b + 1, :]

    def box_level(b):
        mine = box_skel[b]
        centre = mine[:, 0:1]
        blocks, weights = [], []
        for j in range(box_width):
            entry = box_far[j, b]
            m = jnp.maximum(entry - device * boxes, 0)
            blocks.append(box_skel[m])
            weights.append(jnp.where(entry >= 0, q1[m], 0.0))
        source = centred(jnp.concatenate(blocks, axis=1), centre)[0]
        k = distances(source, centred(mine, centre)[1])
        z1[b] = weigh(jnp.concatenate(weights, axis=1), profile(k))

    def two_levels(g, c):
        box_level(2 * g)
        box_level(2 * g + 1)
        return c

    lax.fori_loop(0, boxes // 2, two_levels, 0)
    first = origin[:, 0:1]
    centre_sk = jnp.concatenate([first[3:8], first[0:3]], axis=0)
    sources = (src, xw, src_lo, src_hi, qw)

    def load(g, c):
        for block, start in ((left, 0), (right, HALO)):
            for j in range(8):
                i = g * 8 + j
                prepare_source(block[i], i + start, first, centre_sk, *sources)
        return c

    lax.fori_loop(0, HALO // 8, load, 0)
    clear(sources, NONE)
    run(
        near_pass(near_ids, src, tgt, xw, near_out, near_dist),
        far_pass(far_ids, src_lo, src_hi, tgt_far, qw, far_out, far_dist),
    )


def finish_kernel(
    morton, sub_far, near_own, far_own, near, far,
    z1, gathered, group_skel3, basis_hbm, leaf_hbm, box_hbm, sub_hbm,
    out,
    group_skel, rows, pad, tall, tall_too, l1s, basis, leaf_tr, box_tr, sub_tr, sems,
    *, groups, sub_width, near_factor, f0, f1, f2, f3,
):
    copies = fetch(
        ((basis_hbm, basis), (leaf_hbm, leaf_tr), (box_hbm, box_tr), (sub_hbm, sub_tr)), sems
    )
    boxes = z1.shape[0]
    leaves = near.shape[0] - 1
    group = lax.axis_index("group")
    subs = lax.axis_size("sub")
    device = group * subs + lax.axis_index("sub")
    group_skel[...] = jnp.zeros_like(group_skel)
    for b in range(groups):
        for c in range(3):
            group_skel[b, c : c + 1, :] = group_skel3[c, b : b + 1, :]

    own = gathered[device, 64:72, :]
    centre = own[:, 0:1]
    target = centred(own, centre)[1]

    def sub_term(j, acc):
        entry = sub_far[j]
        m = jnp.maximum(entry, 0)
        source = centred(gathered[m, 64:72, :], centre)[0]
        q2 = jnp.where(entry >= 0, gathered[m, 0:32, :], 0.0)
        return acc + weigh(q2, profile(distances(source, target)))

    many = 4 if sub_width % 4 == 0 else 1

    def sub_terms(g, acc):
        for j in range(many):
            acc = sub_term(g * many + j, acc)
        return acc

    none = jnp.zeros((32, gathered.shape[2]), f32)
    z2 = lax.fori_loop(0, sub_width // many, sub_terms, none)
    g_own = group_skel[group]
    g_centre = g_own[:, 0:1]
    g_target = centred(g_own, g_centre)[1]
    z3 = none
    for step in range(1, groups):
        h = lax.rem(group + step, groups)

        def eight(s, t):
            for k in range(8):
                t = t + gathered[h * subs + s * 8 + k, 32:64, :]
            return t

        q3 = lax.fori_loop(0, subs // 8, eight, none)
        source = centred(group_skel[h], g_centre)[0]
        z3 = z3 + weigh(q3, profile(distances(source, g_target)))
    for copy in copies:
        copy.wait()
    l2 = z2 * f2 + hdot_nt(z3 * f3, sub_tr[0])
    for b in range(boxes):
        l1s[b] = z1[b] * f1 + hdot_nt(l2, box_tr[b])

    def down(b, into):
        l1 = l1s[b]
        for j in range(CH):
            i = b * CH + j
            turned = (far_own[i] + far[i]).T
            l0 = (turned[0:32] + turned[32:64]) * f0 + hdot_nt(l1, leaf_tr[i])
            pad[j, 0:32, :] = (near_own[i] + near[i]) * near_factor + hdot(l0, basis[i])
        for j in range(CH):
            into[j] = pad[j].T

    def scatter(b, held):
        for j in range(CH):
            for k in range(P_SIZE):
                rows[pl.ds(row_of(morton, b, j * P_SIZE + k), 1), :] = held[j, k : k + 1, :]

    pad[...] = jnp.zeros_like(pad)
    tall_too[...] = jnp.zeros_like(tall_too)

    def two_boxes(g, c):
        scatter(jnp.maximum(2 * g - 1, 1), tall_too)
        down(2 * g, tall)
        scatter(2 * g, tall)
        down(2 * g + 1, tall_too)
        return c

    lax.fori_loop(0, boxes // 2, two_boxes, 0)
    scatter(boxes - 1, tall_too)

    def flip(g, c):
        for j in range(8):
            at = pl.ds(pl.multiple_of((8 * g + j) * P_SIZE, P_SIZE), P_SIZE)
            out[:, at] = rows[at, :].T[0:32]
        return c

    lax.fori_loop(0, leaves // 8, flip, 0)


VMEM = pl.BlockSpec(memory_space=pltpu.VMEM)
SMEM = pl.BlockSpec(memory_space=pltpu.SMEM)
ANY = pl.BlockSpec(memory_space=pl.ANY)
params = pltpu.CompilerParams(vmem_limit_bytes=56 * 2**20)


def body(
    points, probes, morton, near_list, leaf_far, box_far, subtree_far,
    leaf_skeleton, box_skeleton, subtree_skeleton, group_skeleton,
    leaf_basis, leaf_transfer, box_transfer, subtree_transfer,
):
    leaves = near_list.shape[0]
    count = points.shape[1]
    nv = probes.shape[0]
    boxes = box_far.shape[0]
    r0, r1 = leaf_basis.shape[1], box_transfer.shape[1]
    r2, r3 = subtree_transfer.shape[1:]
    subs, groups = lax.axis_size("sub"), lax.axis_size("group")
    i32 = jnp.int32
    front = lambda a: jnp.transpose(a, (1, 0, 2))
    bases = (leaf_basis, leaf_transfer, box_transfer, subtree_transfer)
    held = [pltpu.VMEM(a.shape, f32) for a in bases]
    sems = pltpu.SemaphoreType.DMA((len(bases),))

    geo_lo, geo_hi, near_ids, near_ids_out, far_ids, far_ids_out, q1, packed = pl.pallas_call(
        arrange_kernel,
        out_shape=(
            jax.ShapeDtypeStruct((leaves // 2, 56, P_SIZE), f32),
            jax.ShapeDtypeStruct((leaves // 2, 56, P_SIZE), f32),
            *[jax.ShapeDtypeStruct((FLAT // P_SIZE, P_SIZE), i32)] * 4,
            jax.ShapeDtypeStruct((boxes, nv, r1), f32),
            jax.ShapeDtypeStruct((72, r2), f32),
        ),
        in_specs=[SMEM] + [VMEM] * 6 + [ANY] * 4,
        out_specs=(VMEM,) * 8,
        scratch_shapes=[
            pltpu.VMEM((count, P_SIZE), f32),
            pltpu.VMEM((CH, P_SIZE, P_SIZE), f32),
            pltpu.VMEM((CH, P_SIZE, P_SIZE), f32),
            pltpu.VMEM((2 * SLOTS, P_SIZE), i32),
        ]
        + held
        + [sems],
        compiler_params=params,
        name="arrange",
    )(
        morton, near_list.T, leaf_far.T, points, probes, front(leaf_skeleton),
        front(subtree_skeleton), *bases,
    )

    both = ("group", "sub")
    ends = subs * groups - 1
    left = lax.ppermute(geo_hi, both, [(i, i + 1) for i in range(ends)])
    right = lax.ppermute(geo_lo, both, [(i + 1, i) for i in range(ends)])
    gathered = lax.all_gather(packed, both, axis=0)

    acc_shapes = ((leaves + 1, nv, P_SIZE), (leaves + 1, r0, P_SIZE))
    tables = [
        pltpu.VMEM((NONE + 1, P_SIZE, 64), bf16),
        pltpu.VMEM((NONE + 1, 2 * nv, P_SIZE), bf16),
        pltpu.VMEM((NONE + 1, 64, P_SIZE), bf16),
        pltpu.VMEM((NONE + 1, 64, P_SIZE), bf16),
        pltpu.VMEM((NONE + 1, 64, P_SIZE), bf16),
        pltpu.VMEM((2 * NEAR_BATCH, P_SIZE, P_SIZE), f32),
        pltpu.VMEM((FAR_BATCH, 64, P_SIZE), f32),
    ]
    near, far, tgt, tgt_far, origin = pl.pallas_call(
        inner_kernel,
        out_shape=tuple(jax.ShapeDtypeStruct(a, f32) for a in acc_shapes)
        + (
            jax.ShapeDtypeStruct((leaves + 1, 64, P_SIZE), bf16),
            jax.ShapeDtypeStruct((leaves + 1, 64, P_SIZE), bf16),
            jax.ShapeDtypeStruct((8, P_SIZE), f32),
        ),
        in_specs=[SMEM] * 2 + [VMEM] * 2,
        out_specs=(VMEM,) * 5,
        scratch_shapes=tables,
        compiler_params=params,
        cost_estimate=pl.CostEstimate(flops=2 * 10**10, bytes_accessed=10**7, transcendentals=5 * 10**7),
        name="inner",
    )(near_ids.reshape(-1), far_ids.reshape(-1), geo_lo, geo_hi)

    near_halo, far_halo, z1 = pl.pallas_call(
        outer_kernel,
        out_shape=tuple(
            jax.ShapeDtypeStruct(a, f32) for a in acc_shapes + ((boxes, nv, r1),)
        ),
        in_specs=[SMEM] * 3 + [VMEM] * 7,
        out_specs=(VMEM,) * 3,
        scratch_shapes=tables + [pltpu.VMEM((boxes, 8, r1), f32)],
        compiler_params=params,
        cost_estimate=pl.CostEstimate(flops=10**10, bytes_accessed=10**7, transcendentals=3 * 10**7),
        name="outer",
    )(
        near_ids_out.reshape(-1), far_ids_out.reshape(-1), box_far.T,
        origin, left, right, tgt, tgt_far, q1, front(box_skeleton),
    )

    return pl.pallas_call(
        functools.partial(
            finish_kernel,
            groups=groups,
            sub_width=subtree_far.shape[1],
            near_factor=(P_SIZE * near_list.shape[1]) ** -0.5,
            f0=(r0 * leaf_far.shape[1]) ** -0.5,
            f1=(r1 * box_far.shape[1]) ** -0.5,
            f2=(r2 * subtree_far.shape[1]) ** -0.5,
            f3=r3**-0.5,
        ),
        out_shape=jax.ShapeDtypeStruct((nv, count), f32),
        in_specs=[SMEM] * 2 + [VMEM] * 7 + [ANY] * 4,
        out_specs=VMEM,
        scratch_shapes=[
            pltpu.VMEM((groups, 8, r3), f32),
            pltpu.VMEM((count, P_SIZE), f32),
            pltpu.VMEM((CH, P_SIZE, P_SIZE), f32),
            pltpu.VMEM((CH, P_SIZE, P_SIZE), f32),
            pltpu.VMEM((CH, P_SIZE, P_SIZE), f32),
            pltpu.VMEM((boxes, nv, P_SIZE), f32),
        ]
        + held
        + [sems],
        compiler_params=params,
        name="finish",
    )(
        morton, subtree_far.reshape(-1), near, far, near_halo, far_halo,
        z1, gathered, front(group_skeleton), *bases,
    )


def solution(mesh):
    two = ("group", "sub")
    placed = (
        (P(None, two),) * 2
        + (P(two),)
        + (P(two, None),) * 4
        + (P(two, None, None),) * 3
        + (P(),)
        + (P(two, None, None),) * 4
    )
    return jax.shard_map(
        body, mesh=mesh, in_specs=placed, out_specs=P(None, two), check_vma=False
    )
```
